32 devices in a mesh: row: 8 (over y, x, core), col: 4 (over z).
Axes of the slice: x: 2, y: 2, z: 4, core: 2. Of those that a mesh axis runs over, the one named last changes fastest.
Arguments:
- row_frames: float32 [3, 1024, 256], P(None, ('row', 'col')), may hold values from -40 to 40, as said below
- col_frames: float32 [3, 1024, 256], P(None, ('col', 'row')), may hold values from -40 to 40, as said below
- vectors: float32 [64, 1024], P(None, ('col', 'row')), may hold values from -6 to 6
Outputs:
- embedding_product: float32 [64, 1024], P(None, ('row', 'col'))
The draws below stay inside these ranges and needn't reach their ends.
Inputs may be any that keep to these rules, and one draw needn't show every extreme that they name: `row_frames`: frames of one chain of 256 atoms, each rigidly rotated and moved and perturbed by its own amount. `col_frames`: frames of one chain of 256 atoms, each rigidly rotated and moved and perturbed by its own amount.
All inputs are finite; a program needn't handle non-finite values.
Results may differ from the reference program's by a relative error of at most 0.00017.
Values sent between devices are 32-bit elements; how exact they have to be, the bound alone decides.
No kernel may reach another device: no remote copies, remote signals or barrier semaphores. Data moves between devices by JAX's collectives and lax.ppermute only.
A program may use at most 64 MiB of HBM per device.

```python
import math
import jax
import jax.numpy as jnp
from jax import lax

A = 256
NV = 64
NEWTON = 8
FR_DEV = 32
ROWS = 1024
COLS = 1024
N_ROW = 8
N_COL = 4


def make_frames(key, label, count):
    base = jax.random.truncated_normal(jax.random.fold_in(key, 11), -4.0, 4.0, (3, A)) * 3.0
    own_key = jax.random.fold_in(key, label)
    key_scale, key_noise, key_turn, key_shift = jax.random.split(own_key, 4)
    spread = jnp.exp(jax.random.uniform(key_scale, (count,), jnp.float32, math.log(0.3), math.log(1.2)))
    noise = jax.random.truncated_normal(key_noise, -4.0, 4.0, (3, count, A))
    shape_body = base[:, None, :] + spread[None, :, None] * noise
    quaternion = jax.random.normal(key_turn, (4, count))
    quaternion = quaternion / jnp.sqrt(jnp.sum(quaternion * quaternion, axis=0, keepdims=True) + 1e-06)
    quat_w, quat_x, quat_y, quat_z = (quaternion[0], quaternion[1], quaternion[2], quaternion[3])
    turn = [[1 - 2 * (quat_y * quat_y + quat_z * quat_z), 2 * (quat_x * quat_y - quat_z * quat_w), 2 * (quat_x * quat_z + quat_y * quat_w)], [2 * (quat_x * quat_y + quat_z * quat_w), 1 - 2 * (quat_x * quat_x + quat_z * quat_z), 2 * (quat_y * quat_z - quat_x * quat_w)], [2 * (quat_x * quat_z - quat_y * quat_w), 2 * (quat_y * quat_z + quat_x * quat_w), 1 - 2 * (quat_x * quat_x + quat_y * quat_y)]]
    shift = jax.random.uniform(key_shift, (3, count), jnp.float32, -10.0, 10.0)
    rotated = [turn[row_id][0][:, None] * shape_body[0] + turn[row_id][1][:, None] * shape_body[1] + turn[row_id][2][:, None] * shape_body[2] + shift[row_id][:, None] for row_id in range(3)]
    return jnp.stack(rotated, axis=0).astype(jnp.float32)


def draw_row_frames(key, part):
    return make_frames(key, 1, ROWS)


def draw_col_frames(key, part):
    return make_frames(key, 2, COLS)


def steps_of(key, shape, shards, low, top_value):
    factor_of, own = 1.0, jax.random.fold_in(key, 6)
    for axis_at, parts in shards:
        heights = jnp.exp(jax.random.uniform(jax.random.fold_in(own, axis_at), (parts,), jnp.float32, low / len(shards), top_value / len(shards)))
        factor_of = factor_of * jnp.repeat(heights, shape[axis_at] // parts).reshape([-1 if axis == axis_at else 1 for axis in range(len(shape))])
    return factor_of


def scatter_about(key, extent, scale, bound, cuts=(), kind=jnp.bfloat16):
    drawn = scale * jax.random.normal(key, extent, jnp.float32)
    if cuts:
        drawn = drawn * steps_of(key, extent, cuts, -0.22, 0.18)
    return jnp.clip(drawn, -bound, bound).astype(kind)


def setup_inputs(seed: int = 0) -> dict:
    keys = jax.random.split(jax.random.key(seed), 4)
    return {
        "row_frames": draw_row_frames(jax.random.fold_in(keys[3], 71), 0),
        "col_frames": draw_col_frames(jax.random.fold_in(keys[3], 71), 0),
        "vectors": scatter_about(keys[2], (NV, COLS), 1.0, 6.0, ((1, 32),), jnp.float32),
    }


band_width = 2.0


def centre(frames):
    return frames - jnp.mean(frames, axis=2, keepdims=True)


def kernel_tile(rows, cols):
    count_rows = rows.shape[1]
    count_cols = cols.shape[1]
    atoms = rows.shape[2]
    row_norms = jnp.sum(rows * rows, axis=(0, 2))
    col_norms = jnp.sum(cols * cols, axis=(0, 2))
    product = jnp.dot(cols.reshape(3 * count_cols, atoms), rows.reshape(3 * count_rows, atoms).T,
                      precision=lax.Precision.HIGHEST, preferred_element_type=jnp.float32)
    product = product.reshape(3, count_cols, 3, count_rows)
    moment = [[product[second, :, first, :] for second in range(3)] for first in range(3)]
    half_norm = 0.5 * (row_norms[None, :] + col_norms[:, None])
    coef_two = -2.0 * sum(moment[first][second] * moment[first][second] for first in range(3) for second in range(3))
    coef_one = 8.0 * (moment[0][0] * moment[1][2] * moment[2][1] + moment[1][1] * moment[2][0] * moment[0][2]
                      + moment[2][2] * moment[0][1] * moment[1][0]) - 8.0 * (
        moment[0][0] * moment[1][1] * moment[2][2] + moment[1][2] * moment[2][0] * moment[0][1]
        + moment[2][1] * moment[1][0] * moment[0][2])
    trace_one = moment[0][0] + moment[1][1] + moment[2][2]
    key_matrix = [
        [trace_one, moment[1][2] - moment[2][1], moment[2][0] - moment[0][2], moment[0][1] - moment[1][0]],
        [moment[1][2] - moment[2][1], moment[0][0] - moment[1][1] - moment[2][2], moment[0][1] + moment[1][0], moment[2][0] + moment[0][2]],
        [moment[2][0] - moment[0][2], moment[0][1] + moment[1][0], -moment[0][0] + moment[1][1] - moment[2][2], moment[1][2] + moment[2][1]],
        [moment[0][1] - moment[1][0], moment[2][0] + moment[0][2], moment[1][2] + moment[2][1], -moment[0][0] - moment[1][1] + moment[2][2]],
    ]
    upper = key_matrix
    minor_top = [upper[0][0] * upper[1][1] - upper[1][0] * upper[0][1],
                 upper[0][0] * upper[1][2] - upper[1][0] * upper[0][2],
                 upper[0][0] * upper[1][3] - upper[1][0] * upper[0][3],
                 upper[0][1] * upper[1][2] - upper[1][1] * upper[0][2],
                 upper[0][1] * upper[1][3] - upper[1][1] * upper[0][3],
                 upper[0][2] * upper[1][3] - upper[1][2] * upper[0][3]]
    minor_low = [upper[2][0] * upper[3][1] - upper[3][0] * upper[2][1],
                 upper[2][0] * upper[3][2] - upper[3][0] * upper[2][2],
                 upper[2][0] * upper[3][3] - upper[3][0] * upper[2][3],
                 upper[2][1] * upper[3][2] - upper[3][1] * upper[2][2],
                 upper[2][1] * upper[3][3] - upper[3][1] * upper[2][3],
                 upper[2][2] * upper[3][3] - upper[3][2] * upper[2][3]]
    coef_zero = (minor_top[0] * minor_low[5] - minor_top[1] * minor_low[4] + minor_top[2] * minor_low[3]
                 + minor_top[3] * minor_low[2] - minor_top[4] * minor_low[1] + minor_top[5] * minor_low[0])
    eigen = half_norm
    for newton_step in range(NEWTON):
        eigen_sq = eigen * eigen
        value = (eigen_sq + coef_two) * eigen_sq + coef_one * eigen + coef_zero
        slope = 4.0 * eigen_sq * eigen + 2.0 * coef_two * eigen + coef_one
        eigen = eigen - value / slope
    squared = jnp.maximum(2.0 * (half_norm - eigen) / atoms, 0.0)
    return jnp.exp(-squared / band_width)


def reference(row_frames, col_frames, vectors):
    centred_rows = centre(row_frames)
    centred_cols = centre(col_frames)
    block = FR_DEV * N_COL
    blocks = centred_rows.reshape(3, N_ROW, block, A).transpose(1, 0, 2, 3)

    def one_block(rows):
        tile = kernel_tile(rows, centred_cols)
        degree = jnp.sum(tile, axis=0)
        weighted = jnp.dot(vectors, tile, precision=lax.Precision.HIGHEST, preferred_element_type=jnp.float32)
        return weighted / degree[None, :]

    result = lax.map(one_block, blocks)
    return result.transpose(1, 0, 2).reshape(NV, N_ROW * block)
```

```python
import functools

import jax
import jax.numpy as jnp
from jax import lax
from jax.experimental import pallas as pl
from jax.experimental.pallas import tpu as pltpu
from jax.sharding import PartitionSpec as P

NEWTON = 8
BAND = 2.0
LANES = 128
VM = pl.BlockSpec(memory_space=pltpu.VMEM)
NT = (((1,), (1,)), ((), ()))


def centre(frames):
    return frames - jnp.mean(frames, axis=-1, keepdims=True)


def split(x):
    high = x.astype(jnp.bfloat16)
    low = (x - high.astype(jnp.float32)).astype(jnp.bfloat16)
    return high, low


def pack_kernel(cols_ref, vec_ref, out_ref):
    comps, frames, atoms = cols_ref.shape
    nv = vec_ref.shape[1]
    for comp in range(comps):
        out_ref[comp * frames:(comp + 1) * frames, :] = centre(cols_ref[comp])
    groups = atoms // nv
    step = frames // groups
    out_ref[comps * frames:, :] = jnp.concatenate(
        [vec_ref[group * step:(group + 1) * step, :] for group in range(groups)], axis=1
    )


def eigen_tile(m, half_norm, atoms):
    s00, s01, s02, s10, s11, s12, s20, s21, s22 = m
    coef_two = -2.0 * (
        s00 * s00 + s01 * s01 + s02 * s02 + s10 * s10 + s11 * s11 + s12 * s12 + s20 * s20 + s21 * s21 + s22 * s22
    )
    coef_one = 8.0 * (s00 * s12 * s21 + s11 * s20 * s02 + s22 * s01 * s10) - 8.0 * (
        s00 * s11 * s22 + s12 * s20 * s01 + s21 * s10 * s02
    )
    k00 = s00 + s11 + s22
    k11 = s00 - s11 - s22
    k22 = s11 - s00 - s22
    k33 = s22 - s00 - s11
    k01 = s12 - s21
    k02 = s20 - s02
    k03 = s01 - s10
    k12 = s01 + s10
    k13 = s20 + s02
    k23 = s12 + s21
    top0 = k00 * k11 - k01 * k01
    top1 = k00 * k12 - k01 * k02
    top2 = k00 * k13 - k01 * k03
    top3 = k01 * k12 - k11 * k02
    top4 = k01 * k13 - k11 * k03
    top5 = k02 * k13 - k12 * k03
    low0 = k02 * k13 - k03 * k12
    low1 = k02 * k23 - k03 * k22
    low2 = k02 * k33 - k03 * k23
    low3 = k12 * k23 - k13 * k22
    low4 = k12 * k33 - k13 * k23
    low5 = k22 * k33 - k23 * k23
    coef_zero = top0 * low5 - top1 * low4 + top2 * low3 + top3 * low2 - top4 * low1 + top5 * low0
    eigen = half_norm
    twice = coef_two + coef_two
    for _ in range(NEWTON):
        eigen_sq = eigen * eigen
        value = (eigen_sq + coef_two) * eigen_sq + coef_one * eigen + coef_zero
        slope = (4.0 * eigen_sq + twice) * eigen + coef_one
        eigen = eigen - value / slope
    squared = jnp.maximum(2.0 * (half_norm - eigen) / atoms, 0.0)
    return jnp.exp(-squared / BAND)


def tile_kernel(n_rows, n_cols, frames, nv, *refs):
    row_refs = refs[:n_rows]
    col_refs = refs[n_rows:n_rows + n_cols]
    out_refs = refs[n_rows + n_cols:2 * n_rows + n_cols]
    moment, tile = refs[2 * n_rows + n_cols:]
    atoms = row_refs[0].shape[-1]
    count_cols = n_cols * frames
    per_group = max(1, min(n_rows, LANES // frames))
    groups = atoms // nv
    step = frames // groups

    cols = [
        jnp.concatenate([ref[comp * frames:(comp + 1) * frames, :] for ref in col_refs], axis=0) for comp in range(3)
    ]
    col_square = cols[0] * cols[0] + cols[1] * cols[1] + cols[2] * cols[2]
    col_norm = lax.dot_general(
        jnp.ones((8, atoms), jnp.float32), col_square, NT,
        precision=lax.Precision.HIGHEST, preferred_element_type=jnp.float32,
    )[0:1, :]
    col_high, col_low = split(jnp.concatenate(cols, axis=0))
    col_side = jnp.concatenate([col_high, col_high, col_low], axis=1)

    lane = lax.broadcasted_iota(jnp.int32, (step, LANES), 1)
    vec_parts = []
    for ref in col_refs:
        for group in range(groups):
            place = group * nv
            piece = ref[3 * frames:, place // LANES * LANES:place // LANES * LANES + LANES]
            if place % LANES:
                piece = pltpu.roll(piece, LANES - place % LANES, 1)
            vec_parts.append(jnp.where(lane < nv, piece, jnp.where(lane == nv, 1.0, 0.0)))
    vec_high, vec_low = split(jnp.concatenate(vec_parts, axis=0))
    vec_side = jnp.concatenate([vec_high, vec_high, vec_low], axis=0)

    for first in range(0, n_rows, per_group):
        slots = row_refs[first:first + per_group]
        count = len(slots) * frames
        rows = [centre(jnp.concatenate([ref[comp] for ref in slots], axis=0)) for comp in range(3)]
        row_norm = jnp.sum(rows[0] * rows[0] + rows[1] * rows[1] + rows[2] * rows[2], axis=1, keepdims=True)
        row_high, row_low = split(jnp.concatenate(rows, axis=0))
        moment[0:3 * count, :] = lax.dot_general(
            jnp.concatenate([row_high, row_low, row_high], axis=1), col_side, NT,
            preferred_element_type=jnp.float32,
        )
        for at in range(0, count, 8):
            m = [
                moment[a * count + at:a * count + at + 8, b * count_cols:(b + 1) * count_cols]
                for a in range(3) for b in range(3)
            ]
            half_norm = 0.5 * (row_norm[at:at + 8, :] + col_norm)
            tile[at:at + 8, :] = eigen_tile(m, half_norm, atoms)
        tile_high, tile_low = split(tile[0:count, :])
        product = jnp.dot(
            jnp.concatenate([tile_high, tile_low, tile_high], axis=1), vec_side, preferred_element_type=jnp.float32
        )
        for slot in range(len(slots)):
            out_refs[first + slot][...] = product[slot * frames:(slot + 1) * frames, :]


def finish_kernel(nv, *refs):
    total = refs[0][...]
    for ref in refs[1:-1]:
        total = total + ref[...]
    refs[-1][...] = total[:, 0:nv] / total[:, nv:nv + 1]


def per_device(n_row, n_col, row_frames, col_frames, vectors):
    comps, frames, atoms = row_frames.shape
    nv = vectors.shape[0]
    row_blocks = [row_frames] + [
        lax.ppermute(row_frames, "col", [(at, (at + shift) % n_col) for at in range(n_col)])
        for shift in range(1, n_col)
    ]
    packed = pl.pallas_call(
        pack_kernel,
        out_shape=jax.ShapeDtypeStruct((comps * frames + frames * nv // atoms, atoms), jnp.float32),
        in_specs=[VM, VM],
        out_specs=VM,
        name="centre_pack",
    )(col_frames, vectors.T)
    col_blocks = [packed] + [
        lax.ppermute(packed, "row", [(at, (at + shift) % n_row) for at in range(n_row)])
        for shift in range(1, n_row)
    ]
    group = max(1, min(n_col, LANES // frames)) * frames
    partial = pl.pallas_call(
        functools.partial(tile_kernel, n_col, n_row, frames, nv),
        out_shape=[jax.ShapeDtypeStruct((frames, LANES), jnp.float32)] * n_col,
        in_specs=[VM] * (n_col + n_row),
        out_specs=[VM] * n_col,
        scratch_shapes=[
            pltpu.VMEM((3 * group, 3 * n_row * frames), jnp.float32),
            pltpu.VMEM((group, n_row * frames), jnp.float32),
        ],
        compiler_params=pltpu.CompilerParams(vmem_limit_bytes=40 * 1024 * 1024),
        name="kernel_tile",
    )(*row_blocks, *col_blocks)
    shares = [partial[0]] + [
        lax.ppermute(partial[shift], "col", [(at, (at - shift) % n_col) for at in range(n_col)])
        for shift in range(1, n_col)
    ]
    result = pl.pallas_call(
        functools.partial(finish_kernel, nv),
        out_shape=jax.ShapeDtypeStruct((frames, nv), jnp.float32),
        in_specs=[VM] * n_col,
        out_specs=VM,
        name="sum_divide",
    )(*shares)
    return result.T


def solution(mesh):
    return jax.shard_map(
        functools.partial(per_device, mesh.shape["row"], mesh.shape["col"]),
        mesh=mesh,
        in_specs=(
            P(None, ("row", "col"), None),
            P(None, ("col", "row"), None),
            P(None, ("col", "row")),
        ),
        out_specs=P(None, ("row", "col")),
        check_vma=False,
    )
```

```python
import functools

import jax
import jax.numpy as jnp
from jax import lax
from jax.experimental import pallas as pl
from jax.experimental.pallas import tpu as pltpu
from jax.sharding import PartitionSpec as P

NEWTON = 8
BAND = 2.0
LANES = 128
VM = pl.BlockSpec(memory_space=pltpu.VMEM)
NT = (((1,), (1,)), ((), ()))


def centre(frames):
    return frames - jnp.mean(frames, axis=-1, keepdims=True)


def split(x):
    high = x.astype(jnp.bfloat16)
    low = (x - high.astype(jnp.float32)).astype(jnp.bfloat16)
    return high, low


def pack_kernel(cols_ref, vec_ref, out_ref):
    comps, frames, atoms = cols_ref.shape
    nv = vec_ref.shape[1]
    for comp in range(comps):
        out_ref[comp * frames:(comp + 1) * frames, :] = centre(cols_ref[comp])
    groups = atoms // nv
    step = frames // groups
    out_ref[comps * frames:, :] = jnp.concatenate(
        [vec_ref[group * step:(group + 1) * step, :] for group in range(groups)], axis=1
    )


def eigen_tile(m, half_norm, atoms):
    s00, s01, s02, s10, s11, s12, s20, s21, s22 = m
    coef_two = -2.0 * (
        s00 * s00 + s01 * s01 + s02 * s02 + s10 * s10 + s11 * s11 + s12 * s12 + s20 * s20 + s21 * s21 + s22 * s22
    )
    coef_one = 8.0 * (s00 * s12 * s21 + s11 * s20 * s02 + s22 * s01 * s10) - 8.0 * (
        s00 * s11 * s22 + s12 * s20 * s01 + s21 * s10 * s02
    )
    k00 = s00 + s11 + s22
    k11 = s00 - s11 - s22
    k22 = s11 - s00 - s22
    k33 = s22 - s00 - s11
    k01 = s12 - s21
    k02 = s20 - s02
    k03 = s01 - s10
    k12 = s01 + s10
    k13 = s20 + s02
    k23 = s12 + s21
    top0 = k00 * k11 - k01 * k01
    top1 = k00 * k12 - k01 * k02
    top2 = k00 * k13 - k01 * k03
    top3 = k01 * k12 - k11 * k02
    top4 = k01 * k13 - k11 * k03
    top5 = k02 * k13 - k12 * k03
    low0 = k02 * k13 - k03 * k12
    low1 = k02 * k23 - k03 * k22
    low2 = k02 * k33 - k03 * k23
    low3 = k12 * k23 - k13 * k22
    low4 = k12 * k33 - k13 * k23
    low5 = k22 * k33 - k23 * k23
    coef_zero = top0 * low5 - top1 * low4 + top2 * low3 + top3 * low2 - top4 * low1 + top5 * low0
    eigen = half_norm
    twice = coef_two + coef_two
    for _ in range(NEWTON):
        eigen_sq = eigen * eigen
        value = (eigen_sq + coef_two) * eigen_sq + coef_one * eigen + coef_zero
        slope = (4.0 * eigen_sq + twice) * eigen + coef_one
        eigen = eigen - value / slope
    squared = jnp.maximum(2.0 * (half_norm - eigen) / atoms, 0.0)
    return jnp.exp(-squared / BAND)


def tile_kernel(n_rows, n_cols, frames, nv, *refs):
    row_refs = refs[:n_rows]
    col_refs = refs[n_rows:n_rows + n_cols]
    out_ref, moment, tile = refs[n_rows + n_cols:]
    me = lax.axis_index("col")
    atoms = row_refs[0].shape[-1]
    count_cols = n_cols * frames
    per_group = max(1, min(n_rows, LANES // frames))
    groups = atoms // nv
    step = frames // groups

    cols = [
        jnp.concatenate([ref[comp * frames:(comp + 1) * frames, :] for ref in col_refs], axis=0) for comp in range(3)
    ]
    col_square = cols[0] * cols[0] + cols[1] * cols[1] + cols[2] * cols[2]
    col_norm = lax.dot_general(
        jnp.ones((8, atoms), jnp.float32), col_square, NT,
        precision=lax.Precision.HIGHEST, preferred_element_type=jnp.float32,
    )[0:1, :]
    col_high, col_low = split(jnp.concatenate(cols, axis=0))
    col_side = jnp.concatenate([col_high, col_high, col_low], axis=1)

    lane = lax.broadcasted_iota(jnp.int32, (step, LANES), 1)
    vec_parts = []
    for ref in col_refs:
        for group in range(groups):
            place = group * nv
            piece = ref[3 * frames:, place // LANES * LANES:place // LANES * LANES + LANES]
            if place % LANES:
                piece = pltpu.roll(piece, LANES - place % LANES, 1)
            vec_parts.append(jnp.where(lane < nv, piece, jnp.where(lane == nv, 1.0, 0.0)))
    vec_high, vec_low = split(jnp.concatenate(vec_parts, axis=0))
    vec_side = jnp.concatenate([vec_high, vec_high, vec_low], axis=0)

    for first in range(0, n_rows, per_group):
        slots = row_refs[first:first + per_group]
        count = len(slots) * frames
        rows = [centre(jnp.concatenate([ref[comp] for ref in slots], axis=0)) for comp in range(3)]
        row_norm = jnp.sum(rows[0] * rows[0] + rows[1] * rows[1] + rows[2] * rows[2], axis=1, keepdims=True)
        row_high, row_low = split(jnp.concatenate(rows, axis=0))
        moment[0:3 * count, :] = lax.dot_general(
            jnp.concatenate([row_high, row_low, row_high], axis=1), col_side, NT,
            preferred_element_type=jnp.float32,
        )
        for at in range(0, count, 8):
            m = [
                moment[a * count + at:a * count + at + 8, b * count_cols:(b + 1) * count_cols]
                for a in range(3) for b in range(3)
            ]
            half_norm = 0.5 * (row_norm[at:at + 8, :] + col_norm)
            tile[at:at + 8, :] = eigen_tile(m, half_norm, atoms)
        tile_high, tile_low = split(tile[0:count, :])
        product = jnp.dot(
            jnp.concatenate([tile_high, tile_low, tile_high], axis=1), vec_side, preferred_element_type=jnp.float32
        )
        for slot in range(len(slots)):
            out_ref[origin(me, first + slot, n_rows)] = product[slot * frames:(slot + 1) * frames, :]


def finish_kernel(nv, parts_ref, out_ref):
    total = parts_ref[0]
    for part in range(1, parts_ref.shape[0]):
        total = total + parts_ref[part]
    out_ref[...] = total[:, 0:nv] / total[:, nv:nv + 1]


def partner(at, mask, count):
    return at ^ mask if count & (count - 1) == 0 else (at + mask) % count


def exchange(x, axis, mask, count):
    return lax.ppermute(x, axis, [(at, partner(at, mask, count)) for at in range(count)])


def origin(me, mask, count):
    return jnp.bitwise_xor(me, mask) if count & (count - 1) == 0 else lax.rem(me + count - mask, count)


def params(megabytes):
    return pltpu.CompilerParams(vmem_limit_bytes=megabytes * 1024 * 1024)


def per_device(n_row, n_col, row_frames, col_frames, vectors):
    comps, frames, atoms = row_frames.shape
    nv = vectors.shape[0]
    row_blocks = [row_frames] + [exchange(row_frames, "col", mask, n_col) for mask in range(1, n_col)]
    packed = pl.pallas_call(
        pack_kernel,
        out_shape=jax.ShapeDtypeStruct((comps * frames + frames * nv // atoms, atoms), jnp.float32),
        in_specs=[VM, VM],
        out_specs=VM,
        compiler_params=params(4),
        name="centre_pack",
    )(col_frames, vectors.T)
    same_core = [packed] + [exchange(packed, "row", mask, n_row) for mask in range(2, n_row, 2)]
    col_blocks = same_core + [exchange(block, "row", 1, n_row) for block in same_core]
    group = max(1, min(n_col, LANES // frames)) * frames
    partial = pl.pallas_call(
        functools.partial(tile_kernel, n_col, n_row, frames, nv),
        out_shape=jax.ShapeDtypeStruct((n_col, frames, LANES), jnp.float32),
        in_specs=[VM] * (n_col + n_row),
        out_specs=VM,
        scratch_shapes=[
            pltpu.VMEM((3 * group, 3 * n_row * frames), jnp.float32),
            pltpu.VMEM((group, n_row * frames), jnp.float32),
        ],
        compiler_params=params(40),
        name="kernel_tile",
    )(*row_blocks, *col_blocks)
    shares = lax.all_to_all(partial, "col", 0, 0, tiled=True)
    result = pl.pallas_call(
        functools.partial(finish_kernel, nv),
        out_shape=jax.ShapeDtypeStruct((frames, nv), jnp.float32),
        in_specs=[VM],
        out_specs=VM,
        compiler_params=params(4),
        name="sum_divide",
    )(shares)
    return result.T


def solution(mesh):
    return jax.shard_map(
        functools.partial(per_device, mesh.shape["row"], mesh.shape["col"]),
        mesh=mesh,
        in_specs=(
            P(None, ("row", "col"), None),
            P(None, ("col", "row"), None),
            P(None, ("col", "row")),
        ),
        out_specs=P(None, ("row", "col")),
        check_vma=False,
    )
```

```python
import functools

import jax
import jax.numpy as jnp
from jax import lax
from jax.experimental import pallas as pl
from jax.experimental.pallas import tpu as pltpu
from jax.sharding import PartitionSpec as P

NEWTON = 8
BAND = 2.0
LANES = 128
VM = pl.BlockSpec(memory_space=pltpu.VMEM)
NT = (((1,), (1,)), ((), ()))


def centre(frames):
    return frames - jnp.mean(frames, axis=-1, keepdims=True)


def split(x):
    high = x.astype(jnp.bfloat16)
    low = (x - high.astype(jnp.float32)).astype(jnp.bfloat16)
    return high, low


def pack_kernel(cols_ref, vec_ref, out_ref):
    comps, frames, atoms = cols_ref.shape
    nv = vec_ref.shape[1]
    for comp in range(comps):
        out_ref[comp * frames:(comp + 1) * frames, :] = centre(cols_ref[comp])
    groups = atoms // nv
    step = frames // groups
    out_ref[comps * frames:, :] = jnp.concatenate(
        [vec_ref[group * step:(group + 1) * step, :] for group in range(groups)], axis=1
    )


def join_kernel(n_blocks, *refs):
    joined_ref, again_ref = refs[-2:]
    for at in range(n_blocks):
        joined_ref[at] = refs[at][...]
    again_ref[...] = refs[n_blocks][...]


def eigen_tile(m, half_norm, atoms):
    s00, s01, s02, s10, s11, s12, s20, s21, s22 = m
    coef_two = -2.0 * (
        s00 * s00 + s01 * s01 + s02 * s02 + s10 * s10 + s11 * s11 + s12 * s12 + s20 * s20 + s21 * s21 + s22 * s22
    )
    coef_one = 8.0 * (s00 * s12 * s21 + s11 * s20 * s02 + s22 * s01 * s10) - 8.0 * (
        s00 * s11 * s22 + s12 * s20 * s01 + s21 * s10 * s02
    )
    k00 = s00 + s11 + s22
    k11 = s00 - s11 - s22
    k22 = s11 - s00 - s22
    k33 = s22 - s00 - s11
    k01 = s12 - s21
    k02 = s20 - s02
    k03 = s01 - s10
    k12 = s01 + s10
    k13 = s20 + s02
    k23 = s12 + s21
    top0 = k00 * k11 - k01 * k01
    top1 = k00 * k12 - k01 * k02
    top2 = k00 * k13 - k01 * k03
    top3 = k01 * k12 - k11 * k02
    top4 = k01 * k13 - k11 * k03
    top5 = k02 * k13 - k12 * k03
    low0 = k02 * k13 - k03 * k12
    low1 = k02 * k23 - k03 * k22
    low2 = k02 * k33 - k03 * k23
    low3 = k12 * k23 - k13 * k22
    low4 = k12 * k33 - k13 * k23
    low5 = k22 * k33 - k23 * k23
    coef_zero = top0 * low5 - top1 * low4 + top2 * low3 + top3 * low2 - top4 * low1 + top5 * low0
    eigen = half_norm
    twice = coef_two + coef_two
    for _ in range(NEWTON):
        eigen_sq = eigen * eigen
        value = (eigen_sq + coef_two) * eigen_sq + coef_one * eigen + coef_zero
        slope = (4.0 * eigen_sq + twice) * eigen + coef_one
        eigen = eigen - value / slope
    squared = jnp.maximum(2.0 * (half_norm - eigen) / atoms, 0.0)
    return jnp.exp(-squared / BAND)


def column_side(col_refs, frames, nv, side_ref, norm_ref, vec_ref):
    atoms = col_refs[0].shape[-1]
    groups = atoms // nv
    step = frames // groups
    cols = [
        jnp.concatenate([ref[comp * frames:(comp + 1) * frames, :] for ref in col_refs], axis=0) for comp in range(3)
    ]
    col_square = cols[0] * cols[0] + cols[1] * cols[1] + cols[2] * cols[2]
    norm_ref[...] = lax.dot_general(
        jnp.ones((8, atoms), jnp.float32), col_square, NT,
        precision=lax.Precision.HIGHEST, preferred_element_type=jnp.float32,
    )
    col_high, col_low = split(jnp.concatenate(cols, axis=0))
    side_ref[...] = jnp.concatenate([col_high, col_high, col_low], axis=1)
    lane = lax.broadcasted_iota(jnp.int32, (step, LANES), 1)
    vec_parts = []
    for ref in col_refs:
        for group in range(groups):
            place = group * nv
            piece = ref[3 * frames:, place // LANES * LANES:place // LANES * LANES + LANES]
            if place % LANES:
                piece = pltpu.roll(piece, LANES - place % LANES, 1)
            vec_parts.append(jnp.where(lane < nv, piece, jnp.where(lane == nv, 1.0, 0.0)))
    vec_high, vec_low = split(jnp.concatenate(vec_parts, axis=0))
    vec_ref[...] = jnp.concatenate([vec_high, vec_high, vec_low], axis=0)


def row_part(row_refs, out_refs, side_ref, norm_ref, vec_ref, moment, tile):
    _, frames, atoms = row_refs[0].shape
    count_cols = norm_ref.shape[1]
    per_group = max(1, LANES // frames)
    for first in range(0, len(row_refs), per_group):
        slots = row_refs[first:first + per_group]
        count = len(slots) * frames
        rows = [centre(jnp.concatenate([ref[comp] for ref in slots], axis=0)) for comp in range(3)]
        row_norm = jnp.sum(rows[0] * rows[0] + rows[1] * rows[1] + rows[2] * rows[2], axis=1, keepdims=True)
        row_high, row_low = split(jnp.concatenate(rows, axis=0))
        moment[0:3 * count, :] = lax.dot_general(
            jnp.concatenate([row_high, row_low, row_high], axis=1), side_ref[...], NT,
            preferred_element_type=jnp.float32,
        )
        for at in range(0, count, 8):
            m = [
                moment[a * count + at:a * count + at + 8, b * count_cols:(b + 1) * count_cols]
                for a in range(3) for b in range(3)
            ]
            half_norm = 0.5 * (row_norm[at:at + 8, :] + norm_ref[0:1, :])
            tile[at:at + 8, :] = eigen_tile(m, half_norm, atoms)
        tile_high, tile_low = split(tile[0:count, :])
        product = jnp.dot(
            jnp.concatenate([tile_high, tile_low, tile_high], axis=1), vec_ref[...],
            preferred_element_type=jnp.float32,
        )
        for slot in range(len(slots)):
            out_refs[first + slot][...] = product[slot * frames:(slot + 1) * frames, :]


def early_kernel(n_rows, nv, *refs):
    row_refs, halves, out_refs = refs[:n_rows], refs[n_rows:n_rows + 2], refs[n_rows + 2:2 * n_rows + 2]
    side_ref, norm_ref, vec_ref, moment, tile = refs[2 * n_rows + 2:]
    col_refs = [half.at[at] for half in halves for at in range(half.shape[0])]
    column_side(col_refs, row_refs[0].shape[1], nv, side_ref, norm_ref, vec_ref)
    row_part(row_refs, out_refs, side_ref, norm_ref, vec_ref, moment, tile)


def late_kernel(row_ref, side_ref, norm_ref, vec_ref, out_ref, moment, tile):
    row_part([row_ref], [out_ref], side_ref, norm_ref, vec_ref, moment, tile)


def finish_kernel(nv, *refs):
    total = refs[0][...]
    for ref in refs[1:-1]:
        total = total + ref[...]
    refs[-1][...] = total[:, 0:nv] / total[:, nv:nv + 1]


def partner(at, mask, count):
    return at ^ mask if count & (count - 1) == 0 else (at + mask) % count


def exchange(x, axis, mask, count, back=False):
    pairs = [(at, partner(at, mask, count)) for at in range(count)]
    return lax.ppermute(x, axis, [(to, at) for at, to in pairs] if back else pairs)


def params(megabytes):
    return pltpu.CompilerParams(vmem_limit_bytes=megabytes * 1024 * 1024)


def per_device(n_row, n_col, row_frames, col_frames, vectors):
    comps, frames, atoms = row_frames.shape
    nv = vectors.shape[0]
    f32 = jnp.float32
    count_cols = n_row * frames
    late = n_col // 2
    early = [mask for mask in range(1, n_col) if mask != late]

    early_rows = [exchange(row_frames, "col", mask, n_col) for mask in early]
    packed = pl.pallas_call(
        pack_kernel,
        out_shape=jax.ShapeDtypeStruct((comps * frames + frames * nv // atoms, atoms), f32),
        in_specs=[VM, VM],
        out_specs=VM,
        compiler_params=params(4),
        name="centre_pack",
    )(col_frames, vectors.T)
    same_core = [packed] + [exchange(packed, "row", mask, n_row) for mask in range(2, n_row, 2)]
    joined, rows_again = pl.pallas_call(
        functools.partial(join_kernel, len(same_core)),
        out_shape=[
            jax.ShapeDtypeStruct((len(same_core), *packed.shape), f32),
            jax.ShapeDtypeStruct(row_frames.shape, f32),
        ],
        in_specs=[VM] * (len(same_core) + 1 + len(early)),
        out_specs=[VM, VM],
        compiler_params=params(8),
        name="join",
    )(*same_core, row_frames, *early_rows)
    other_core = exchange(joined, "row", 1, n_row)
    late_rows = exchange(rows_again, "col", late, n_col)

    group = min(1 + len(early), max(1, LANES // frames)) * frames
    work = 2 * frames * 3 * 3 * count_cols * 3 * atoms
    block = jax.ShapeDtypeStruct((frames, LANES), f32)
    *parts, side, norm, vec = pl.pallas_call(
        functools.partial(early_kernel, 1 + len(early), nv),
        out_shape=[block] * (1 + len(early)) + [
            jax.ShapeDtypeStruct((3 * count_cols, 3 * atoms), jnp.bfloat16),
            jax.ShapeDtypeStruct((8, count_cols), f32),
            jax.ShapeDtypeStruct((3 * count_cols, LANES), jnp.bfloat16),
        ],
        in_specs=[VM] * (3 + len(early)),
        out_specs=[VM] * (4 + len(early)),
        scratch_shapes=[pltpu.VMEM((3 * group, 3 * count_cols), f32), pltpu.VMEM((group, count_cols), f32)],
        compiler_params=params(40),
        cost_estimate=pl.CostEstimate(flops=work * (1 + len(early)), bytes_accessed=1 << 22, transcendentals=0),
        name="early_tile",
    )(rows_again, *early_rows, joined, other_core)
    shares = [parts[0]] + [
        exchange(part, "col", mask, n_col, back=True) for mask, part in zip(early, parts[1:])
    ]
    last = pl.pallas_call(
        late_kernel,
        out_shape=block,
        in_specs=[VM] * 4,
        out_specs=VM,
        scratch_shapes=[pltpu.VMEM((3 * frames, 3 * count_cols), f32), pltpu.VMEM((frames, count_cols), f32)],
        compiler_params=params(40),
        cost_estimate=pl.CostEstimate(flops=work, bytes_accessed=1 << 20, transcendentals=0),
        name="late_tile",
    )(late_rows, side, norm, vec)
    shares.append(exchange(last, "col", late, n_col, back=True))
    result = pl.pallas_call(
        functools.partial(finish_kernel, nv),
        out_shape=jax.ShapeDtypeStruct((frames, nv), f32),
        in_specs=[VM] * n_col,
        out_specs=VM,
        compiler_params=params(4),
        name="sum_divide",
    )(*shares)
    return result.T


def solution(mesh):
    return jax.shard_map(
        functools.partial(per_device, mesh.shape["row"], mesh.shape["col"]),
        mesh=mesh,
        in_specs=(
            P(None, ("row", "col"), None),
            P(None, ("col", "row"), None),
            P(None, ("col", "row")),
        ),
        out_specs=P(None, ("row", "col")),
        check_vma=False,
    )
```

```python
import functools

import jax
import jax.numpy as jnp
from jax import lax
from jax.experimental import pallas as pl
from jax.experimental.pallas import tpu as pltpu
from jax.sharding import PartitionSpec as P

NEWTON = 8
BAND = 2.0
LANES = 128
VM = pl.BlockSpec(memory_space=pltpu.VMEM)
NT = (((1,), (1,)), ((), ()))


def centre(frames):
    return frames - jnp.mean(frames, axis=-1, keepdims=True)


def split(x):
    high = x.astype(jnp.bfloat16)
    low = (x - high.astype(jnp.float32)).astype(jnp.bfloat16)
    return high, low


def pack(cols_ref, vec_ref, out_ref):
    comps, frames, atoms = cols_ref.shape
    nv = vec_ref.shape[1]
    for comp in range(comps):
        out_ref[comp * frames:(comp + 1) * frames, :] = centre(cols_ref[comp])
    groups = atoms // nv
    step = frames // groups
    out_ref[comps * frames:, :] = jnp.concatenate(
        [vec_ref[group * step:(group + 1) * step, :] for group in range(groups)], axis=1
    )


def own_kernel(rows_ref, cols_ref, vec_ref, rows_out, packed_out):
    rows_out[0] = rows_ref[...]
    pack(cols_ref, vec_ref, packed_out)


def join_first_kernel(rows_ref, got_rows_ref, packed_ref, got_cols_ref, got_vec_ref, rows_out, blocks_out):
    rows_out[0] = rows_ref[0]
    rows_out[1] = got_rows_ref[...]
    blocks_out[0] = packed_ref[...]
    pack(got_cols_ref, got_vec_ref, blocks_out.at[1])


def join_kernel(*refs):
    pairs = len(refs) // 3
    for at in range(pairs):
        first_ref, second_ref, out_ref = refs[2 * at], refs[2 * at + 1], refs[2 * pairs + at]
        count = first_ref.shape[0]
        out_ref[0:count] = first_ref[...]
        out_ref[count:] = second_ref[...]


def eigen_tile(m, half_norm, atoms):
    s00, s01, s02, s10, s11, s12, s20, s21, s22 = m
    coef_two = -2.0 * (
        s00 * s00 + s01 * s01 + s02 * s02 + s10 * s10 + s11 * s11 + s12 * s12 + s20 * s20 + s21 * s21 + s22 * s22
    )
    coef_one = 8.0 * (s00 * s12 * s21 + s11 * s20 * s02 + s22 * s01 * s10) - 8.0 * (
        s00 * s11 * s22 + s12 * s20 * s01 + s21 * s10 * s02
    )
    k00 = s00 + s11 + s22
    k11 = s00 - s11 - s22
    k22 = s11 - s00 - s22
    k33 = s22 - s00 - s11
    k01 = s12 - s21
    k02 = s20 - s02
    k03 = s01 - s10
    k12 = s01 + s10
    k13 = s20 + s02
    k23 = s12 + s21
    top0 = k00 * k11 - k01 * k01
    top1 = k00 * k12 - k01 * k02
    top2 = k00 * k13 - k01 * k03
    top3 = k01 * k12 - k11 * k02
    top4 = k01 * k13 - k11 * k03
    top5 = k02 * k13 - k12 * k03
    low0 = k02 * k13 - k03 * k12
    low1 = k02 * k23 - k03 * k22
    low2 = k02 * k33 - k03 * k23
    low3 = k12 * k23 - k13 * k22
    low4 = k12 * k33 - k13 * k23
    low5 = k22 * k33 - k23 * k23
    coef_zero = top0 * low5 - top1 * low4 + top2 * low3 + top3 * low2 - top4 * low1 + top5 * low0
    eigen = half_norm
    twice = coef_two + coef_two
    for _ in range(NEWTON):
        eigen_sq = eigen * eigen
        value = (eigen_sq + coef_two) * eigen_sq + coef_one * eigen + coef_zero
        slope = (4.0 * eigen_sq + twice) * eigen + coef_one
        eigen = eigen - value / slope
    squared = jnp.maximum(2.0 * (half_norm - eigen) / atoms, 0.0)
    return jnp.exp(-squared / BAND)


def column_side(blocks_ref, frames, nv):
    count, _, atoms = blocks_ref.shape
    groups = atoms // nv
    step = frames // groups
    cols = [
        jnp.concatenate([blocks_ref[at, comp * frames:(comp + 1) * frames, :] for at in range(count)], axis=0)
        for comp in range(3)
    ]
    col_square = cols[0] * cols[0] + cols[1] * cols[1] + cols[2] * cols[2]
    norm = lax.dot_general(
        jnp.ones((8, atoms), jnp.float32), col_square, NT,
        precision=lax.Precision.HIGHEST, preferred_element_type=jnp.float32,
    )[0:1, :]
    high, low = split(jnp.concatenate(cols, axis=0))
    side = jnp.concatenate([high, high, low], axis=1)
    lane = lax.broadcasted_iota(jnp.int32, (step, LANES), 1)
    vec_parts = []
    for at in range(count):
        for group in range(groups):
            place = group * nv
            piece = blocks_ref[at, 3 * frames:, place // LANES * LANES:place // LANES * LANES + LANES]
            if place % LANES:
                piece = pltpu.roll(piece, LANES - place % LANES, 1)
            vec_parts.append(jnp.where(lane < nv, piece, jnp.where(lane == nv, 1.0, 0.0)))
    high, low = split(jnp.concatenate(vec_parts, axis=0))
    return side, norm, jnp.concatenate([high, high, low], axis=0)


def multiply(row_side, row_norm, side, norm, vec, atoms, moment, tile):
    count = row_norm.shape[0]
    count_cols = norm.shape[1]
    moment[...] = lax.dot_general(row_side, side, NT, preferred_element_type=jnp.float32)
    for at in range(0, count, 8):
        m = [
            moment[a * count + at:a * count + at + 8, b * count_cols:(b + 1) * count_cols]
            for a in range(3) for b in range(3)
        ]
        half_norm = 0.5 * (row_norm[at:at + 8, 0:1] + norm)
        tile[at:at + 8, :] = eigen_tile(m, half_norm, atoms)
    high, low = split(tile[...])
    return jnp.dot(jnp.concatenate([high, low, high], axis=1), vec, preferred_element_type=jnp.float32)


def first_kernel(nv, rows_ref, blocks_ref, sum_ref, side_ref, norm_ref, moment, tile):
    slots = [rows_ref.at[at] for at in range(rows_ref.shape[0])]
    _, frames, atoms = slots[0].shape
    groups, count, _ = sum_ref.shape
    side, norm, vec = column_side(blocks_ref, frames, nv)
    for group in range(groups):
        own = slots[group * count // frames:(group + 1) * count // frames]
        rows = [centre(jnp.concatenate([ref[comp] for ref in own], axis=0)) for comp in range(3)]
        square = jnp.sum(rows[0] * rows[0] + rows[1] * rows[1] + rows[2] * rows[2], axis=1, keepdims=True)
        row_norm = jnp.broadcast_to(square, (count, LANES))
        high, low = split(jnp.concatenate(rows, axis=0))
        row_side = jnp.concatenate([high, low, high], axis=1)
        side_ref[group] = row_side
        norm_ref[group] = row_norm
        sum_ref[group] = multiply(row_side, row_norm, side, norm, vec, atoms, moment, tile)


def second_kernel(nv, frames, keep, send, sum_ref, side_ref, norm_ref, blocks_ref, keep_ref, send_ref, moment, tile):
    atoms = blocks_ref.shape[-1]
    groups, count, _ = sum_ref.shape
    side, norm, vec = column_side(blocks_ref, frames, nv)
    for group in range(groups):
        total = sum_ref[group] + multiply(side_ref[group], norm_ref[group], side, norm, vec, atoms, moment, tile)
        for at in range(count // frames):
            slot = group * count // frames + at
            target = keep_ref.at[keep.index(slot)] if slot in keep else send_ref.at[send.index(slot)]
            target[...] = total[at * frames:(at + 1) * frames, :]


def halve_kernel(own_ref, got_ref, keep_ref, send_ref):
    half = keep_ref.shape[0]
    keep_ref[...] = own_ref[0:half] + got_ref[0:half]
    send_ref[...] = own_ref[half:] + got_ref[half:]


def finish_kernel(nv, own_ref, got_ref, out_ref):
    total = own_ref[0] + got_ref[0]
    out_ref[...] = total[:, 0:nv] / total[:, nv:nv + 1]


def exchange(x, axis, mask, count):
    return lax.ppermute(x, axis, [(at, at ^ mask) for at in range(count)])


def call(kernel, outs, ins, name, scratch=(), megabytes=8, flops=0):
    out_shape = [jax.ShapeDtypeStruct(*out) for out in outs]
    moved = sum(x.size * 4 for x in ins)
    return pl.pallas_call(
        kernel,
        out_shape=out_shape,
        in_specs=[VM] * len(ins),
        out_specs=[VM] * len(outs),
        scratch_shapes=list(scratch),
        compiler_params=pltpu.CompilerParams(vmem_limit_bytes=megabytes * 1024 * 1024),
        cost_estimate=pl.CostEstimate(flops=flops, bytes_accessed=moved, transcendentals=0),
        name=name,
    )(*ins)


def per_device(n_row, n_col, row_frames, col_frames, vectors):
    comps, frames, atoms = row_frames.shape
    nv = vectors.shape[0]
    f32, bf16 = jnp.float32, jnp.bfloat16
    vec_own = vectors.T
    row_masks = [n_col >> at for at in range(1, n_col.bit_length())]
    col_masks = [1 << at for at in range(1, n_row.bit_length() - 1)]

    got_rows = exchange(row_frames, "col", row_masks[0], n_col)
    got_cols = exchange(col_frames, "row", col_masks[0], n_row)
    got_vec = exchange(vec_own, "row", col_masks[0], n_row)
    packed_shape = (comps * frames + frames * nv // atoms, atoms)
    rows, packed = call(
        own_kernel, [((1, *row_frames.shape), f32), (packed_shape, f32)], [row_frames, col_frames, vec_own], "own"
    )
    rows, blocks = call(
        join_first_kernel, [((2, *row_frames.shape), f32), ((2, *packed_shape), f32)],
        [rows, got_rows, packed, got_cols, got_vec], "join",
    )
    order = [0, row_masks[0]]
    for at in range(1, max(len(row_masks), len(col_masks))):
        joins = []
        if at < len(row_masks):
            joins += [rows, exchange(rows, "col", row_masks[at], n_col)]
            order = order + [row_masks[at] ^ slot for slot in order]
        if at < len(col_masks):
            joins += [blocks, exchange(blocks, "row", col_masks[at], n_row)]
        joined = call(join_kernel, [((2 * x.shape[0], *x.shape[1:]), f32) for x in joins[::2]], joins, "join")
        if at < len(col_masks):
            blocks = joined[-1]
        if at < len(row_masks):
            rows = joined[0]
    other = exchange(blocks, "row", 1, n_row)

    half_cols = n_row // 2 * frames
    count = min(n_col, max(1, LANES // frames)) * frames
    groups = n_col * frames // count
    scratch = [pltpu.VMEM((3 * count, 3 * half_cols), f32), pltpu.VMEM((count, half_cols), f32)]
    work = 2 * 3 * n_col * frames * 3 * half_cols * 3 * atoms
    sums, side, norm = call(
        functools.partial(first_kernel, nv),
        [((groups, count, LANES), f32), ((groups, 3 * count, 3 * atoms), bf16), ((groups, count, LANES), f32)],
        [rows, blocks], "first_tile", scratch, 32, work,
    )
    middle = n_col // 2
    keep = [order.index(mask) for mask in range(middle)]
    send = [order.index(mask) for mask in range(middle, n_col)]
    near, far = call(
        functools.partial(second_kernel, nv, frames, keep, send),
        [((middle, frames, LANES), f32)] * 2,
        [sums, side, norm, other], "second_tile", scratch, 32, work,
    )
    for mask in row_masks[:-1]:
        got = exchange(far, "col", mask, n_col)
        middle //= 2
        near, far = call(halve_kernel, [((middle, frames, LANES), f32)] * 2, [near, got], "halve")
    got = exchange(far, "col", 1, n_col)
    (result,) = call(functools.partial(finish_kernel, nv), [((frames, nv), f32)], [near, got], "sum_divide")
    return result.T


def solution(mesh):
    return jax.shard_map(
        functools.partial(per_device, mesh.shape["row"], mesh.shape["col"]),
        mesh=mesh,
        in_specs=(
            P(None, ("row", "col"), None),
            P(None, ("col", "row"), None),
            P(None, ("col", "row")),
        ),
        out_specs=P(None, ("row", "col")),
        check_vma=False,
    )
```

```python
import functools

import jax
import jax.numpy as jnp
from jax import lax
from jax.experimental import pallas as pl
from jax.experimental.pallas import tpu as pltpu
from jax.sharding import PartitionSpec as P

NEWTON = 8
BAND = 2.0
LANES = 128
VM = pl.BlockSpec(memory_space=pltpu.VMEM)
NT = (((1,), (1,)), ((), ()))


def centre(frames):
    return frames - jnp.mean(frames, axis=-1, keepdims=True)


def split(x):
    high = x.astype(jnp.bfloat16)
    low = (x - high.astype(jnp.float32)).astype(jnp.bfloat16)
    return high, low


def pack(cols_ref, vec_ref, out_ref):
    comps, frames, atoms = cols_ref.shape
    nv = vec_ref.shape[1]
    for comp in range(comps):
        out_ref[comp * frames:(comp + 1) * frames, :] = centre(cols_ref[comp])
    groups = atoms // nv
    step = frames // groups
    out_ref[comps * frames:, :] = jnp.concatenate(
        [vec_ref[group * step:(group + 1) * step, :] for group in range(groups)], axis=1
    )


def own_kernel(rows_ref, cols_ref, vec_ref, rows_out, packed_out):
    rows_out[...] = rows_ref[...]
    pack(cols_ref, vec_ref, packed_out)


def after_first_kernel(packed_ref, x_cols_ref, x_vec_ref, far_ref, y_cols_ref, near_ref, pair_out, send_out, far_out):
    del y_cols_ref, near_ref
    used = packed_ref.shape[0]
    frames = 3 * x_cols_ref.shape[1]
    pair_out[0] = packed_ref[...]
    pack(x_cols_ref, x_vec_ref, pair_out.at[1])
    send_out[0:used, :] = pair_out[1]
    send_out[used:, :] = packed_ref[frames:, :]
    far_out[...] = far_ref[...]


def after_second_kernel(pair_ref, y_cols_ref, got_ref, own_ref, far_ref, near_ref, both_ref, blocks_out, rows_out):
    used = pair_ref.shape[1]
    frames = y_cols_ref.shape[1]
    blocks_out[0:2] = pair_ref[...]
    for comp in range(3):
        blocks_out[2, comp * frames:(comp + 1) * frames, :] = centre(y_cols_ref[comp])
    blocks_out[2, 3 * frames:, :] = got_ref[used:, :]
    blocks_out[3] = got_ref[0:used, :]
    for at, ref in enumerate((own_ref, far_ref, near_ref, both_ref)):
        rows_out[at] = ref[...]


def join_kernel(*refs):
    pairs = len(refs) // 3
    for at in range(pairs):
        first_ref, second_ref, out_ref = refs[2 * at], refs[2 * at + 1], refs[2 * pairs + at]
        count = first_ref.shape[0]
        out_ref[0:count] = first_ref[...]
        out_ref[count:] = second_ref[...]


def inverse(x):
    guess = pl.reciprocal(x, approx=True)
    return guess * (2.0 - x * guess)


def eigen_tile(m, half_norm, atoms):
    s00, s01, s02, s10, s11, s12, s20, s21, s22 = m
    coef_two = -2.0 * (
        s00 * s00 + s01 * s01 + s02 * s02 + s10 * s10 + s11 * s11 + s12 * s12 + s20 * s20 + s21 * s21 + s22 * s22
    )
    coef_one = 8.0 * (s00 * s12 * s21 + s11 * s20 * s02 + s22 * s01 * s10) - 8.0 * (
        s00 * s11 * s22 + s12 * s20 * s01 + s21 * s10 * s02
    )
    k00 = s00 + s11 + s22
    k11 = s00 - s11 - s22
    k22 = s11 - s00 - s22
    k33 = s22 - s00 - s11
    k01 = s12 - s21
    k02 = s20 - s02
    k03 = s01 - s10
    k12 = s01 + s10
    k13 = s20 + s02
    k23 = s12 + s21
    top0 = k00 * k11 - k01 * k01
    top1 = k00 * k12 - k01 * k02
    top2 = k00 * k13 - k01 * k03
    top3 = k01 * k12 - k11 * k02
    top4 = k01 * k13 - k11 * k03
    top5 = k02 * k13 - k12 * k03
    low0 = k02 * k13 - k03 * k12
    low1 = k02 * k23 - k03 * k22
    low2 = k02 * k33 - k03 * k23
    low3 = k12 * k23 - k13 * k22
    low4 = k12 * k33 - k13 * k23
    low5 = k22 * k33 - k23 * k23
    coef_zero = top0 * low5 - top1 * low4 + top2 * low3 + top3 * low2 - top4 * low1 + top5 * low0
    eigen = half_norm
    twice = coef_two + coef_two
    for _ in range(NEWTON):
        eigen_sq = eigen * eigen
        value = (eigen_sq + coef_two) * eigen_sq + coef_one * eigen + coef_zero
        slope = (4.0 * eigen_sq + twice) * eigen + coef_one
        eigen = eigen - value * inverse(slope)
    squared = jnp.maximum(2.0 * (half_norm - eigen) / atoms, 0.0)
    return jnp.exp(-squared / BAND)


def column_side(blocks_ref, frames, nv):
    count, _, atoms = blocks_ref.shape
    groups = atoms // nv
    step = frames // groups
    cols = [
        jnp.concatenate([blocks_ref[at, comp * frames:(comp + 1) * frames, :] for at in range(count)], axis=0)
        for comp in range(3)
    ]
    col_square = cols[0] * cols[0] + cols[1] * cols[1] + cols[2] * cols[2]
    norm = lax.dot_general(
        jnp.ones((8, atoms), jnp.float32), col_square, NT,
        precision=lax.Precision.HIGHEST, preferred_element_type=jnp.float32,
    )[0:1, :]
    high, low = split(jnp.concatenate(cols, axis=0))
    side = jnp.concatenate([high, high, low], axis=1)
    lane = lax.broadcasted_iota(jnp.int32, (step, LANES), 1)
    vec_parts = []
    for at in range(count):
        for group in range(groups):
            place = group * nv
            piece = blocks_ref[at, 3 * frames:, place // LANES * LANES:place // LANES * LANES + LANES]
            if place % LANES:
                piece = pltpu.roll(piece, LANES - place % LANES, 1)
            vec_parts.append(jnp.where(lane < nv, piece, jnp.where(lane == nv, 1.0, 0.0)))
    high, low = split(jnp.concatenate(vec_parts, axis=0))
    return side, norm, jnp.concatenate([high, high, low], axis=0)


def multiply(row_side, row_norm, side, norm, vec, atoms, moment, tile):
    count = row_norm.shape[0]
    count_cols = norm.shape[1]
    moment[...] = lax.dot_general(row_side, side, NT, preferred_element_type=jnp.float32)
    for at in range(0, count, 8):
        m = [
            moment[a * count + at:a * count + at + 8, b * count_cols:(b + 1) * count_cols]
            for a in range(3) for b in range(3)
        ]
        half_norm = 0.5 * (row_norm[at:at + 8, 0:1] + norm)
        tile[at:at + 8, :] = eigen_tile(m, half_norm, atoms)
    high, low = split(tile[...])
    return jnp.dot(jnp.concatenate([high, low, high], axis=1), vec, preferred_element_type=jnp.float32)


def first_kernel(nv, rows_ref, blocks_ref, sum_ref, side_ref, norm_ref, moment, tile):
    slots = [rows_ref.at[at] for at in range(rows_ref.shape[0])]
    _, frames, atoms = slots[0].shape
    groups, count, _ = sum_ref.shape
    side, norm, vec = column_side(blocks_ref, frames, nv)
    for group in range(groups):
        own = slots[group * count // frames:(group + 1) * count // frames]
        rows = [centre(jnp.concatenate([ref[comp] for ref in own], axis=0)) for comp in range(3)]
        square = jnp.sum(rows[0] * rows[0] + rows[1] * rows[1] + rows[2] * rows[2], axis=1, keepdims=True)
        row_norm = jnp.broadcast_to(square, (count, LANES))
        high, low = split(jnp.concatenate(rows, axis=0))
        row_side = jnp.concatenate([high, low, high], axis=1)
        side_ref[group] = row_side
        norm_ref[group] = row_norm
        sum_ref[group] = multiply(row_side, row_norm, side, norm, vec, atoms, moment, tile)


def second_kernel(nv, frames, sum_ref, side_ref, norm_ref, blocks_ref, *refs):
    moment, tile = refs[-2:]
    atoms = blocks_ref.shape[-1]
    groups, count, _ = sum_ref.shape
    side, norm, vec = column_side(blocks_ref, frames, nv)
    for group in range(groups):
        total = sum_ref[group] + multiply(side_ref[group], norm_ref[group], side, norm, vec, atoms, moment, tile)
        for at in range(count // frames):
            refs[group * count // frames + at][...] = total[at * frames:(at + 1) * frames, :]


def finish_kernel(nv, *refs):
    total = refs[0][...]
    for ref in refs[1:-1]:
        total = total + ref[...]
    refs[-1][...] = total[:, 0:nv] / total[:, nv:nv + 1]


def exchange(x, axis, mask, count):
    return lax.ppermute(x, axis, [(at, at ^ mask) for at in range(count)])


def call(kernel, outs, ins, name, scratch=(), megabytes=8, flops=0):
    out_shape = [jax.ShapeDtypeStruct(*out) for out in outs]
    moved = sum(x.size * 4 for x in ins)
    return pl.pallas_call(
        kernel,
        out_shape=out_shape,
        in_specs=[VM] * len(ins),
        out_specs=[VM] * len(outs),
        scratch_shapes=list(scratch),
        compiler_params=pltpu.CompilerParams(vmem_limit_bytes=megabytes * 1024 * 1024),
        cost_estimate=pl.CostEstimate(flops=flops, bytes_accessed=moved, transcendentals=0),
        name=name,
    )(*ins)


def per_device(n_row, n_col, row_frames, col_frames, vectors):
    comps, frames, atoms = row_frames.shape
    nv = vectors.shape[0]
    f32, bf16 = jnp.float32, jnp.bfloat16
    vec_own = vectors.T
    row_masks = [n_col >> at for at in range(1, n_col.bit_length())]
    col_masks = [1 << at for at in range(1, n_row.bit_length() - 1)]

    far = exchange(row_frames, "col", row_masks[0], n_col)
    x_cols = exchange(col_frames, "row", col_masks[0], n_row)
    y_cols = exchange(col_frames, "row", col_masks[1], n_row)
    near = exchange(row_frames, "col", row_masks[1], n_col)
    x_vec = exchange(vec_own, "row", col_masks[0], n_row)
    extra = frames * nv // atoms
    packed_shape = (comps * frames + extra, atoms)
    own, packed = call(
        own_kernel, [(row_frames.shape, f32), (packed_shape, f32)], [row_frames, col_frames, vec_own], "own"
    )
    pair, onward, far = call(
        after_first_kernel,
        [((2, *packed_shape), f32), ((packed_shape[0] + extra, atoms), f32), (row_frames.shape, f32)],
        [packed, x_cols, x_vec, far, y_cols, near], "after_first",
    )
    both = exchange(far, "col", row_masks[1], n_col)
    xy = exchange(onward, "row", col_masks[1], n_row)
    blocks, rows = call(
        after_second_kernel, [((4, *packed_shape), f32), ((4, *row_frames.shape), f32)],
        [pair, y_cols, xy, own, far, near, both], "after_second",
    )
    order = [0, row_masks[0], row_masks[1], row_masks[0] ^ row_masks[1]]
    for at in range(2, max(len(row_masks), len(col_masks))):
        joins = []
        if at < len(row_masks):
            joins += [rows, exchange(rows, "col", row_masks[at], n_col)]
            order = order + [row_masks[at] ^ slot for slot in order]
        if at < len(col_masks):
            joins += [blocks, exchange(blocks, "row", col_masks[at], n_row)]
        joined = call(join_kernel, [((2 * x.shape[0], *x.shape[1:]), f32) for x in joins[::2]], joins, "join")
        if at < len(col_masks):
            blocks = joined[-1]
        if at < len(row_masks):
            rows = joined[0]
    other = exchange(blocks, "row", 1, n_row)

    half_cols = n_row // 2 * frames
    count = min(n_col, max(1, LANES // frames)) * frames
    groups = n_col * frames // count
    scratch = [pltpu.VMEM((3 * count, 3 * half_cols), f32), pltpu.VMEM((count, half_cols), f32)]
    work = 2 * 3 * n_col * frames * 3 * half_cols * 3 * atoms
    sums, side, norm = call(
        functools.partial(first_kernel, nv),
        [((groups, count, LANES), f32), ((groups, 3 * count, 3 * atoms), bf16), ((groups, count, LANES), f32)],
        [rows, blocks], "first_tile", scratch, 32, work,
    )
    parts = call(
        functools.partial(second_kernel, nv, frames), [((frames, LANES), f32)] * n_col,
        [sums, side, norm, other], "second_tile", scratch, 32, work,
    )
    shares = [parts[0]] + [
        exchange(parts[order.index(mask)], "col", mask, n_col) for mask in range(n_col - 1, 0, -1)
    ]
    (result,) = call(functools.partial(finish_kernel, nv), [((frames, nv), f32)], shares, "sum_divide")
    return result.T


def solution(mesh):
    return jax.shard_map(
        functools.partial(per_device, mesh.shape["row"], mesh.shape["col"]),
        mesh=mesh,
        in_specs=(
            P(None, ("row", "col"), None),
            P(None, ("col", "row"), None),
            P(None, ("col", "row")),
        ),
        out_specs=P(None, ("row", "col")),
        check_vma=False,
    )
```

```python
import functools

import jax
import jax.numpy as jnp
from jax import lax
from jax.experimental import pallas as pl
from jax.experimental.pallas import tpu as pltpu
from jax.sharding import PartitionSpec as P

NEWTON = 8
BAND = 2.0
LANES = 128
VM = pl.BlockSpec(memory_space=pltpu.VMEM)
NT = (((1,), (1,)), ((), ()))


def centre(frames):
    return frames - jnp.mean(frames, axis=-1, keepdims=True)


def split(x):
    high = x.astype(jnp.bfloat16)
    low = (x - high.astype(jnp.float32)).astype(jnp.bfloat16)
    return high, low


def pack(cols_ref, vec_ref, out_ref):
    comps, frames, atoms = cols_ref.shape
    nv = vec_ref.shape[1]
    for comp in range(comps):
        out_ref[comp * frames:(comp + 1) * frames, :] = centre(cols_ref[comp])
    out_ref[comps * frames:, :] = pack_vectors(vec_ref, atoms // nv)


def own_kernel(rows_ref, cols_ref, extra_ref, after_ref, rows_out, packed_out):
    del after_ref
    rows_out[...] = rows_ref[...]
    frames = cols_ref.shape[1]
    for comp in range(3):
        packed_out[comp * frames:(comp + 1) * frames, :] = centre(cols_ref[comp])
    packed_out[3 * frames:, :] = extra_ref[...]


def pack_vectors(vec_ref, groups):
    step = vec_ref.shape[0] // groups
    return jnp.concatenate([vec_ref[group * step:(group + 1) * step, :] for group in range(groups)], axis=1)


def vectors_kernel(vec_ref, out_ref):
    out_ref[...] = pack_vectors(vec_ref, out_ref.shape[1] // vec_ref.shape[1])


def after_first_kernel(extra_ref, x_cols_ref, x_vec_ref, far_ref, y_cols_ref, near_ref, send_out, far_out):
    del y_cols_ref, near_ref
    used = send_out.shape[0] - extra_ref.shape[0]
    pack(x_cols_ref, x_vec_ref, send_out.at[0:used])
    send_out[used:, :] = extra_ref[...]
    far_out[...] = far_ref[...]


def after_second_kernel(
    packed_ref, sent_ref, y_cols_ref, got_ref, own_ref, far_ref, near_ref, both_ref, blocks_out, rows_out
):
    used = packed_ref.shape[0]
    frames = y_cols_ref.shape[1]
    blocks_out[0] = packed_ref[...]
    blocks_out[1] = sent_ref[0:used, :]
    for comp in range(3):
        blocks_out[2, comp * frames:(comp + 1) * frames, :] = centre(y_cols_ref[comp])
    blocks_out[2, 3 * frames:, :] = got_ref[used:, :]
    blocks_out[3] = got_ref[0:used, :]
    for at, ref in enumerate((own_ref, far_ref, near_ref, both_ref)):
        rows_out[at] = ref[...]


def join_kernel(*refs):
    pairs = len(refs) // 3
    for at in range(pairs):
        first_ref, second_ref, out_ref = refs[2 * at], refs[2 * at + 1], refs[2 * pairs + at]
        count = first_ref.shape[0]
        out_ref[0:count] = first_ref[...]
        out_ref[count:] = second_ref[...]


def inverse(x):
    guess = pl.reciprocal(x, approx=True)
    return guess * (2.0 - x * guess)


def eigen_tile(m, half_norm, atoms):
    s00, s01, s02, s10, s11, s12, s20, s21, s22 = m
    coef_two = -2.0 * (
        s00 * s00 + s01 * s01 + s02 * s02 + s10 * s10 + s11 * s11 + s12 * s12 + s20 * s20 + s21 * s21 + s22 * s22
    )
    coef_one = 8.0 * (s00 * s12 * s21 + s11 * s20 * s02 + s22 * s01 * s10) - 8.0 * (
        s00 * s11 * s22 + s12 * s20 * s01 + s21 * s10 * s02
    )
    k00 = s00 + s11 + s22
    k11 = s00 - s11 - s22
    k22 = s11 - s00 - s22
    k33 = s22 - s00 - s11
    k01 = s12 - s21
    k02 = s20 - s02
    k03 = s01 - s10
    k12 = s01 + s10
    k13 = s20 + s02
    k23 = s12 + s21
    top0 = k00 * k11 - k01 * k01
    top1 = k00 * k12 - k01 * k02
    top2 = k00 * k13 - k01 * k03
    top3 = k01 * k12 - k11 * k02
    top4 = k01 * k13 - k11 * k03
    top5 = k02 * k13 - k12 * k03
    low0 = k02 * k13 - k03 * k12
    low1 = k02 * k23 - k03 * k22
    low2 = k02 * k33 - k03 * k23
    low3 = k12 * k23 - k13 * k22
    low4 = k12 * k33 - k13 * k23
    low5 = k22 * k33 - k23 * k23
    coef_zero = top0 * low5 - top1 * low4 + top2 * low3 + top3 * low2 - top4 * low1 + top5 * low0
    eigen = half_norm
    twice = coef_two + coef_two
    for _ in range(NEWTON):
        eigen_sq = eigen * eigen
        value = (eigen_sq + coef_two) * eigen_sq + coef_one * eigen + coef_zero
        slope = (4.0 * eigen_sq + twice) * eigen + coef_one
        eigen = eigen - value * inverse(slope)
    squared = jnp.maximum(2.0 * (half_norm - eigen) / atoms, 0.0)
    return jnp.exp(-squared / BAND)


def column_side(blocks_ref, frames, nv):
    count, _, atoms = blocks_ref.shape
    groups = atoms // nv
    step = frames // groups
    cols = [
        jnp.concatenate([blocks_ref[at, comp * frames:(comp + 1) * frames, :] for at in range(count)], axis=0)
        for comp in range(3)
    ]
    col_square = cols[0] * cols[0] + cols[1] * cols[1] + cols[2] * cols[2]
    norm = lax.dot_general(
        jnp.ones((8, atoms), jnp.float32), col_square, NT,
        precision=lax.Precision.HIGHEST, preferred_element_type=jnp.float32,
    )[0:1, :]
    high, low = split(jnp.concatenate(cols, axis=0))
    side = jnp.concatenate([high, high, low], axis=1)
    lane = lax.broadcasted_iota(jnp.int32, (step, LANES), 1)
    vec_parts = []
    for at in range(count):
        for group in range(groups):
            place = group * nv
            piece = blocks_ref[at, 3 * frames:, place // LANES * LANES:place // LANES * LANES + LANES]
            if place % LANES:
                piece = pltpu.roll(piece, LANES - place % LANES, 1)
            vec_parts.append(jnp.where(lane < nv, piece, jnp.where(lane == nv, 1.0, 0.0)))
    high, low = split(jnp.concatenate(vec_parts, axis=0))
    return side, norm, jnp.concatenate([high, high, low], axis=0)


def multiply(row_side, row_norm, side, norm, vec, atoms, moment, tile):
    count = row_norm.shape[0]
    count_cols = norm.shape[1]
    moment[...] = lax.dot_general(row_side, side, NT, preferred_element_type=jnp.float32)
    for at in range(0, count, 8):
        m = [
            moment[a * count + at:a * count + at + 8, b * count_cols:(b + 1) * count_cols]
            for a in range(3) for b in range(3)
        ]
        half_norm = 0.5 * (row_norm[at:at + 8, 0:1] + norm)
        tile[at:at + 8, :] = eigen_tile(m, half_norm, atoms)
    high, low = split(tile[...])
    return jnp.dot(jnp.concatenate([high, low, high], axis=1), vec, preferred_element_type=jnp.float32)


def first_kernel(nv, rows_ref, blocks_ref, sum_ref, side_ref, norm_ref, moment, tile):
    slots = [rows_ref.at[at] for at in range(rows_ref.shape[0])]
    _, frames, atoms = slots[0].shape
    groups, count, _ = sum_ref.shape
    side, norm, vec = column_side(blocks_ref, frames, nv)
    for group in range(groups):
        own = slots[group * count // frames:(group + 1) * count // frames]
        rows = [centre(jnp.concatenate([ref[comp] for ref in own], axis=0)) for comp in range(3)]
        square = jnp.sum(rows[0] * rows[0] + rows[1] * rows[1] + rows[2] * rows[2], axis=1, keepdims=True)
        row_norm = jnp.broadcast_to(square, (count, LANES))
        high, low = split(jnp.concatenate(rows, axis=0))
        row_side = jnp.concatenate([high, low, high], axis=1)
        side_ref[group] = row_side
        norm_ref[group] = row_norm
        sum_ref[group] = multiply(row_side, row_norm, side, norm, vec, atoms, moment, tile)


def second_kernel(nv, frames, sum_ref, side_ref, norm_ref, blocks_ref, *refs):
    moment, tile = refs[-2:]
    atoms = blocks_ref.shape[-1]
    groups, count, _ = sum_ref.shape
    side, norm, vec = column_side(blocks_ref, frames, nv)
    for group in range(groups):
        total = sum_ref[group] + multiply(side_ref[group], norm_ref[group], side, norm, vec, atoms, moment, tile)
        for at in range(count // frames):
            refs[group * count // frames + at][...] = total[at * frames:(at + 1) * frames, :]


def finish_kernel(nv, *refs):
    total = refs[0][...]
    for ref in refs[1:-1]:
        total = total + ref[...]
    refs[-1][...] = total[:, 0:nv] / total[:, nv:nv + 1]


def exchange(x, axis, mask, count):
    return lax.ppermute(x, axis, [(at, at ^ mask) for at in range(count)])


def call(kernel, outs, ins, name, scratch=(), megabytes=8, flops=0):
    out_shape = [jax.ShapeDtypeStruct(*out) for out in outs]
    moved = sum(x.size * 4 for x in ins)
    return pl.pallas_call(
        kernel,
        out_shape=out_shape,
        in_specs=[VM] * len(ins),
        out_specs=[VM] * len(outs),
        scratch_shapes=list(scratch),
        compiler_params=pltpu.CompilerParams(vmem_limit_bytes=megabytes * 1024 * 1024),
        cost_estimate=pl.CostEstimate(flops=flops, bytes_accessed=moved, transcendentals=0),
        name=name,
    )(*ins)


def per_device(n_row, n_col, row_frames, col_frames, vectors):
    comps, frames, atoms = row_frames.shape
    nv = vectors.shape[0]
    f32, bf16 = jnp.float32, jnp.bfloat16
    vec_own = vectors.T
    row_masks = [n_col >> at for at in range(1, n_col.bit_length())]
    col_masks = [1 << at for at in range(1, n_row.bit_length() - 1)]

    far = exchange(row_frames, "col", row_masks[0], n_col)
    x_cols = exchange(col_frames, "row", col_masks[0], n_row)
    y_cols = exchange(col_frames, "row", col_masks[1], n_row)
    near = exchange(row_frames, "col", row_masks[1], n_col)
    x_vec = exchange(vec_own, "row", col_masks[0], n_row)
    extra = frames * nv // atoms
    packed_shape = (comps * frames + extra, atoms)
    (own_extra,) = call(vectors_kernel, [((extra, atoms), f32)], [vec_own], "vectors", flops=1 << 30)
    onward, far = call(
        after_first_kernel,
        [((packed_shape[0] + extra, atoms), f32), (row_frames.shape, f32)],
        [own_extra, x_cols, x_vec, far, y_cols, near], "after_first",
    )
    both = exchange(far, "col", row_masks[1], n_col)
    xy = exchange(onward, "row", col_masks[1], n_row)
    own, packed = call(
        own_kernel, [(row_frames.shape, f32), (packed_shape, f32)], [row_frames, col_frames, own_extra, far], "own",
        flops=1 << 30,
    )
    blocks, rows = call(
        after_second_kernel, [((4, *packed_shape), f32), ((4, *row_frames.shape), f32)],
        [packed, onward, y_cols, xy, own, far, near, both], "after_second",
    )
    order = [0, row_masks[0], row_masks[1], row_masks[0] ^ row_masks[1]]
    for at in range(2, max(len(row_masks), len(col_masks))):
        joins = []
        if at < len(row_masks):
            joins += [rows, exchange(rows, "col", row_masks[at], n_col)]
            order = order + [row_masks[at] ^ slot for slot in order]
        if at < len(col_masks):
            joins += [blocks, exchange(blocks, "row", col_masks[at], n_row)]
        joined = call(join_kernel, [((2 * x.shape[0], *x.shape[1:]), f32) for x in joins[::2]], joins, "join")
        if at < len(col_masks):
            blocks = joined[-1]
        if at < len(row_masks):
            rows = joined[0]
    other = exchange(blocks, "row", 1, n_row)

    half_cols = n_row // 2 * frames
    count = min(n_col, max(1, LANES // frames)) * frames
    groups = n_col * frames // count
    scratch = [pltpu.VMEM((3 * count, 3 * half_cols), f32), pltpu.VMEM((count, half_cols), f32)]
    work = 2 * 3 * n_col * frames * 3 * half_cols * 3 * atoms
    sums, side, norm = call(
        functools.partial(first_kernel, nv),
        [((groups, count, LANES), f32), ((groups, 3 * count, 3 * atoms), bf16), ((groups, count, LANES), f32)],
        [rows, blocks], "first_tile", scratch, 32, work,
    )
    parts = call(
        functools.partial(second_kernel, nv, frames), [((frames, LANES), f32)] * n_col,
        [sums, side, norm, other], "second_tile", scratch, 32, work,
    )
    shares = [parts[0]] + [
        exchange(parts[order.index(mask)], "col", mask, n_col) for mask in range(n_col - 1, 0, -1)
    ]
    (result,) = call(functools.partial(finish_kernel, nv), [((frames, nv), f32)], shares, "sum_divide")
    return result.T


def solution(mesh):
    return jax.shard_map(
        functools.partial(per_device, mesh.shape["row"], mesh.shape["col"]),
        mesh=mesh,
        in_specs=(
            P(None, ("row", "col"), None),
            P(None, ("col", "row"), None),
            P(None, ("col", "row")),
        ),
        out_specs=P(None, ("row", "col")),
        check_vma=False,
    )
```

```python
import functools

import jax
import jax.numpy as jnp
from jax import lax
from jax.experimental import pallas as pl
from jax.experimental.pallas import tpu as pltpu
from jax.sharding import PartitionSpec as P

NEWTON = 8
BAND = 2.0
LANES = 128
VM = pl.BlockSpec(memory_space=pltpu.VMEM)
NT = (((1,), (1,)), ((), ()))


def centre(frames):
    return frames - jnp.mean(frames, axis=-1, keepdims=True)


def split(x):
    high = x.astype(jnp.bfloat16)
    low = (x - high.astype(jnp.float32)).astype(jnp.bfloat16)
    return high, low


def pack(cols_ref, vec_ref, out_ref):
    comps, frames, atoms = cols_ref.shape
    nv = vec_ref.shape[1]
    for comp in range(comps):
        out_ref[comp * frames:(comp + 1) * frames, :] = centre(cols_ref[comp])
    out_ref[comps * frames:, :] = pack_vectors(vec_ref, atoms // nv)


def own_kernel(rows_ref, cols_ref, extra_ref, after_ref, rows_out, packed_out):
    del after_ref
    rows_out[...] = rows_ref[...]
    frames = cols_ref.shape[1]
    for comp in range(3):
        packed_out[comp * frames:(comp + 1) * frames, :] = centre(cols_ref[comp])
    packed_out[3 * frames:, :] = extra_ref[...]


def pack_vectors(vec_ref, groups):
    step = vec_ref.shape[0] // groups
    return jnp.concatenate([vec_ref[group * step:(group + 1) * step, :] for group in range(groups)], axis=1)


def vectors_kernel(vec_ref, out_ref):
    out_ref[...] = pack_vectors(vec_ref, out_ref.shape[1] // vec_ref.shape[1])


def after_first_kernel(extra_ref, first_cols_ref, first_vec_ref, far_ref, second_cols_ref, near_ref, send_out, far_out):
    del second_cols_ref, near_ref
    used = send_out.shape[0] - extra_ref.shape[0]
    pack(first_cols_ref, first_vec_ref, send_out.at[0:used])
    send_out[used:, :] = extra_ref[...]
    far_out[...] = far_ref[...]


def after_second_kernel(
    packed_ref, sent_ref, second_cols_ref, got_ref, own_ref, far_ref, near_ref, both_ref, blocks_out, rows_out
):
    used = packed_ref.shape[0]
    frames = second_cols_ref.shape[1]
    blocks_out[0] = packed_ref[...]
    blocks_out[1] = sent_ref[0:used, :]
    for comp in range(3):
        blocks_out[2, comp * frames:(comp + 1) * frames, :] = centre(second_cols_ref[comp])
    blocks_out[2, 3 * frames:, :] = got_ref[used:, :]
    blocks_out[3] = got_ref[0:used, :]
    for at, ref in enumerate((own_ref, far_ref, near_ref, both_ref)):
        rows_out[at] = ref[...]


def join_kernel(*refs):
    pairs = len(refs) // 3
    for at in range(pairs):
        first_ref, second_ref, out_ref = refs[2 * at], refs[2 * at + 1], refs[2 * pairs + at]
        count = first_ref.shape[0]
        out_ref[0:count] = first_ref[...]
        out_ref[count:] = second_ref[...]


def inverse(x):
    guess = pl.reciprocal(x, approx=True)
    return guess * (2.0 - x * guess)


def eigen_tile(m, half_norm, atoms):
    s00, s01, s02, s10, s11, s12, s20, s21, s22 = m
    coef_two = -2.0 * (
        s00 * s00 + s01 * s01 + s02 * s02 + s10 * s10 + s11 * s11 + s12 * s12 + s20 * s20 + s21 * s21 + s22 * s22
    )
    coef_one = 8.0 * (s00 * s12 * s21 + s11 * s20 * s02 + s22 * s01 * s10) - 8.0 * (
        s00 * s11 * s22 + s12 * s20 * s01 + s21 * s10 * s02
    )
    k00 = s00 + s11 + s22
    k11 = s00 - s11 - s22
    k22 = s11 - s00 - s22
    k33 = s22 - s00 - s11
    k01 = s12 - s21
    k02 = s20 - s02
    k03 = s01 - s10
    k12 = s01 + s10
    k13 = s20 + s02
    k23 = s12 + s21
    top0 = k00 * k11 - k01 * k01
    top1 = k00 * k12 - k01 * k02
    top2 = k00 * k13 - k01 * k03
    top3 = k01 * k12 - k11 * k02
    top4 = k01 * k13 - k11 * k03
    top5 = k02 * k13 - k12 * k03
    low0 = k02 * k13 - k03 * k12
    low1 = k02 * k23 - k03 * k22
    low2 = k02 * k33 - k03 * k23
    low3 = k12 * k23 - k13 * k22
    low4 = k12 * k33 - k13 * k23
    low5 = k22 * k33 - k23 * k23
    coef_zero = top0 * low5 - top1 * low4 + top2 * low3 + top3 * low2 - top4 * low1 + top5 * low0
    eigen = half_norm
    twice = coef_two + coef_two
    for _ in range(NEWTON):
        eigen_sq = eigen * eigen
        value = (eigen_sq + coef_two) * eigen_sq + coef_one * eigen + coef_zero
        slope = (4.0 * eigen_sq + twice) * eigen + coef_one
        eigen = eigen - value * inverse(slope)
    squared = jnp.maximum(2.0 * (half_norm - eigen) / atoms, 0.0)
    return jnp.exp(-squared / BAND)


def column_side(blocks_ref, frames, nv):
    count, _, atoms = blocks_ref.shape
    groups = atoms // nv
    step = frames // groups
    cols = [
        jnp.concatenate([blocks_ref[at, comp * frames:(comp + 1) * frames, :] for at in range(count)], axis=0)
        for comp in range(3)
    ]
    col_square = cols[0] * cols[0] + cols[1] * cols[1] + cols[2] * cols[2]
    norm = lax.dot_general(
        jnp.ones((8, atoms), jnp.float32), col_square, NT,
        precision=lax.Precision.HIGHEST, preferred_element_type=jnp.float32,
    )[0:1, :]
    high, low = split(jnp.concatenate(cols, axis=0))
    side = jnp.concatenate([high, high, low], axis=1)
    lane = lax.broadcasted_iota(jnp.int32, (step, LANES), 1)
    vec_parts = []
    for at in range(count):
        for group in range(groups):
            place = group * nv
            piece = blocks_ref[at, 3 * frames:, place // LANES * LANES:place // LANES * LANES + LANES]
            if place % LANES:
                piece = pltpu.roll(piece, LANES - place % LANES, 1)
            vec_parts.append(jnp.where(lane < nv, piece, jnp.where(lane == nv, 1.0, 0.0)))
    high, low = split(jnp.concatenate(vec_parts, axis=0))
    return side, norm, jnp.concatenate([high, high, low], axis=0)


def multiply(row_side, row_norm, side, norm, vec, atoms, moment, tile):
    count = row_norm.shape[0]
    count_cols = norm.shape[1]
    moment[...] = lax.dot_general(row_side, side, NT, preferred_element_type=jnp.float32)
    for at in range(0, count, 8):
        m = [
            moment[a * count + at:a * count + at + 8, b * count_cols:(b + 1) * count_cols]
            for a in range(3) for b in range(3)
        ]
        half_norm = 0.5 * (row_norm[at:at + 8, 0:1] + norm)
        tile[at:at + 8, :] = eigen_tile(m, half_norm, atoms)
    high, low = split(tile[...])
    return jnp.dot(jnp.concatenate([high, low, high], axis=1), vec, preferred_element_type=jnp.float32)


def first_kernel(nv, rows_ref, blocks_ref, sum_ref, side_ref, norm_ref, moment, tile):
    slots = [rows_ref.at[at] for at in range(rows_ref.shape[0])]
    _, frames, atoms = slots[0].shape
    groups, count, _ = sum_ref.shape
    side, norm, vec = column_side(blocks_ref, frames, nv)
    for group in range(groups):
        own = slots[group * count // frames:(group + 1) * count // frames]
        rows = [centre(jnp.concatenate([ref[comp] for ref in own], axis=0)) for comp in range(3)]
        square = jnp.sum(rows[0] * rows[0] + rows[1] * rows[1] + rows[2] * rows[2], axis=1, keepdims=True)
        row_norm = jnp.broadcast_to(square, (count, LANES))
        high, low = split(jnp.concatenate(rows, axis=0))
        row_side = jnp.concatenate([high, low, high], axis=1)
        side_ref[group] = row_side
        norm_ref[group] = row_norm
        sum_ref[group] = multiply(row_side, row_norm, side, norm, vec, atoms, moment, tile)


def second_kernel(nv, frames, sum_ref, side_ref, norm_ref, blocks_ref, *refs):
    moment, tile = refs[-2:]
    atoms = blocks_ref.shape[-1]
    groups, count, _ = sum_ref.shape
    side, norm, vec = column_side(blocks_ref, frames, nv)
    for group in range(groups):
        total = sum_ref[group] + multiply(side_ref[group], norm_ref[group], side, norm, vec, atoms, moment, tile)
        for at in range(count // frames):
            refs[group * count // frames + at][...] = total[at * frames:(at + 1) * frames, :]


def finish_kernel(nv, *refs):
    total = refs[0][...]
    for ref in refs[1:-1]:
        total = total + ref[...]
    refs[-1][...] = total[:, 0:nv] / total[:, nv:nv + 1]


def exchange(x, axis, mask, count):
    return lax.ppermute(x, axis, [(at, at ^ mask) for at in range(count)])


def call(kernel, outs, ins, name, scratch=(), megabytes=8, flops=0):
    out_shape = [jax.ShapeDtypeStruct(*out) for out in outs]
    moved = sum(x.size * 4 for x in ins)
    return pl.pallas_call(
        kernel,
        out_shape=out_shape,
        in_specs=[VM] * len(ins),
        out_specs=[VM] * len(outs),
        scratch_shapes=list(scratch),
        compiler_params=pltpu.CompilerParams(vmem_limit_bytes=megabytes * 1024 * 1024),
        cost_estimate=pl.CostEstimate(flops=flops, bytes_accessed=moved, transcendentals=0),
        name=name,
    )(*ins)


def per_device(n_row, n_col, row_frames, col_frames, vectors):
    comps, frames, atoms = row_frames.shape
    nv = vectors.shape[0]
    f32, bf16 = jnp.float32, jnp.bfloat16
    vec_own = vectors.T
    row_masks = [n_row >> at for at in range(1, n_row.bit_length() - 1)]
    col_masks = [n_col >> at for at in range(1, n_col.bit_length())]
    n_mine = n_row // 2

    far = exchange(row_frames, "row", row_masks[0], n_row)
    first_cols = exchange(col_frames, "col", col_masks[0], n_col)
    second_cols = exchange(col_frames, "col", col_masks[1], n_col)
    near = exchange(row_frames, "row", row_masks[1], n_row)
    first_vec = exchange(vec_own, "col", col_masks[0], n_col)
    extra = frames * nv // atoms
    packed_shape = (comps * frames + extra, atoms)
    (own_extra,) = call(vectors_kernel, [((extra, atoms), f32)], [vec_own], "vectors", flops=1 << 30)
    onward, far = call(
        after_first_kernel,
        [((packed_shape[0] + extra, atoms), f32), (row_frames.shape, f32)],
        [own_extra, first_cols, first_vec, far, second_cols, near], "after_first",
    )
    both = exchange(far, "row", row_masks[1], n_row)
    both_cols = exchange(onward, "col", col_masks[1], n_col)
    own, packed = call(
        own_kernel, [(row_frames.shape, f32), (packed_shape, f32)], [row_frames, col_frames, own_extra, far], "own",
        flops=1 << 30,
    )
    blocks, rows = call(
        after_second_kernel, [((4, *packed_shape), f32), ((4, *row_frames.shape), f32)],
        [packed, onward, second_cols, both_cols, own, far, near, both], "after_second",
    )
    order = [0, row_masks[0], row_masks[1], row_masks[0] ^ row_masks[1]]
    for at in range(2, max(len(row_masks), len(col_masks))):
        joins = []
        if at < len(row_masks):
            joins += [rows, exchange(rows, "row", row_masks[at], n_row)]
            order = order + [row_masks[at] ^ slot for slot in order]
        if at < len(col_masks):
            joins += [blocks, exchange(blocks, "col", col_masks[at], n_col)]
        joined = call(join_kernel, [((2 * x.shape[0], *x.shape[1:]), f32) for x in joins[::2]], joins, "join")
        if at < len(col_masks):
            blocks = joined[-1]
        if at < len(row_masks):
            rows = joined[0]
    other = exchange(blocks, "row", 1, n_row)

    half_cols = n_col * frames
    count = min(n_mine, max(1, LANES // frames)) * frames
    groups = n_mine * frames // count
    scratch = [pltpu.VMEM((3 * count, 3 * half_cols), f32), pltpu.VMEM((count, half_cols), f32)]
    work = 2 * 3 * n_mine * frames * 3 * half_cols * 3 * atoms
    sums, side, norm = call(
        functools.partial(first_kernel, nv),
        [((groups, count, LANES), f32), ((groups, 3 * count, 3 * atoms), bf16), ((groups, count, LANES), f32)],
        [rows, blocks], "first_tile", scratch, 32, work,
    )
    parts = call(
        functools.partial(second_kernel, nv, frames), [((frames, LANES), f32)] * n_mine,
        [sums, side, norm, other], "second_tile", scratch, 32, work,
    )
    shares = [parts[0]] + [
        exchange(parts[order.index(mask)], "row", mask, n_row) for mask in range(n_row - 2, 0, -2)
    ]
    (result,) = call(functools.partial(finish_kernel, nv), [((frames, nv), f32)], shares, "sum_divide")
    return result.T


def solution(mesh):
    return jax.shard_map(
        functools.partial(per_device, mesh.shape["row"], mesh.shape["col"]),
        mesh=mesh,
        in_specs=(
            P(None, ("row", "col"), None),
            P(None, ("col", "row"), None),
            P(None, ("col", "row")),
        ),
        out_specs=P(None, ("row", "col")),
        check_vma=False,
    )
```

```python
import functools

import jax
import jax.numpy as jnp
from jax import lax
from jax.experimental import pallas as pl
from jax.experimental.pallas import tpu as pltpu
from jax.sharding import PartitionSpec as P

NEWTON = 8
BAND = 2.0
LANES = 128
VM = pl.BlockSpec(memory_space=pltpu.VMEM)
NT = (((1,), (1,)), ((), ()))


def centre(frames):
    return frames - jnp.mean(frames, axis=-1, keepdims=True)


def split(x):
    high = x.astype(jnp.bfloat16)
    low = (x - high.astype(jnp.float32)).astype(jnp.bfloat16)
    return high, low


def pack_kernel(cols_ref, vec_ref, out_ref):
    comps, frames, atoms = cols_ref.shape
    for comp in range(comps):
        out_ref[comp * frames:(comp + 1) * frames, :] = centre(cols_ref[comp])
    groups = atoms // vec_ref.shape[1]
    step = frames // groups
    out_ref[comps * frames:, :] = jnp.concatenate(
        [vec_ref[group * step:(group + 1) * step, :] for group in range(groups)], axis=1
    )


def join_kernel(*refs):
    for at, ref in enumerate(refs[:-1]):
        refs[-1][at] = ref[...]


def inverse(x):
    guess = pl.reciprocal(x, approx=True)
    return guess * (2.0 - x * guess)


def eigen_tile(m, half_norm, atoms):
    s00, s01, s02, s10, s11, s12, s20, s21, s22 = m
    coef_two = -2.0 * (
        s00 * s00 + s01 * s01 + s02 * s02 + s10 * s10 + s11 * s11 + s12 * s12 + s20 * s20 + s21 * s21 + s22 * s22
    )
    coef_one = 8.0 * (s00 * s12 * s21 + s11 * s20 * s02 + s22 * s01 * s10) - 8.0 * (
        s00 * s11 * s22 + s12 * s20 * s01 + s21 * s10 * s02
    )
    k00 = s00 + s11 + s22
    k11 = s00 - s11 - s22
    k22 = s11 - s00 - s22
    k33 = s22 - s00 - s11
    k01 = s12 - s21
    k02 = s20 - s02
    k03 = s01 - s10
    k12 = s01 + s10
    k13 = s20 + s02
    k23 = s12 + s21
    top0 = k00 * k11 - k01 * k01
    top1 = k00 * k12 - k01 * k02
    top2 = k00 * k13 - k01 * k03
    top3 = k01 * k12 - k11 * k02
    top4 = k01 * k13 - k11 * k03
    top5 = k02 * k13 - k12 * k03
    low0 = k02 * k13 - k03 * k12
    low1 = k02 * k23 - k03 * k22
    low2 = k02 * k33 - k03 * k23
    low3 = k12 * k23 - k13 * k22
    low4 = k12 * k33 - k13 * k23
    low5 = k22 * k33 - k23 * k23
    coef_zero = top0 * low5 - top1 * low4 + top2 * low3 + top3 * low2 - top4 * low1 + top5 * low0
    eigen = half_norm
    twice = coef_two + coef_two
    for _ in range(NEWTON):
        eigen_sq = eigen * eigen
        value = (eigen_sq + coef_two) * eigen_sq + coef_one * eigen + coef_zero
        slope = (4.0 * eigen_sq + twice) * eigen + coef_one
        eigen = eigen - value * inverse(slope)
    squared = jnp.maximum(2.0 * (half_norm - eigen) / atoms, 0.0)
    return jnp.exp(-squared / BAND)


def column_side(blocks_ref, frames, nv):
    count, _, atoms = blocks_ref.shape
    groups = atoms // nv
    step = frames // groups
    cols = [
        jnp.concatenate([blocks_ref[at, comp * frames:(comp + 1) * frames, :] for at in range(count)], axis=0)
        for comp in range(3)
    ]
    col_square = cols[0] * cols[0] + cols[1] * cols[1] + cols[2] * cols[2]
    norm = lax.dot_general(
        jnp.ones((8, atoms), jnp.float32), col_square, NT,
        precision=lax.Precision.HIGHEST, preferred_element_type=jnp.float32,
    )[0:1, :]
    high, low = split(jnp.concatenate(cols, axis=0))
    side = jnp.concatenate([high, high, low], axis=1)
    lane = lax.broadcasted_iota(jnp.int32, (step, LANES), 1)
    vec_parts = []
    for at in range(count):
        for group in range(groups):
            place = group * nv
            piece = blocks_ref[at, 3 * frames:, place // LANES * LANES:place // LANES * LANES + LANES]
            if place % LANES:
                piece = pltpu.roll(piece, LANES - place % LANES, 1)
            vec_parts.append(jnp.where(lane < nv, piece, jnp.where(lane == nv, 1.0, 0.0)))
    high, low = split(jnp.concatenate(vec_parts, axis=0))
    return side, norm, jnp.concatenate([high, high, low], axis=0)


def multiply(row_side, row_norm, side, norm, vec, atoms, moment, tile):
    count = row_norm.shape[0]
    count_cols = norm.shape[1]
    moment[...] = lax.dot_general(row_side, side, NT, preferred_element_type=jnp.float32)
    for at in range(0, count, 8):
        m = [
            moment[a * count + at:a * count + at + 8, b * count_cols:(b + 1) * count_cols]
            for a in range(3) for b in range(3)
        ]
        half_norm = 0.5 * (row_norm[at:at + 8, 0:1] + norm)
        tile[at:at + 8, :] = eigen_tile(m, half_norm, atoms)
    high, low = split(tile[...])
    return jnp.dot(jnp.concatenate([high, low, high], axis=1), vec, preferred_element_type=jnp.float32)


def first_kernel(nv, frames, rows_ref, blocks_ref, sum_ref, side_ref, norm_ref, moment, tile):
    atoms = rows_ref.shape[2]
    groups, count, _ = sum_ref.shape
    side, norm, vec = column_side(blocks_ref, frames, nv)
    for group in range(groups):
        rows = [centre(rows_ref[comp, group * count:(group + 1) * count, :]) for comp in range(3)]
        square = jnp.sum(rows[0] * rows[0] + rows[1] * rows[1] + rows[2] * rows[2], axis=1, keepdims=True)
        row_norm = jnp.broadcast_to(square, (count, LANES))
        high, low = split(jnp.concatenate(rows, axis=0))
        row_side = jnp.concatenate([high, low, high], axis=1)
        side_ref[group] = row_side
        norm_ref[group] = row_norm
        sum_ref[group] = multiply(row_side, row_norm, side, norm, vec, atoms, moment, tile)


def second_kernel(nv, frames, sum_ref, side_ref, norm_ref, blocks_ref, out_ref, moment, tile):
    atoms = blocks_ref.shape[-1]
    groups, count, _ = sum_ref.shape
    side, norm, vec = column_side(blocks_ref, frames, nv)
    for group in range(groups):
        total = sum_ref[group] + multiply(side_ref[group], norm_ref[group], side, norm, vec, atoms, moment, tile)
        for at in range(count // frames):
            out_ref[group * count // frames + at] = total[at * frames:(at + 1) * frames, :]


def finish_kernel(nv, shares_ref, out_ref):
    me = lax.div(lax.axis_index("row"), 2)
    frames = out_ref.shape[0]
    total = shares_ref[me, 0:frames, :]
    for at in range(frames, shares_ref.shape[1], frames):
        total = total + shares_ref[me, at:at + frames, :]
    out_ref[...] = total[:, 0:nv] / total[:, nv:nv + 1]


def exchange(x, axis, mask, count):
    return lax.ppermute(x, axis, [(at, at ^ mask) for at in range(count)])


def call(kernel, outs, ins, name, scratch=(), megabytes=8, flops=0):
    out_shape = [jax.ShapeDtypeStruct(*out) for out in outs]
    moved = sum(x.size * 4 for x in ins)
    return pl.pallas_call(
        kernel,
        out_shape=out_shape,
        in_specs=[VM] * len(ins),
        out_specs=[VM] * len(outs),
        scratch_shapes=list(scratch),
        compiler_params=pltpu.CompilerParams(vmem_limit_bytes=megabytes * 1024 * 1024),
        cost_estimate=pl.CostEstimate(flops=flops, bytes_accessed=moved, transcendentals=0),
        name=name,
    )(*ins)


def per_device(n_row, n_col, row_frames, col_frames, vectors):
    comps, frames, atoms = row_frames.shape
    nv = vectors.shape[0]
    f32, bf16 = jnp.float32, jnp.bfloat16
    n_mine = n_row // 2
    mine = [list(range(core, n_row, 2)) for core in range(2)]

    packed_shape = (comps * frames + frames * nv // atoms, atoms)
    (packed,) = call(pack_kernel, [(packed_shape, f32)], [col_frames, vectors.T], "pack")
    masks = sorted(range(1, n_col), key=lambda mask: -mask)
    got = [exchange(packed, "col", mask, n_col) for mask in masks]
    rows = lax.all_gather(row_frames, "row", axis_index_groups=mine, axis=1, tiled=True)
    (blocks,) = call(join_kernel, [((n_col, *packed_shape), f32)], [packed, *got], "join")
    other = exchange(blocks, "row", 1, n_row)

    half_cols = n_col * frames
    count = min(n_mine, max(1, LANES // frames)) * frames
    groups = n_mine * frames // count
    scratch = [pltpu.VMEM((3 * count, 3 * half_cols), f32), pltpu.VMEM((count, half_cols), f32)]
    work = 2 * 3 * n_mine * frames * 3 * half_cols * 3 * atoms
    sums, side, norm = call(
        functools.partial(first_kernel, nv, frames),
        [((groups, count, LANES), f32), ((groups, 3 * count, 3 * atoms), bf16), ((groups, count, LANES), f32)],
        [rows, blocks], "first_tile", scratch, 32, work,
    )
    (parts,) = call(
        functools.partial(second_kernel, nv, frames), [((n_mine, frames, LANES), f32)],
        [sums, side, norm, other], "second_tile", scratch, 32, work,
    )
    shares = lax.all_gather(parts, "row", axis_index_groups=mine, axis=1, tiled=True)
    (result,) = call(functools.partial(finish_kernel, nv), [((frames, nv), f32)], [shares], "sum_divide")
    return result.T


def solution(mesh):
    return jax.shard_map(
        functools.partial(per_device, mesh.shape["row"], mesh.shape["col"]),
        mesh=mesh,
        in_specs=(
            P(None, ("row", "col"), None),
            P(None, ("col", "row"), None),
            P(None, ("col", "row")),
        ),
        out_specs=P(None, ("row", "col")),
        check_vma=False,
    )
```

```python
import functools

import jax
import jax.numpy as jnp
from jax import lax
from jax.experimental import pallas as pl
from jax.experimental.pallas import tpu as pltpu
from jax.sharding import PartitionSpec as P

NEWTON = 8
BAND = 2.0
LANES = 128
VM = pl.BlockSpec(memory_space=pltpu.VMEM)
NT = (((1,), (1,)), ((), ()))


def centre(frames):
    return frames - jnp.mean(frames, axis=-1, keepdims=True)


def split(x):
    high = x.astype(jnp.bfloat16)
    low = (x - high.astype(jnp.float32)).astype(jnp.bfloat16)
    return high, low


def pack(cols_ref, vec_ref, out_ref):
    comps, frames, atoms = cols_ref.shape
    nv = vec_ref.shape[1]
    for comp in range(comps):
        out_ref[comp * frames:(comp + 1) * frames, :] = centre(cols_ref[comp])
    out_ref[comps * frames:, :] = pack_vectors(vec_ref, atoms // nv)


def own_kernel(rows_ref, cols_ref, extra_ref, after_ref, near_ref, rows_out, packed_out):
    del after_ref, near_ref
    rows_out[...] = rows_ref[...]
    frames = cols_ref.shape[1]
    for comp in range(3):
        packed_out[comp * frames:(comp + 1) * frames, :] = centre(cols_ref[comp])
    packed_out[3 * frames:, :] = extra_ref[...]


def pack_vectors(vec_ref, groups):
    step = vec_ref.shape[0] // groups
    return jnp.concatenate([vec_ref[group * step:(group + 1) * step, :] for group in range(groups)], axis=1)


def vectors_kernel(vec_ref, out_ref):
    out_ref[...] = pack_vectors(vec_ref, out_ref.shape[1] // vec_ref.shape[1])


def after_first_kernel(extra_ref, first_cols_ref, first_vec_ref, far_ref, send_out, far_out):
    used = send_out.shape[0] - extra_ref.shape[0]
    pack(first_cols_ref, first_vec_ref, send_out.at[0:used])
    send_out[used:, :] = extra_ref[...]
    far_out[...] = far_ref[...]


def after_second_kernel(
    packed_ref, sent_ref, second_cols_ref, got_ref, own_ref, far_ref, near_ref, both_ref, blocks_out, rows_out
):
    used = packed_ref.shape[0]
    frames = second_cols_ref.shape[1]
    blocks_out[0] = packed_ref[...]
    blocks_out[1] = sent_ref[0:used, :]
    for comp in range(3):
        blocks_out[2, comp * frames:(comp + 1) * frames, :] = centre(second_cols_ref[comp])
    blocks_out[2, 3 * frames:, :] = got_ref[used:, :]
    blocks_out[3] = got_ref[0:used, :]
    for at, ref in enumerate((own_ref, far_ref, near_ref, both_ref)):
        rows_out[at] = ref[...]


def join_kernel(*refs):
    pairs = len(refs) // 3
    for at in range(pairs):
        first_ref, second_ref, out_ref = refs[2 * at], refs[2 * at + 1], refs[2 * pairs + at]
        count = first_ref.shape[0]
        out_ref[0:count] = first_ref[...]
        out_ref[count:] = second_ref[...]


def inverse(x):
    guess = pl.reciprocal(x, approx=True)
    return guess * (2.0 - x * guess)


def eigen_tile(m, half_norm, atoms):
    s00, s01, s02, s10, s11, s12, s20, s21, s22 = m
    coef_two = -2.0 * (
        s00 * s00 + s01 * s01 + s02 * s02 + s10 * s10 + s11 * s11 + s12 * s12 + s20 * s20 + s21 * s21 + s22 * s22
    )
    coef_one = 8.0 * (s00 * s12 * s21 + s11 * s20 * s02 + s22 * s01 * s10) - 8.0 * (
        s00 * s11 * s22 + s12 * s20 * s01 + s21 * s10 * s02
    )
    k00 = s00 + s11 + s22
    k11 = s00 - s11 - s22
    k22 = s11 - s00 - s22
    k33 = s22 - s00 - s11
    k01 = s12 - s21
    k02 = s20 - s02
    k03 = s01 - s10
    k12 = s01 + s10
    k13 = s20 + s02
    k23 = s12 + s21
    top0 = k00 * k11 - k01 * k01
    top1 = k00 * k12 - k01 * k02
    top2 = k00 * k13 - k01 * k03
    top3 = k01 * k12 - k11 * k02
    top4 = k01 * k13 - k11 * k03
    top5 = k02 * k13 - k12 * k03
    low0 = k02 * k13 - k03 * k12
    low1 = k02 * k23 - k03 * k22
    low2 = k02 * k33 - k03 * k23
    low3 = k12 * k23 - k13 * k22
    low4 = k12 * k33 - k13 * k23
    low5 = k22 * k33 - k23 * k23
    coef_zero = top0 * low5 - top1 * low4 + top2 * low3 + top3 * low2 - top4 * low1 + top5 * low0
    eigen = half_norm
    twice = coef_two + coef_two
    for _ in range(NEWTON):
        eigen_sq = eigen * eigen
        value = (eigen_sq + coef_two) * eigen_sq + coef_one * eigen + coef_zero
        slope = (4.0 * eigen_sq + twice) * eigen + coef_one
        eigen = eigen - value * inverse(slope)
    squared = jnp.maximum(2.0 * (half_norm - eigen) / atoms, 0.0)
    return jnp.exp(-squared / BAND)


def column_side(blocks_ref, frames, nv):
    count, _, atoms = blocks_ref.shape
    groups = atoms // nv
    step = frames // groups
    cols = [
        jnp.concatenate([blocks_ref[at, comp * frames:(comp + 1) * frames, :] for at in range(count)], axis=0)
        for comp in range(3)
    ]
    col_square = cols[0] * cols[0] + cols[1] * cols[1] + cols[2] * cols[2]
    norm = lax.dot_general(
        jnp.ones((8, atoms), jnp.float32), col_square, NT,
        precision=lax.Precision.HIGHEST, preferred_element_type=jnp.float32,
    )[0:1, :]
    high, low = split(jnp.concatenate(cols, axis=0))
    side = jnp.concatenate([high, high, low], axis=1)
    lane = lax.broadcasted_iota(jnp.int32, (step, LANES), 1)
    vec_parts = []
    for at in range(count):
        for group in range(groups):
            place = group * nv
            piece = blocks_ref[at, 3 * frames:, place // LANES * LANES:place // LANES * LANES + LANES]
            if place % LANES:
                piece = pltpu.roll(piece, LANES - place % LANES, 1)
            vec_parts.append(jnp.where(lane < nv, piece, jnp.where(lane == nv, 1.0, 0.0)))
    high, low = split(jnp.concatenate(vec_parts, axis=0))
    return side, norm, jnp.concatenate([high, high, low], axis=0)


def multiply(row_side, row_norm, side, norm, vec, atoms, moment, tile):
    count = row_norm.shape[0]
    count_cols = norm.shape[1]
    moment[...] = lax.dot_general(row_side, side, NT, preferred_element_type=jnp.float32)
    for at in range(0, count, 8):
        m = [
            moment[a * count + at:a * count + at + 8, b * count_cols:(b + 1) * count_cols]
            for a in range(3) for b in range(3)
        ]
        half_norm = 0.5 * (row_norm[at:at + 8, 0:1] + norm)
        tile[at:at + 8, :] = eigen_tile(m, half_norm, atoms)
    high, low = split(tile[...])
    return jnp.dot(jnp.concatenate([high, low, high], axis=1), vec, preferred_element_type=jnp.float32)


def first_kernel(nv, rows_ref, blocks_ref, sum_ref, side_ref, norm_ref, moment, tile):
    slots = [rows_ref.at[at] for at in range(rows_ref.shape[0])]
    _, frames, atoms = slots[0].shape
    groups, count, _ = sum_ref.shape
    side, norm, vec = column_side(blocks_ref, frames, nv)
    for group in range(groups):
        own = slots[group * count // frames:(group + 1) * count // frames]
        rows = [centre(jnp.concatenate([ref[comp] for ref in own], axis=0)) for comp in range(3)]
        square = jnp.sum(rows[0] * rows[0] + rows[1] * rows[1] + rows[2] * rows[2], axis=1, keepdims=True)
        row_norm = jnp.broadcast_to(square, (count, LANES))
        high, low = split(jnp.concatenate(rows, axis=0))
        row_side = jnp.concatenate([high, low, high], axis=1)
        side_ref[group] = row_side
        norm_ref[group] = row_norm
        sum_ref[group] = multiply(row_side, row_norm, side, norm, vec, atoms, moment, tile)


def second_kernel(nv, frames, sum_ref, side_ref, norm_ref, blocks_ref, *refs):
    moment, tile = refs[-2:]
    atoms = blocks_ref.shape[-1]
    groups, count, _ = sum_ref.shape
    side, norm, vec = column_side(blocks_ref, frames, nv)
    for group in range(groups):
        total = sum_ref[group] + multiply(side_ref[group], norm_ref[group], side, norm, vec, atoms, moment, tile)
        for at in range(count // frames):
            refs[group * count // frames + at][...] = total[at * frames:(at + 1) * frames, :]


def finish_kernel(nv, *refs):
    total = refs[0][...]
    for ref in refs[1:-1]:
        total = total + ref[...]
    refs[-1][...] = total[:, 0:nv] / total[:, nv:nv + 1]


def exchange(x, axis, mask, count):
    return lax.ppermute(x, axis, [(at, at ^ mask) for at in range(count)])


def call(kernel, outs, ins, name, scratch=(), megabytes=8, flops=0):
    out_shape = [jax.ShapeDtypeStruct(*out) for out in outs]
    moved = sum(x.size * 4 for x in ins)
    return pl.pallas_call(
        kernel,
        out_shape=out_shape,
        in_specs=[VM] * len(ins),
        out_specs=[VM] * len(outs),
        scratch_shapes=list(scratch),
        compiler_params=pltpu.CompilerParams(vmem_limit_bytes=megabytes * 1024 * 1024),
        cost_estimate=pl.CostEstimate(flops=flops, bytes_accessed=moved, transcendentals=0),
        name=name,
    )(*ins)


def per_device(n_row, n_col, row_frames, col_frames, vectors):
    comps, frames, atoms = row_frames.shape
    nv = vectors.shape[0]
    f32, bf16 = jnp.float32, jnp.bfloat16
    vec_own = vectors.T
    row_masks = [n_col >> at for at in range(1, n_col.bit_length())]
    col_masks = [1 << at for at in range(1, n_row.bit_length() - 1)]

    far = exchange(row_frames, "col", row_masks[0], n_col)
    first_cols = exchange(col_frames, "row", col_masks[0], n_row)
    second_cols = exchange(col_frames, "row", col_masks[1], n_row)
    near = exchange(row_frames, "col", row_masks[1], n_col)
    first_vec = exchange(vec_own, "row", col_masks[0], n_row)
    extra = frames * nv // atoms
    packed_shape = (comps * frames + extra, atoms)
    (own_extra,) = call(vectors_kernel, [((extra, atoms), f32)], [vec_own], "vectors", flops=1 << 30)
    onward, far = call(
        after_first_kernel,
        [((packed_shape[0] + extra, atoms), f32), (row_frames.shape, f32)],
        [own_extra, first_cols, first_vec, far], "after_first",
    )
    both = exchange(far, "col", row_masks[1], n_col)
    xy = exchange(onward, "row", col_masks[1], n_row)
    own, packed = call(
        own_kernel, [(row_frames.shape, f32), (packed_shape, f32)], [row_frames, col_frames, own_extra, far, near], "own",
        flops=1 << 30,
    )
    blocks, rows = call(
        after_second_kernel, [((4, *packed_shape), f32), ((4, *row_frames.shape), f32)],
        [packed, onward, second_cols, xy, own, far, near, both], "after_second",
    )
    order = [0, row_masks[0], row_masks[1], row_masks[0] ^ row_masks[1]]
    for at in range(2, max(len(row_masks), len(col_masks))):
        joins = []
        if at < len(row_masks):
            joins += [rows, exchange(rows, "col", row_masks[at], n_col)]
            order = order + [row_masks[at] ^ slot for slot in order]
        if at < len(col_masks):
            joins += [blocks, exchange(blocks, "row", col_masks[at], n_row)]
        joined = call(join_kernel, [((2 * x.shape[0], *x.shape[1:]), f32) for x in joins[::2]], joins, "join")
        if at < len(col_masks):
            blocks = joined[-1]
        if at < len(row_masks):
            rows = joined[0]
    other = exchange(blocks, "row", 1, n_row)

    half_cols = n_row // 2 * frames
    count = min(n_col, max(1, LANES // frames)) * frames
    groups = n_col * frames // count
    scratch = [pltpu.VMEM((3 * count, 3 * half_cols), f32), pltpu.VMEM((count, half_cols), f32)]
    work = 2 * 3 * n_col * frames * 3 * half_cols * 3 * atoms
    sums, side, norm = call(
        functools.partial(first_kernel, nv),
        [((groups, count, LANES), f32), ((groups, 3 * count, 3 * atoms), bf16), ((groups, count, LANES), f32)],
        [rows, blocks], "first_tile", scratch, 32, work,
    )
    parts = call(
        functools.partial(second_kernel, nv, frames), [((frames, LANES), f32)] * n_col,
        [sums, side, norm, other], "second_tile", scratch, 32, work,
    )
    shares = [parts[0]] + [
        exchange(parts[order.index(mask)], "col", mask, n_col) for mask in range(n_col - 1, 0, -1)
    ]
    (result,) = call(functools.partial(finish_kernel, nv), [((frames, nv), f32)], shares, "sum_divide")
    return result.T


def solution(mesh):
    return jax.shard_map(
        functools.partial(per_device, mesh.shape["row"], mesh.shape["col"]),
        mesh=mesh,
        in_specs=(
            P(None, ("row", "col"), None),
            P(None, ("col", "row"), None),
            P(None, ("col", "row")),
        ),
        out_specs=P(None, ("row", "col")),
        check_vma=False,
    )
```

```python
import functools

import jax
import jax.numpy as jnp
from jax import lax
from jax.experimental import pallas as pl
from jax.experimental.pallas import tpu as pltpu
from jax.sharding import PartitionSpec as P

NEWTON = 8
BAND = 2.0
LANES = 128
VM = pl.BlockSpec(memory_space=pltpu.VMEM)
NT = (((1,), (1,)), ((), ()))


def centre(frames):
    return frames - jnp.mean(frames, axis=-1, keepdims=True)


def split(x):
    high = x.astype(jnp.bfloat16)
    low = (x - high.astype(jnp.float32)).astype(jnp.bfloat16)
    return high, low


def own_kernel(rows_ref, cols_ref, extra_ref, after_ref, second_cols_ref, near_ref, rows_out, packed_out):
    del after_ref, second_cols_ref, near_ref
    rows_out[...] = rows_ref[...]
    frames = cols_ref.shape[1]
    for comp in range(3):
        packed_out[comp * frames:(comp + 1) * frames, :] = centre(cols_ref[comp])
    packed_out[3 * frames:, :] = extra_ref[...]


def pack_vectors(vec_ref, groups):
    step = vec_ref.shape[0] // groups
    return jnp.concatenate([vec_ref[group * step:(group + 1) * step, :] for group in range(groups)], axis=1)


def vectors_kernel(vec_ref, out_ref):
    out_ref[...] = pack_vectors(vec_ref, out_ref.shape[1] // vec_ref.shape[1])


def after_first_kernel(extra_ref, cols_ref, far_ref, send_out, far_out):
    frames = cols_ref.shape[1]
    for comp in range(3):
        send_out[comp * frames:(comp + 1) * frames, :] = centre(cols_ref[comp])
    send_out[3 * frames:, :] = extra_ref[...]
    far_out[...] = far_ref[...]


def after_second_kernel(
    packed_ref, sent_ref, second_cols_ref, got_ref, first_vec_ref, both_vec_ref,
    own_ref, far_ref, near_ref, both_ref, blocks_out, rows_out
):
    frames = second_cols_ref.shape[1]
    used = 3 * frames
    groups = packed_ref.shape[1] // first_vec_ref.shape[1]
    blocks_out[0] = packed_ref[...]
    blocks_out[1, 0:used, :] = sent_ref[0:used, :]
    blocks_out[1, used:, :] = pack_vectors(first_vec_ref, groups)
    for comp in range(3):
        blocks_out[2, comp * frames:(comp + 1) * frames, :] = centre(second_cols_ref[comp])
    blocks_out[2, used:, :] = got_ref[used:, :]
    blocks_out[3, 0:used, :] = got_ref[0:used, :]
    blocks_out[3, used:, :] = pack_vectors(both_vec_ref, groups)
    for at, ref in enumerate((own_ref, far_ref, near_ref, both_ref)):
        rows_out[at] = ref[...]


def join_kernel(*refs):
    pairs = len(refs) // 3
    for at in range(pairs):
        first_ref, second_ref, out_ref = refs[2 * at], refs[2 * at + 1], refs[2 * pairs + at]
        count = first_ref.shape[0]
        out_ref[0:count] = first_ref[...]
        out_ref[count:] = second_ref[...]


def inverse(x):
    guess = pl.reciprocal(x, approx=True)
    return guess * (2.0 - x * guess)


def eigen_tile(m, half_norm, atoms):
    s00, s01, s02, s10, s11, s12, s20, s21, s22 = m
    coef_two = -2.0 * (
        s00 * s00 + s01 * s01 + s02 * s02 + s10 * s10 + s11 * s11 + s12 * s12 + s20 * s20 + s21 * s21 + s22 * s22
    )
    coef_one = 8.0 * (s00 * s12 * s21 + s11 * s20 * s02 + s22 * s01 * s10) - 8.0 * (
        s00 * s11 * s22 + s12 * s20 * s01 + s21 * s10 * s02
    )
    k00 = s00 + s11 + s22
    k11 = s00 - s11 - s22
    k22 = s11 - s00 - s22
    k33 = s22 - s00 - s11
    k01 = s12 - s21
    k02 = s20 - s02
    k03 = s01 - s10
    k12 = s01 + s10
    k13 = s20 + s02
    k23 = s12 + s21
    top0 = k00 * k11 - k01 * k01
    top1 = k00 * k12 - k01 * k02
    top2 = k00 * k13 - k01 * k03
    top3 = k01 * k12 - k11 * k02
    top4 = k01 * k13 - k11 * k03
    top5 = k02 * k13 - k12 * k03
    low0 = k02 * k13 - k03 * k12
    low1 = k02 * k23 - k03 * k22
    low2 = k02 * k33 - k03 * k23
    low3 = k12 * k23 - k13 * k22
    low4 = k12 * k33 - k13 * k23
    low5 = k22 * k33 - k23 * k23
    coef_zero = top0 * low5 - top1 * low4 + top2 * low3 + top3 * low2 - top4 * low1 + top5 * low0
    eigen = half_norm
    twice = coef_two + coef_two
    for _ in range(NEWTON):
        eigen_sq = eigen * eigen
        value = (eigen_sq + coef_two) * eigen_sq + coef_one * eigen + coef_zero
        slope = (4.0 * eigen_sq + twice) * eigen + coef_one
        eigen = eigen - value * inverse(slope)
    squared = jnp.maximum(2.0 * (half_norm - eigen) / atoms, 0.0)
    return jnp.exp(-squared / BAND)


def column_side(blocks_ref, frames, nv):
    count, _, atoms = blocks_ref.shape
    groups = atoms // nv
    step = frames // groups
    cols = [
        jnp.concatenate([blocks_ref[at, comp * frames:(comp + 1) * frames, :] for at in range(count)], axis=0)
        for comp in range(3)
    ]
    col_square = cols[0] * cols[0] + cols[1] * cols[1] + cols[2] * cols[2]
    norm = lax.dot_general(
        jnp.ones((8, atoms), jnp.float32), col_square, NT,
        precision=lax.Precision.HIGHEST, preferred_element_type=jnp.float32,
    )[0:1, :]
    high, low = split(jnp.concatenate(cols, axis=0))
    side = jnp.concatenate([high, high, low], axis=1)
    lane = lax.broadcasted_iota(jnp.int32, (step, LANES), 1)
    vec_parts = []
    for at in range(count):
        for group in range(groups):
            place = group * nv
            piece = blocks_ref[at, 3 * frames:, place // LANES * LANES:place // LANES * LANES + LANES]
            if place % LANES:
                piece = pltpu.roll(piece, LANES - place % LANES, 1)
            vec_parts.append(jnp.where(lane < nv, piece, jnp.where(lane == nv, 1.0, 0.0)))
    high, low = split(jnp.concatenate(vec_parts, axis=0))
    return side, norm, jnp.concatenate([high, high, low], axis=0)


def multiply(row_side, row_norm, side, norm, vec, atoms, moment, tile):
    count = row_norm.shape[0]
    count_cols = norm.shape[1]
    moment[...] = lax.dot_general(row_side, side, NT, preferred_element_type=jnp.float32)
    for at in range(0, count, 8):
        m = [
            moment[a * count + at:a * count + at + 8, b * count_cols:(b + 1) * count_cols]
            for a in range(3) for b in range(3)
        ]
        half_norm = 0.5 * (row_norm[at:at + 8, 0:1] + norm)
        tile[at:at + 8, :] = eigen_tile(m, half_norm, atoms)
    high, low = split(tile[...])
    return jnp.dot(jnp.concatenate([high, low, high], axis=1), vec, preferred_element_type=jnp.float32)


def first_kernel(nv, rows_ref, blocks_ref, sum_ref, side_ref, norm_ref, moment, tile):
    slots = [rows_ref.at[at] for at in range(rows_ref.shape[0])]
    _, frames, atoms = slots[0].shape
    groups, count, _ = sum_ref.shape
    side, norm, vec = column_side(blocks_ref, frames, nv)
    for group in range(groups):
        own = slots[group * count // frames:(group + 1) * count // frames]
        rows = [centre(jnp.concatenate([ref[comp] for ref in own], axis=0)) for comp in range(3)]
        square = jnp.sum(rows[0] * rows[0] + rows[1] * rows[1] + rows[2] * rows[2], axis=1, keepdims=True)
        row_norm = jnp.broadcast_to(square, (count, LANES))
        high, low = split(jnp.concatenate(rows, axis=0))
        row_side = jnp.concatenate([high, low, high], axis=1)
        side_ref[group] = row_side
        norm_ref[group] = row_norm
        sum_ref[group] = multiply(row_side, row_norm, side, norm, vec, atoms, moment, tile)


def second_kernel(nv, frames, sum_ref, side_ref, norm_ref, blocks_ref, *refs):
    moment, tile = refs[-2:]
    atoms = blocks_ref.shape[-1]
    groups, count, _ = sum_ref.shape
    side, norm, vec = column_side(blocks_ref, frames, nv)
    for group in range(groups):
        total = sum_ref[group] + multiply(side_ref[group], norm_ref[group], side, norm, vec, atoms, moment, tile)
        for at in range(count // frames):
            refs[group * count // frames + at][...] = total[at * frames:(at + 1) * frames, :]


def finish_kernel(nv, *refs):
    total = refs[0][...]
    for ref in refs[1:-1]:
        total = total + ref[...]
    refs[-1][...] = total[:, 0:nv] / total[:, nv:nv + 1]


def exchange(x, axis, mask, count):
    return lax.ppermute(x, axis, [(at, at ^ mask) for at in range(count)])


def call(kernel, outs, ins, name, scratch=(), megabytes=8, flops=0):
    out_shape = [jax.ShapeDtypeStruct(*out) for out in outs]
    moved = sum(x.size * 4 for x in ins)
    return pl.pallas_call(
        kernel,
        out_shape=out_shape,
        in_specs=[VM] * len(ins),
        out_specs=[VM] * len(outs),
        scratch_shapes=list(scratch),
        compiler_params=pltpu.CompilerParams(vmem_limit_bytes=megabytes * 1024 * 1024),
        cost_estimate=pl.CostEstimate(flops=flops, bytes_accessed=moved, transcendentals=0),
        name=name,
    )(*ins)


def per_device(n_row, n_col, row_frames, col_frames, vectors):
    comps, frames, atoms = row_frames.shape
    nv = vectors.shape[0]
    f32, bf16 = jnp.float32, jnp.bfloat16
    vec_own = vectors.T
    row_masks = [n_col >> at for at in range(1, n_col.bit_length())]
    col_masks = [1 << at for at in range(1, n_row.bit_length() - 1)]

    extra = frames * nv // atoms
    packed_shape = (comps * frames + extra, atoms)
    far = exchange(row_frames, "col", row_masks[0], n_col)
    near = exchange(row_frames, "col", row_masks[1], n_col)
    first_cols = exchange(col_frames, "row", col_masks[0], n_row)
    second_cols = exchange(col_frames, "row", col_masks[1], n_row)
    first_vec = exchange(vec_own, "row", col_masks[0], n_row)
    (own_extra,) = call(vectors_kernel, [((extra, atoms), f32)], [vec_own], "vectors", flops=1 << 30)
    onward, far = call(
        after_first_kernel, [(packed_shape, f32), (row_frames.shape, f32)], [own_extra, first_cols, far], "after_first"
    )
    both = exchange(far, "col", row_masks[1], n_col)
    got = exchange(onward, "row", col_masks[1], n_row)
    both_vec = exchange(first_vec, "row", col_masks[1], n_row)
    own, packed = call(
        own_kernel, [(row_frames.shape, f32), (packed_shape, f32)],
        [row_frames, col_frames, own_extra, far, second_cols, near], "own", flops=1 << 30,
    )
    blocks, rows = call(
        after_second_kernel, [((4, *packed_shape), f32), ((4, *row_frames.shape), f32)],
        [packed, onward, second_cols, got, first_vec, both_vec, own, far, near, both], "after_second",
    )
    order = [0, row_masks[0], row_masks[1], row_masks[0] ^ row_masks[1]]
    for at in range(2, max(len(row_masks), len(col_masks))):
        joins = []
        if at < len(row_masks):
            joins += [rows, exchange(rows, "col", row_masks[at], n_col)]
            order = order + [row_masks[at] ^ slot for slot in order]
        if at < len(col_masks):
            joins += [blocks, exchange(blocks, "row", col_masks[at], n_row)]
        joined = call(join_kernel, [((2 * x.shape[0], *x.shape[1:]), f32) for x in joins[::2]], joins, "join")
        if at < len(col_masks):
            blocks = joined[-1]
        if at < len(row_masks):
            rows = joined[0]
    other = exchange(blocks, "row", 1, n_row)

    half_cols = n_row // 2 * frames
    count = min(n_col, max(1, LANES // frames)) * frames
    groups = n_col * frames // count
    scratch = [pltpu.VMEM((3 * count, 3 * half_cols), f32), pltpu.VMEM((count, half_cols), f32)]
    work = 2 * 3 * n_col * frames * 3 * half_cols * 3 * atoms
    sums, side, norm = call(
        functools.partial(first_kernel, nv),
        [((groups, count, LANES), f32), ((groups, 3 * count, 3 * atoms), bf16), ((groups, count, LANES), f32)],
        [rows, blocks], "first_tile", scratch, 32, work,
    )
    parts = call(
        functools.partial(second_kernel, nv, frames), [((frames, LANES), f32)] * n_col,
        [sums, side, norm, other], "second_tile", scratch, 32, work,
    )
    shares = [parts[0]] + [
        exchange(parts[order.index(mask)], "col", mask, n_col) for mask in range(n_col - 1, 0, -1)
    ]
    (result,) = call(functools.partial(finish_kernel, nv), [((frames, nv), f32)], shares, "sum_divide")
    return result.T


def solution(mesh):
    return jax.shard_map(
        functools.partial(per_device, mesh.shape["row"], mesh.shape["col"]),
        mesh=mesh,
        in_specs=(
            P(None, ("row", "col"), None),
            P(None, ("col", "row"), None),
            P(None, ("col", "row")),
        ),
        out_specs=P(None, ("row", "col")),
        check_vma=False,
    )
```

```python
import functools

import jax
import jax.numpy as jnp
from jax import lax
from jax.experimental import pallas as pl
from jax.experimental.pallas import tpu as pltpu
from jax.sharding import PartitionSpec as P

NEWTON = 8
BAND = 2.0
LANES = 128
VM = pl.BlockSpec(memory_space=pltpu.VMEM)
NT = (((1,), (1,)), ((), ()))


def centre(frames):
    return frames - jnp.mean(frames, axis=-1, keepdims=True)


def split(x):
    high = x.astype(jnp.bfloat16)
    low = (x - high.astype(jnp.float32)).astype(jnp.bfloat16)
    return high, low


def copy_kernel(in_ref, out_ref):
    out_ref[...] = in_ref[...]


def join_kernel(first_ref, second_ref, out_ref):
    count = second_ref.shape[0]
    out_ref[0:count] = first_ref[...]
    out_ref[count:] = second_ref[...]


def after_far_kernel(far_ref, vec_ref, got_ref, far_out, vec_out):
    far_out[...] = far_ref[...]
    join_kernel(vec_ref, got_ref, vec_out)


def columns_kernel(n_blocks, *refs):
    for at in range(n_blocks):
        refs[-1][at] = refs[at][...]


def inverse(x):
    guess = pl.reciprocal(x, approx=True)
    return guess * (2.0 - x * guess)


def eigen_tile(m, half_norm, atoms):
    s00, s01, s02, s10, s11, s12, s20, s21, s22 = m
    coef_two = -2.0 * (
        s00 * s00 + s01 * s01 + s02 * s02 + s10 * s10 + s11 * s11 + s12 * s12 + s20 * s20 + s21 * s21 + s22 * s22
    )
    coef_one = 8.0 * (s00 * s12 * s21 + s11 * s20 * s02 + s22 * s01 * s10) - 8.0 * (
        s00 * s11 * s22 + s12 * s20 * s01 + s21 * s10 * s02
    )
    k00 = s00 + s11 + s22
    k11 = s00 - s11 - s22
    k22 = s11 - s00 - s22
    k33 = s22 - s00 - s11
    k01 = s12 - s21
    k02 = s20 - s02
    k03 = s01 - s10
    k12 = s01 + s10
    k13 = s20 + s02
    k23 = s12 + s21
    top0 = k00 * k11 - k01 * k01
    top1 = k00 * k12 - k01 * k02
    top2 = k00 * k13 - k01 * k03
    top3 = k01 * k12 - k11 * k02
    top4 = k01 * k13 - k11 * k03
    top5 = k02 * k13 - k12 * k03
    low0 = k02 * k13 - k03 * k12
    low1 = k02 * k23 - k03 * k22
    low2 = k02 * k33 - k03 * k23
    low3 = k12 * k23 - k13 * k22
    low4 = k12 * k33 - k13 * k23
    low5 = k22 * k33 - k23 * k23
    coef_zero = top0 * low5 - top1 * low4 + top2 * low3 + top3 * low2 - top4 * low1 + top5 * low0
    eigen = half_norm
    twice = coef_two + coef_two
    for _ in range(NEWTON):
        eigen_sq = eigen * eigen
        value = (eigen_sq + coef_two) * eigen_sq + coef_one * eigen + coef_zero
        slope = (4.0 * eigen_sq + twice) * eigen + coef_one
        eigen = eigen - value * inverse(slope)
    squared = jnp.maximum(2.0 * (half_norm - eigen) / atoms, 0.0)
    return jnp.exp(-squared / BAND)


def column_side(blocks_ref, vecs_ref):
    count, _, frames, atoms = blocks_ref.shape
    nv = vecs_ref.shape[2]
    cols = [
        centre(jnp.concatenate([blocks_ref[at, comp] for at in range(count)], axis=0)) for comp in range(3)
    ]
    col_square = cols[0] * cols[0] + cols[1] * cols[1] + cols[2] * cols[2]
    norm = lax.dot_general(
        jnp.ones((8, atoms), jnp.float32), col_square, NT,
        precision=lax.Precision.HIGHEST, preferred_element_type=jnp.float32,
    )[0:1, :]
    high, low = split(jnp.concatenate(cols, axis=0))
    side = jnp.concatenate([high, high, low], axis=1)
    ones = jnp.where(lax.broadcasted_iota(jnp.int32, (count * frames, LANES - nv), 1) == 0, 1.0, 0.0)
    vecs = jnp.concatenate([vecs_ref[at] for at in range(count)], axis=0)
    high, low = split(jnp.concatenate([vecs, ones], axis=1))
    return side, norm, jnp.concatenate([high, high, low], axis=0)


def multiply(row_side, row_norm, side, norm, vec, atoms, moment, tile):
    count = row_norm.shape[0]
    count_cols = norm.shape[1]
    moment[...] = lax.dot_general(row_side, side, NT, preferred_element_type=jnp.float32)
    for at in range(0, count, 8):
        m = [
            moment[a * count + at:a * count + at + 8, b * count_cols:(b + 1) * count_cols]
            for a in range(3) for b in range(3)
        ]
        half_norm = 0.5 * (row_norm[at:at + 8, 0:1] + norm)
        tile[at:at + 8, :] = eigen_tile(m, half_norm, atoms)
    high, low = split(tile[...])
    return jnp.dot(jnp.concatenate([high, low, high], axis=1), vec, preferred_element_type=jnp.float32)


def first_kernel(n_mine, *refs):
    slots, blocks_ref, vecs_ref = refs[:n_mine], refs[n_mine], refs[n_mine + 1]
    sum_ref, side_ref, norm_ref, moment, tile = refs[n_mine + 2:]
    _, frames, atoms = slots[0].shape
    groups, count, _ = sum_ref.shape
    side, norm, vec = column_side(blocks_ref, vecs_ref)
    for group in range(groups):
        own = slots[group * count // frames:(group + 1) * count // frames]
        rows = [centre(jnp.concatenate([ref[comp] for ref in own], axis=0)) for comp in range(3)]
        square = jnp.sum(rows[0] * rows[0] + rows[1] * rows[1] + rows[2] * rows[2], axis=1, keepdims=True)
        row_norm = jnp.broadcast_to(square, (count, LANES))
        high, low = split(jnp.concatenate(rows, axis=0))
        row_side = jnp.concatenate([high, low, high], axis=1)
        side_ref[group] = row_side
        norm_ref[group] = row_norm
        sum_ref[group] = multiply(row_side, row_norm, side, norm, vec, atoms, moment, tile)


def second_kernel(frames, sum_ref, side_ref, norm_ref, blocks_ref, vecs_ref, *refs):
    moment, tile = refs[-2:]
    atoms = blocks_ref.shape[-1]
    groups, count, _ = sum_ref.shape
    side, norm, vec = column_side(blocks_ref, vecs_ref)
    for group in range(groups):
        total = sum_ref[group] + multiply(side_ref[group], norm_ref[group], side, norm, vec, atoms, moment, tile)
        for at in range(count // frames):
            refs[group * count // frames + at][...] = total[at * frames:(at + 1) * frames, :]


def finish_kernel(nv, *refs):
    total = refs[0][...]
    for ref in refs[1:-1]:
        total = total + ref[...]
    refs[-1][...] = total[:, 0:nv] / total[:, nv:nv + 1]


def exchange(x, axis, mask, count):
    return lax.ppermute(x, axis, [(at, at ^ mask) for at in range(count)])


def call(kernel, outs, ins, name, scratch=(), megabytes=8, flops=0):
    out_shape = [jax.ShapeDtypeStruct(*out) for out in outs]
    moved = sum(x.size * 4 for x in ins)
    return pl.pallas_call(
        kernel,
        out_shape=out_shape,
        in_specs=[VM] * len(ins),
        out_specs=[VM] * len(outs),
        scratch_shapes=list(scratch),
        compiler_params=pltpu.CompilerParams(vmem_limit_bytes=megabytes * 1024 * 1024),
        cost_estimate=pl.CostEstimate(flops=flops, bytes_accessed=moved, transcendentals=0),
        name=name,
    )(*ins)


def per_device(n_row, n_col, row_frames, col_frames, vectors):
    comps, frames, atoms = row_frames.shape
    nv = vectors.shape[0]
    f32, bf16 = jnp.float32, jnp.bfloat16
    row_masks = [n_col >> at for at in range(1, n_col.bit_length())]
    col_masks = [1 << at for at in range(1, n_row.bit_length() - 1)]

    vecs = vectors.T[None]
    got_vecs = exchange(vecs, "row", col_masks[0], n_row)
    (vecs,) = call(copy_kernel, [((1, frames, nv), f32)], [vecs], "vectors", flops=1 << 30)
    order = [0]
    rows = {0: row_frames}
    for mask in row_masks:
        for slot in list(order):
            got = exchange(rows[slot], "col", mask, n_col)
            if not slot and mask == row_masks[0]:
                got, vecs = call(
                    after_far_kernel, [(got.shape, f32), ((2, frames, nv), f32)], [got, vecs, got_vecs], "after_far"
                )
            rows[slot ^ mask] = got
            order.append(slot ^ mask)
    col_order = [0]
    for mask in col_masks:
        col_order = col_order + [slot ^ mask for slot in col_order]
    cols = [col_frames] + [exchange(col_frames, "row", mask, n_row) for mask in col_order[1:]]
    for mask in col_masks[1:]:
        got = exchange(vecs, "row", mask, n_row)
        (vecs,) = call(join_kernel, [((2 * vecs.shape[0], frames, nv), f32)], [vecs, got], "vectors")
    (blocks,) = call(
        functools.partial(columns_kernel, len(cols)), [((len(cols), *col_frames.shape), f32)],
        [*cols, rows[row_masks[0]], rows[row_masks[1]]], "columns", flops=10 << 30,
    )
    other = exchange(blocks, "row", 1, n_row)
    other_vecs = exchange(vecs, "row", 1, n_row)

    half_cols = n_row // 2 * frames
    count = min(n_col, max(1, LANES // frames)) * frames
    groups = n_col * frames // count
    scratch = [pltpu.VMEM((3 * count, 3 * half_cols), f32), pltpu.VMEM((count, half_cols), f32)]
    work = 2 * 3 * n_col * frames * 3 * half_cols * 3 * atoms
    sums, side, norm = call(
        functools.partial(first_kernel, n_col),
        [((groups, count, LANES), f32), ((groups, 3 * count, 3 * atoms), bf16), ((groups, count, LANES), f32)],
        [*[rows[slot] for slot in order], blocks, vecs], "first_tile", scratch, 32, work << 8,
    )
    parts = call(
        functools.partial(second_kernel, frames), [((frames, LANES), f32)] * n_col,
        [sums, side, norm, other, other_vecs], "second_tile", scratch, 32, work,
    )
    shares = [parts[0]] + [
        exchange(parts[order.index(mask)], "col", mask, n_col) for mask in range(n_col - 1, 0, -1)
    ]
    (result,) = call(functools.partial(finish_kernel, nv), [((frames, nv), f32)], shares, "sum_divide")
    return result.T


def solution(mesh):
    return jax.shard_map(
        functools.partial(per_device, mesh.shape["row"], mesh.shape["col"]),
        mesh=mesh,
        in_specs=(
            P(None, ("row", "col"), None),
            P(None, ("col", "row"), None),
            P(None, ("col", "row")),
        ),
        out_specs=P(None, ("row", "col")),
        check_vma=False,
    )
```

```python
import functools

import jax
import jax.numpy as jnp
from jax import lax
from jax.experimental import pallas as pl
from jax.experimental.pallas import tpu as pltpu
from jax.sharding import PartitionSpec as P

NEWTON = 8
BAND = 2.0
LANES = 128
VM = pl.BlockSpec(memory_space=pltpu.VMEM)
NT = (((1,), (1,)), ((), ()))


def centre(frames):
    return frames - jnp.mean(frames, axis=-1, keepdims=True)


def split(x):
    high = x.astype(jnp.bfloat16)
    low = (x - high.astype(jnp.float32)).astype(jnp.bfloat16)
    return high, low


def copy_kernel(in_ref, out_ref):
    out_ref[...] = in_ref[...]


def join_kernel(first_ref, second_ref, out_ref):
    count = second_ref.shape[0]
    out_ref[0:count] = first_ref[...]
    out_ref[count:] = second_ref[...]


def after_far_kernel(far_ref, vec_ref, got_ref, far_out, vec_out):
    far_out[...] = far_ref[...]
    join_kernel(vec_ref, got_ref, vec_out)


def pass_kernel(in_ref, *refs):
    refs[-1][...] = in_ref[...]


def columns_kernel(n_blocks, *refs):
    for at in range(n_blocks):
        refs[-1][at] = refs[at][...]


def inverse(x):
    guess = pl.reciprocal(x, approx=True)
    return guess * (2.0 - x * guess)


def eigen_tile(m, half_norm, atoms):
    s00, s01, s02, s10, s11, s12, s20, s21, s22 = m
    coef_two = -2.0 * (
        s00 * s00 + s01 * s01 + s02 * s02 + s10 * s10 + s11 * s11 + s12 * s12 + s20 * s20 + s21 * s21 + s22 * s22
    )
    coef_one = 8.0 * (s00 * s12 * s21 + s11 * s20 * s02 + s22 * s01 * s10) - 8.0 * (
        s00 * s11 * s22 + s12 * s20 * s01 + s21 * s10 * s02
    )
    k00 = s00 + s11 + s22
    k11 = s00 - s11 - s22
    k22 = s11 - s00 - s22
    k33 = s22 - s00 - s11
    k01 = s12 - s21
    k02 = s20 - s02
    k03 = s01 - s10
    k12 = s01 + s10
    k13 = s20 + s02
    k23 = s12 + s21
    top0 = k00 * k11 - k01 * k01
    top1 = k00 * k12 - k01 * k02
    top2 = k00 * k13 - k01 * k03
    top3 = k01 * k12 - k11 * k02
    top4 = k01 * k13 - k11 * k03
    top5 = k02 * k13 - k12 * k03
    low0 = k02 * k13 - k03 * k12
    low1 = k02 * k23 - k03 * k22
    low2 = k02 * k33 - k03 * k23
    low3 = k12 * k23 - k13 * k22
    low4 = k12 * k33 - k13 * k23
    low5 = k22 * k33 - k23 * k23
    coef_zero = top0 * low5 - top1 * low4 + top2 * low3 + top3 * low2 - top4 * low1 + top5 * low0
    eigen = half_norm
    twice = coef_two + coef_two
    for _ in range(NEWTON):
        eigen_sq = eigen * eigen
        value = (eigen_sq + coef_two) * eigen_sq + coef_one * eigen + coef_zero
        slope = (4.0 * eigen_sq + twice) * eigen + coef_one
        eigen = eigen - value * inverse(slope)
    squared = jnp.maximum(2.0 * (half_norm - eigen) / atoms, 0.0)
    return jnp.exp(-squared / BAND)


def column_side(blocks_ref, vecs_ref):
    count, _, frames, atoms = blocks_ref.shape
    nv = vecs_ref.shape[2]
    cols = [
        centre(jnp.concatenate([blocks_ref[at, comp] for at in range(count)], axis=0)) for comp in range(3)
    ]
    col_square = cols[0] * cols[0] + cols[1] * cols[1] + cols[2] * cols[2]
    norm = lax.dot_general(
        jnp.ones((8, atoms), jnp.float32), col_square, NT,
        precision=lax.Precision.HIGHEST, preferred_element_type=jnp.float32,
    )[0:1, :]
    high, low = split(jnp.concatenate(cols, axis=0))
    side = jnp.concatenate([high, high, low], axis=1)
    ones = jnp.where(lax.broadcasted_iota(jnp.int32, (count * frames, LANES - nv), 1) == 0, 1.0, 0.0)
    vecs = jnp.concatenate([vecs_ref[at] for at in range(count)], axis=0)
    high, low = split(jnp.concatenate([vecs, ones], axis=1))
    return side, norm, jnp.concatenate([high, high, low], axis=0)


def multiply(row_side, row_norm, side, norm, vec, atoms, moment, tile):
    count = row_norm.shape[0]
    count_cols = norm.shape[1]
    moment[...] = lax.dot_general(row_side, side, NT, preferred_element_type=jnp.float32)
    for at in range(0, count, 8):
        m = [
            moment[a * count + at:a * count + at + 8, b * count_cols:(b + 1) * count_cols]
            for a in range(3) for b in range(3)
        ]
        half_norm = 0.5 * (row_norm[at:at + 8, 0:1] + norm)
        tile[at:at + 8, :] = eigen_tile(m, half_norm, atoms)
    high, low = split(tile[...])
    return jnp.dot(jnp.concatenate([high, low, high], axis=1), vec, preferred_element_type=jnp.float32)


def first_kernel(n_mine, *refs):
    slots, blocks_ref, vecs_ref = refs[:n_mine], refs[n_mine], refs[n_mine + 1]
    sum_ref, side_ref, norm_ref, moment, tile = refs[n_mine + 2:]
    _, frames, atoms = slots[0].shape
    groups, count, _ = sum_ref.shape
    side, norm, vec = column_side(blocks_ref, vecs_ref)
    for group in range(groups):
        own = slots[group * count // frames:(group + 1) * count // frames]
        rows = [centre(jnp.concatenate([ref[comp] for ref in own], axis=0)) for comp in range(3)]
        square = jnp.sum(rows[0] * rows[0] + rows[1] * rows[1] + rows[2] * rows[2], axis=1, keepdims=True)
        row_norm = jnp.broadcast_to(square, (count, LANES))
        high, low = split(jnp.concatenate(rows, axis=0))
        row_side = jnp.concatenate([high, low, high], axis=1)
        side_ref[group] = row_side
        norm_ref[group] = row_norm
        sum_ref[group] = multiply(row_side, row_norm, side, norm, vec, atoms, moment, tile)


def second_kernel(frames, sum_ref, side_ref, norm_ref, blocks_ref, vecs_ref, *refs):
    moment, tile = refs[-2:]
    atoms = blocks_ref.shape[-1]
    groups, count, _ = sum_ref.shape
    side, norm, vec = column_side(blocks_ref, vecs_ref)
    for group in range(groups):
        total = sum_ref[group] + multiply(side_ref[group], norm_ref[group], side, norm, vec, atoms, moment, tile)
        for at in range(count // frames):
            refs[group * count // frames + at][...] = total[at * frames:(at + 1) * frames, :]


def finish_kernel(nv, *refs):
    total = refs[0][...]
    for ref in refs[1:-1]:
        total = total + ref[...]
    refs[-1][...] = total[:, 0:nv] / total[:, nv:nv + 1]


def exchange(x, axis, mask, count):
    return lax.ppermute(x, axis, [(at, at ^ mask) for at in range(count)])


def call(kernel, outs, ins, name, scratch=(), megabytes=8, flops=0):
    out_shape = [jax.ShapeDtypeStruct(*out) for out in outs]
    moved = sum(x.size * 4 for x in ins)
    return pl.pallas_call(
        kernel,
        out_shape=out_shape,
        in_specs=[VM] * len(ins),
        out_specs=[VM] * len(outs),
        scratch_shapes=list(scratch),
        compiler_params=pltpu.CompilerParams(vmem_limit_bytes=megabytes * 1024 * 1024),
        cost_estimate=pl.CostEstimate(flops=flops, bytes_accessed=moved, transcendentals=0),
        name=name,
    )(*ins)


def per_device(n_row, n_col, row_frames, col_frames, vectors):
    comps, frames, atoms = row_frames.shape
    nv = vectors.shape[0]
    f32, bf16 = jnp.float32, jnp.bfloat16
    row_masks = [n_col >> at for at in range(1, n_col.bit_length())]
    col_masks = [1 << at for at in range(1, n_row.bit_length() - 1)]

    vecs = vectors.T[None]
    got_vecs = exchange(vecs, "row", col_masks[0], n_row)
    (vecs,) = call(copy_kernel, [((1, frames, nv), f32)], [vecs], "vectors", flops=1 << 30)
    order = [0]
    rows = {0: row_frames}
    for mask in row_masks:
        for slot in list(order):
            got = exchange(rows[slot], "col", mask, n_col)
            if not slot and mask == row_masks[0]:
                got, vecs = call(
                    after_far_kernel, [(got.shape, f32), ((2, frames, nv), f32)], [got, vecs, got_vecs], "after_far"
                )
            rows[slot ^ mask] = got
            order.append(slot ^ mask)
    col_order = [0]
    for mask in col_masks:
        col_order = col_order + [slot ^ mask for slot in col_order]
    cols = [col_frames] + [exchange(col_frames, "row", mask, n_row) for mask in col_order[1:]]
    (vecs,) = call(pass_kernel, [((2, frames, nv), f32)], [vecs, rows[row_masks[1]]], "vectors")
    for mask in col_masks[1:]:
        got = exchange(vecs, "row", mask, n_row)
        (vecs,) = call(join_kernel, [((2 * vecs.shape[0], frames, nv), f32)], [vecs, got], "vectors")
    (blocks,) = call(
        functools.partial(columns_kernel, len(cols)), [((len(cols), *col_frames.shape), f32)],
        [*cols, rows[row_masks[0]], rows[row_masks[1]]], "columns", flops=10 << 30,
    )
    other = exchange(blocks, "row", 1, n_row)
    other_vecs = exchange(vecs, "row", 1, n_row)

    half_cols = n_row // 2 * frames
    count = min(n_col, max(1, LANES // frames)) * frames
    groups = n_col * frames // count
    scratch = [pltpu.VMEM((3 * count, 3 * half_cols), f32), pltpu.VMEM((count, half_cols), f32)]
    work = 2 * 3 * n_col * frames * 3 * half_cols * 3 * atoms
    sums, side, norm = call(
        functools.partial(first_kernel, n_col),
        [((groups, count, LANES), f32), ((groups, 3 * count, 3 * atoms), bf16), ((groups, count, LANES), f32)],
        [*[rows[slot] for slot in order], blocks, vecs], "first_tile", scratch, 32, work << 8,
    )
    parts = call(
        functools.partial(second_kernel, frames), [((frames, LANES), f32)] * n_col,
        [sums, side, norm, other, other_vecs], "second_tile", scratch, 32, work,
    )
    shares = [parts[0]] + [
        exchange(parts[order.index(mask)], "col", mask, n_col) for mask in range(n_col - 1, 0, -1)
    ]
    (result,) = call(functools.partial(finish_kernel, nv), [((frames, nv), f32)], shares, "sum_divide")
    return result.T


def solution(mesh):
    return jax.shard_map(
        functools.partial(per_device, mesh.shape["row"], mesh.shape["col"]),
        mesh=mesh,
        in_specs=(
            P(None, ("row", "col"), None),
            P(None, ("col", "row"), None),
            P(None, ("col", "row")),
        ),
        out_specs=P(None, ("row", "col")),
        check_vma=False,
    )
```

```python
import functools

import jax
import jax.numpy as jnp
from jax import lax
from jax.experimental import pallas as pl
from jax.experimental.pallas import tpu as pltpu
from jax.sharding import PartitionSpec as P

NEWTON = 8
BAND = 2.0
LANES = 128
VM = pl.BlockSpec(memory_space=pltpu.VMEM)
NT = (((1,), (1,)), ((), ()))


def centre(frames):
    return frames - jnp.mean(frames, axis=-1, keepdims=True)


def split(x):
    high = x.astype(jnp.bfloat16)
    low = (x - high.astype(jnp.float32)).astype(jnp.bfloat16)
    return high, low


def copy_kernel(in_ref, out_ref):
    out_ref[...] = in_ref[...]


def join_kernel(first_ref, second_ref, out_ref):
    count = second_ref.shape[0]
    out_ref[0:count] = first_ref[...]
    out_ref[count:] = second_ref[...]


def after_far_kernel(far_ref, vec_ref, got_ref, far_out, vec_out):
    far_out[...] = far_ref[...]
    join_kernel(vec_ref, got_ref, vec_out)


def pass_kernel(in_ref, *refs):
    refs[-1][...] = in_ref[...]


def columns_kernel(n_blocks, *refs):
    for at in range(n_blocks):
        refs[-1][at] = refs[at][...]


def inverse(x):
    guess = pl.reciprocal(x, approx=True)
    return guess * (2.0 - x * guess)


def eigen_tile(m, half_norm, atoms):
    s00, s01, s02, s10, s11, s12, s20, s21, s22 = m
    coef_two = -2.0 * (
        s00 * s00 + s01 * s01 + s02 * s02 + s10 * s10 + s11 * s11 + s12 * s12 + s20 * s20 + s21 * s21 + s22 * s22
    )
    coef_one = 8.0 * (s00 * s12 * s21 + s11 * s20 * s02 + s22 * s01 * s10) - 8.0 * (
        s00 * s11 * s22 + s12 * s20 * s01 + s21 * s10 * s02
    )
    k00 = s00 + s11 + s22
    k11 = s00 - s11 - s22
    k22 = s11 - s00 - s22
    k33 = s22 - s00 - s11
    k01 = s12 - s21
    k02 = s20 - s02
    k03 = s01 - s10
    k12 = s01 + s10
    k13 = s20 + s02
    k23 = s12 + s21
    top0 = k00 * k11 - k01 * k01
    top1 = k00 * k12 - k01 * k02
    top2 = k00 * k13 - k01 * k03
    top3 = k01 * k12 - k11 * k02
    top4 = k01 * k13 - k11 * k03
    top5 = k02 * k13 - k12 * k03
    low0 = k02 * k13 - k03 * k12
    low1 = k02 * k23 - k03 * k22
    low2 = k02 * k33 - k03 * k23
    low3 = k12 * k23 - k13 * k22
    low4 = k12 * k33 - k13 * k23
    low5 = k22 * k33 - k23 * k23
    coef_zero = top0 * low5 - top1 * low4 + top2 * low3 + top3 * low2 - top4 * low1 + top5 * low0
    eigen = half_norm
    twice = coef_two + coef_two
    for _ in range(NEWTON):
        eigen_sq = eigen * eigen
        value = (eigen_sq + coef_two) * eigen_sq + coef_one * eigen + coef_zero
        slope = (4.0 * eigen_sq + twice) * eigen + coef_one
        eigen = eigen - value * inverse(slope)
    squared = jnp.maximum(2.0 * (half_norm - eigen) / atoms, 0.0)
    return jnp.exp(-squared / BAND)


def column_side(blocks_ref):
    count, _, _, atoms = blocks_ref.shape
    cols = [
        centre(jnp.concatenate([blocks_ref[at, comp] for at in range(count)], axis=0)) for comp in range(3)
    ]
    col_square = cols[0] * cols[0] + cols[1] * cols[1] + cols[2] * cols[2]
    norm = lax.dot_general(
        jnp.ones((8, atoms), jnp.float32), col_square, NT,
        precision=lax.Precision.HIGHEST, preferred_element_type=jnp.float32,
    )
    high, low = split(jnp.concatenate(cols, axis=0))
    return jnp.concatenate([high, high, low], axis=1), norm


def vector_side(vecs_ref):
    count, frames, nv = vecs_ref.shape
    ones = jnp.where(lax.broadcasted_iota(jnp.int32, (count * frames, LANES - nv), 1) == 0, 1.0, 0.0)
    vecs = jnp.concatenate([vecs_ref[at] for at in range(count)], axis=0)
    high, low = split(jnp.concatenate([vecs, ones], axis=1))
    return [high, high, low]


def row_side(slots):
    rows = [centre(jnp.concatenate([ref[comp] for ref in slots], axis=0)) for comp in range(3)]
    square = jnp.sum(rows[0] * rows[0] + rows[1] * rows[1] + rows[2] * rows[2], axis=1, keepdims=True)
    high, low = split(jnp.concatenate(rows, axis=0))
    return jnp.concatenate([high, low, high], axis=1), jnp.broadcast_to(square, (square.shape[0], LANES))


def kernel_tile(rows, row_norm, side, norm, moment, tile):
    count = row_norm.shape[0]
    count_cols = norm.shape[1]
    atoms = side.shape[1] // 3
    moment[0:3 * count, :] = lax.dot_general(rows, side, NT, preferred_element_type=jnp.float32)
    for at in range(0, count, 8):
        m = [
            moment[a * count + at:a * count + at + 8, b * count_cols:(b + 1) * count_cols]
            for a in range(3) for b in range(3)
        ]
        half_norm = 0.5 * (row_norm[at:at + 8, 0:1] + norm[0:1, :])
        tile[at:at + 8, :] = eigen_tile(m, half_norm, atoms)


def early_kernel(n_early, *refs):
    slots, blocks_ref = refs[:n_early], refs[n_early]
    rows_ref, row_norm_ref, tile_ref, side_ref, norm_ref, moment = refs[n_early + 1:]
    frames = slots[0].shape[1]
    groups, count, _ = tile_ref.shape
    side, norm = column_side(blocks_ref)
    side_ref[...] = side
    norm_ref[...] = norm
    for group in range(groups):
        own = slots[group * count // frames:(group + 1) * count // frames]
        used = len(own) * frames
        rows, row_norm = row_side(own)
        for comp in range(3):
            rows_ref[group, comp * count:comp * count + used, :] = rows[comp * used:(comp + 1) * used]
        row_norm_ref[group, 0:used, :] = row_norm
        kernel_tile(rows, row_norm, side, norm, moment, tile_ref.at[group, 0:used])


def last_kernel(row_ref, side_ref, norm_ref, *refs):
    rows_ref, row_norm_ref, tile_ref, moment = refs[3:]
    frames = row_ref.shape[1]
    groups, count, _ = tile_ref.shape
    rows, row_norm = row_side([row_ref])
    for comp in range(3):
        rows_ref[groups - 1, (comp + 1) * count - frames:(comp + 1) * count, :] = rows[comp * frames:(comp + 1) * frames]
    row_norm_ref[groups - 1, count - frames:, :] = row_norm
    kernel_tile(rows, row_norm, side_ref[...], norm_ref[...], moment, tile_ref.at[groups - 1, count - frames:count])


def second_kernel(frames, rows_ref, row_norm_ref, tile_ref, vecs_ref, blocks_ref, other_vecs_ref, *refs):
    out_refs, moment, other_tile = refs[:-2], refs[-2], refs[-1]
    groups, count, _ = tile_ref.shape
    side, norm = column_side(blocks_ref)
    vecs = jnp.concatenate(vector_side(vecs_ref) + vector_side(other_vecs_ref), axis=0)
    for group in range(groups):
        kernel_tile(rows_ref[group], row_norm_ref[group], side, norm, moment, other_tile)
        high, low = split(tile_ref[group])
        other_high, other_low = split(other_tile[...])
        total = jnp.dot(
            jnp.concatenate([high, low, high, other_high, other_low, other_high], axis=1), vecs,
            preferred_element_type=jnp.float32,
        )
        for at in range(count // frames):
            out_refs[group * count // frames + at][...] = total[at * frames:(at + 1) * frames, :]


def finish_kernel(nv, *refs):
    total = refs[0][...]
    for ref in refs[1:-1]:
        total = total + ref[...]
    refs[-1][...] = total[:, 0:nv] / total[:, nv:nv + 1]


def exchange(x, axis, mask, count):
    return lax.ppermute(x, axis, [(at, at ^ mask) for at in range(count)])


def call(kernel, outs, ins, name, scratch=(), megabytes=8, flops=0, aliases=None):
    out_shape = [jax.ShapeDtypeStruct(*out) for out in outs]
    moved = sum(x.size * 4 for x in ins)
    return pl.pallas_call(
        kernel,
        out_shape=out_shape,
        in_specs=[VM] * len(ins),
        out_specs=[VM] * len(outs),
        scratch_shapes=list(scratch),
        input_output_aliases=aliases or {},
        compiler_params=pltpu.CompilerParams(vmem_limit_bytes=megabytes * 1024 * 1024),
        cost_estimate=pl.CostEstimate(flops=flops, bytes_accessed=moved, transcendentals=0),
        name=name,
    )(*ins)


def per_device(n_row, n_col, row_frames, col_frames, vectors):
    comps, frames, atoms = row_frames.shape
    nv = vectors.shape[0]
    f32, bf16 = jnp.float32, jnp.bfloat16
    row_masks = [n_col >> at for at in range(1, n_col.bit_length())]
    col_masks = [1 << at for at in range(1, n_row.bit_length() - 1)]

    vecs = vectors.T[None]
    got_vecs = exchange(vecs, "row", col_masks[0], n_row)
    (vecs,) = call(copy_kernel, [((1, frames, nv), f32)], [vecs], "vectors", flops=1 << 30)
    order = [0]
    rows = {0: row_frames}
    for mask in row_masks:
        for slot in list(order):
            got = exchange(rows[slot], "col", mask, n_col)
            if not slot and mask == row_masks[0]:
                got, vecs = call(
                    after_far_kernel, [(got.shape, f32), ((2, frames, nv), f32)], [got, vecs, got_vecs], "after_far"
                )
            rows[slot ^ mask] = got
            order.append(slot ^ mask)
    col_order = [0]
    for mask in col_masks:
        col_order = col_order + [slot ^ mask for slot in col_order]
    cols = [col_frames] + [exchange(col_frames, "row", mask, n_row) for mask in col_order[1:]]
    (vecs,) = call(pass_kernel, [((2, frames, nv), f32)], [vecs, rows[row_masks[1]]], "vectors")
    for mask in col_masks[1:]:
        got = exchange(vecs, "row", mask, n_row)
        (vecs,) = call(join_kernel, [((2 * vecs.shape[0], frames, nv), f32)], [vecs, got], "vectors")
    (blocks,) = call(
        functools.partial(columns_kernel, len(cols)), [((len(cols), *col_frames.shape), f32)],
        [*cols, rows[row_masks[0]], rows[row_masks[1]]], "columns", flops=10 << 30,
    )
    other = exchange(blocks, "row", 1, n_row)
    other_vecs = exchange(vecs, "row", 1, n_row)

    half_cols = n_row // 2 * frames
    count = min(n_col, max(1, LANES // frames)) * frames
    groups = n_col * frames // count
    moment = pltpu.VMEM((3 * count, 3 * half_cols), f32)
    tile = pltpu.VMEM((count, half_cols), f32)
    work = 2 * 3 * n_col * frames * 3 * half_cols * 3 * atoms
    outs = [
        ((groups, 3 * count, 3 * atoms), bf16), ((groups, count, LANES), f32), ((groups, count, half_cols), f32),
    ]
    *kept, side, norm = call(
        functools.partial(early_kernel, n_col - 1),
        outs + [((3 * half_cols, 3 * atoms), bf16), ((8, half_cols), f32)],
        [*[rows[slot] for slot in order[:-1]], blocks], "early_tile", [moment], 32, work,
    )
    kept = call(
        last_kernel, outs, [rows[order[-1]], side, norm, *kept], "last_tile",
        [pltpu.VMEM((3 * frames, 3 * half_cols), f32)], 32, work << 8, {3: 0, 4: 1, 5: 2},
    )
    parts = call(
        functools.partial(second_kernel, frames), [((frames, LANES), f32)] * n_col,
        [*kept, vecs, other, other_vecs], "second_tile", [moment, tile], 32, work,
    )
    shares = [parts[0]] + [
        exchange(parts[order.index(mask)], "col", mask, n_col) for mask in range(n_col - 1, 0, -1)
    ]
    (result,) = call(functools.partial(finish_kernel, nv), [((frames, nv), f32)], shares, "sum_divide")
    return result.T


def solution(mesh):
    return jax.shard_map(
        functools.partial(per_device, mesh.shape["row"], mesh.shape["col"]),
        mesh=mesh,
        in_specs=(
            P(None, ("row", "col"), None),
            P(None, ("col", "row"), None),
            P(None, ("col", "row")),
        ),
        out_specs=P(None, ("row", "col")),
        check_vma=False,
    )
```

```python
import functools

import jax
import jax.numpy as jnp
from jax import lax
from jax.experimental import pallas as pl
from jax.experimental.pallas import tpu as pltpu
from jax.sharding import PartitionSpec as P

NEWTON = 8
BAND = 2.0
LANES = 128
VM = pl.BlockSpec(memory_space=pltpu.VMEM)
NT = (((1,), (1,)), ((), ()))


def centre(frames):
    return frames - jnp.mean(frames, axis=-1, keepdims=True)


def split(x):
    high = x.astype(jnp.bfloat16)
    low = (x - high.astype(jnp.float32)).astype(jnp.bfloat16)
    return high, low


def copy_kernel(in_ref, out_ref):
    out_ref[...] = in_ref[...]


def join_kernel(first_ref, second_ref, *refs):
    count = first_ref.shape[0]
    refs[-1][0:count] = first_ref[...]
    refs[-1][count:] = second_ref[...]


def join_inner_kernel(first_ref, second_ref, out_ref):
    count = first_ref.shape[1]
    out_ref[:, 0:count] = first_ref[...]
    out_ref[:, count:] = second_ref[...]


def after_far_kernel(far_ref, vec_ref, got_ref, far_out, vec_out):
    far_out[...] = far_ref[...]
    join_kernel(vec_ref, got_ref, vec_out)


def columns_kernel(n_blocks, *refs):
    for at in range(n_blocks):
        refs[-1][at] = refs[at][...]


def inverse(x):
    guess = pl.reciprocal(x, approx=True)
    return guess * (2.0 - x * guess)


def eigen_tile(m, half_norm, atoms):
    s00, s01, s02, s10, s11, s12, s20, s21, s22 = m
    coef_two = -2.0 * (
        s00 * s00 + s01 * s01 + s02 * s02 + s10 * s10 + s11 * s11 + s12 * s12 + s20 * s20 + s21 * s21 + s22 * s22
    )
    coef_one = 8.0 * (s00 * s12 * s21 + s11 * s20 * s02 + s22 * s01 * s10) - 8.0 * (
        s00 * s11 * s22 + s12 * s20 * s01 + s21 * s10 * s02
    )
    k00 = s00 + s11 + s22
    k11 = s00 - s11 - s22
    k22 = s11 - s00 - s22
    k33 = s22 - s00 - s11
    k01 = s12 - s21
    k02 = s20 - s02
    k03 = s01 - s10
    k12 = s01 + s10
    k13 = s20 + s02
    k23 = s12 + s21
    top0 = k00 * k11 - k01 * k01
    top1 = k00 * k12 - k01 * k02
    top2 = k00 * k13 - k01 * k03
    top3 = k01 * k12 - k11 * k02
    top4 = k01 * k13 - k11 * k03
    top5 = k02 * k13 - k12 * k03
    low0 = k02 * k13 - k03 * k12
    low1 = k02 * k23 - k03 * k22
    low2 = k02 * k33 - k03 * k23
    low3 = k12 * k23 - k13 * k22
    low4 = k12 * k33 - k13 * k23
    low5 = k22 * k33 - k23 * k23
    coef_zero = top0 * low5 - top1 * low4 + top2 * low3 + top3 * low2 - top4 * low1 + top5 * low0
    eigen = half_norm
    twice = coef_two + coef_two
    for _ in range(NEWTON):
        eigen_sq = eigen * eigen
        value = (eigen_sq + coef_two) * eigen_sq + coef_one * eigen + coef_zero
        slope = (4.0 * eigen_sq + twice) * eigen + coef_one
        eigen = eigen - value * inverse(slope)
    squared = jnp.maximum(2.0 * (half_norm - eigen) / atoms, 0.0)
    return jnp.exp(-squared / BAND)


def column_side(blocks_ref):
    count, _, _, atoms = blocks_ref.shape
    cols = [
        centre(jnp.concatenate([blocks_ref[at, comp] for at in range(count)], axis=0)) for comp in range(3)
    ]
    col_square = cols[0] * cols[0] + cols[1] * cols[1] + cols[2] * cols[2]
    norm = lax.dot_general(
        jnp.ones((8, atoms), jnp.float32), col_square, NT,
        precision=lax.Precision.HIGHEST, preferred_element_type=jnp.float32,
    )
    high, low = split(jnp.concatenate(cols, axis=0))
    return jnp.concatenate([high, high, low], axis=1), norm


def vector_side(vecs_ref):
    count, frames, nv = vecs_ref.shape
    ones = jnp.where(lax.broadcasted_iota(jnp.int32, (count * frames, LANES - nv), 1) == 0, 1.0, 0.0)
    vecs = jnp.concatenate([vecs_ref[at] for at in range(count)], axis=0)
    high, low = split(jnp.concatenate([vecs, ones], axis=1))
    return [high, high, low]


def row_side(slots):
    rows = [centre(jnp.concatenate([ref[comp] for ref in slots], axis=0)) for comp in range(3)]
    square = jnp.sum(rows[0] * rows[0] + rows[1] * rows[1] + rows[2] * rows[2], axis=1, keepdims=True)
    high, low = split(jnp.concatenate(rows, axis=0))
    return jnp.concatenate([high, low, high], axis=1), jnp.broadcast_to(square, (square.shape[0], LANES))


def kernel_tile(rows, row_norm, side, norm, moment, tile):
    count = row_norm.shape[0]
    count_cols = norm.shape[1]
    atoms = side.shape[1] // 3
    moment[0:3 * count, :] = lax.dot_general(rows, side, NT, preferred_element_type=jnp.float32)
    for at in range(0, count, 8):
        m = [
            moment[a * count + at:a * count + at + 8, b * count_cols:(b + 1) * count_cols]
            for a in range(3) for b in range(3)
        ]
        half_norm = 0.5 * (row_norm[at:at + 8, 0:1] + norm[0:1, :])
        tile[at:at + 8, :] = eigen_tile(m, half_norm, atoms)


def early_kernel(n_early, *refs):
    slots, blocks_ref = refs[:n_early], refs[n_early]
    rows_ref, row_norm_ref, tile_ref, side_ref, norm_ref, moment = refs[n_early + 1:]
    frames = slots[0].shape[1]
    groups, count, _ = tile_ref.shape
    side, norm = column_side(blocks_ref)
    side_ref[...] = side
    norm_ref[...] = norm
    for group in range(groups):
        own = slots[group * count // frames:(group + 1) * count // frames]
        used = len(own) * frames
        rows, row_norm = row_side(own)
        for comp in range(3):
            rows_ref[group, comp * count:comp * count + used, :] = rows[comp * used:(comp + 1) * used]
        row_norm_ref[group, 0:used, :] = row_norm
        kernel_tile(rows, row_norm, side, norm, moment, tile_ref.at[group, 0:used])


def last_kernel(row_ref, side_ref, norm_ref, *refs):
    rows_ref, row_norm_ref, tile_ref, moment = refs[3:]
    frames = row_ref.shape[1]
    groups, count, _ = tile_ref.shape
    rows, row_norm = row_side([row_ref])
    for comp in range(3):
        rows_ref[groups - 1, (comp + 1) * count - frames:(comp + 1) * count, :] = rows[comp * frames:(comp + 1) * frames]
    row_norm_ref[groups - 1, count - frames:, :] = row_norm
    kernel_tile(rows, row_norm, side_ref[...], norm_ref[...], moment, tile_ref.at[groups - 1, count - frames:count])


def second_kernel(frames, rows_ref, row_norm_ref, tile_ref, vecs_ref, blocks_ref, *refs):
    out_refs, moment, other_tile = refs[:-2], refs[-2], refs[-1]
    groups, count, _ = tile_ref.shape
    side, norm = column_side(blocks_ref)
    vecs = jnp.concatenate(vector_side(vecs_ref.at[0]) + vector_side(vecs_ref.at[1]), axis=0)
    for group in range(groups):
        kernel_tile(rows_ref[group], row_norm_ref[group], side, norm, moment, other_tile)
        high, low = split(tile_ref[group])
        other_high, other_low = split(other_tile[...])
        total = jnp.dot(
            jnp.concatenate([high, low, high, other_high, other_low, other_high], axis=1), vecs,
            preferred_element_type=jnp.float32,
        )
        for at in range(count // frames):
            out_refs[group * count // frames + at][...] = total[at * frames:(at + 1) * frames, :]


def finish_kernel(nv, *refs):
    total = refs[0][...]
    for ref in refs[1:-1]:
        total = total + ref[...]
    refs[-1][...] = total[:, 0:nv] / total[:, nv:nv + 1]


def exchange(x, axis, mask, count):
    return lax.ppermute(x, axis, [(at, at ^ mask) for at in range(count)])


def call(kernel, outs, ins, name, scratch=(), megabytes=8, flops=0, aliases=None):
    out_shape = [jax.ShapeDtypeStruct(*out) for out in outs]
    moved = sum(x.size * 4 for x in ins)
    return pl.pallas_call(
        kernel,
        out_shape=out_shape,
        in_specs=[VM] * len(ins),
        out_specs=[VM] * len(outs),
        scratch_shapes=list(scratch),
        input_output_aliases=aliases or {},
        compiler_params=pltpu.CompilerParams(vmem_limit_bytes=megabytes * 1024 * 1024),
        cost_estimate=pl.CostEstimate(flops=flops, bytes_accessed=moved, transcendentals=0),
        name=name,
    )(*ins)


def per_device(n_row, n_col, row_frames, col_frames, vectors):
    comps, frames, atoms = row_frames.shape
    nv = vectors.shape[0]
    f32, bf16 = jnp.float32, jnp.bfloat16
    row_masks = [n_col >> at for at in range(1, n_col.bit_length())]
    col_masks = [1 << at for at in range(1, n_row.bit_length() - 1)]

    vecs = vectors.T[None]
    got_vecs = exchange(vecs, "row", col_masks[0], n_row)
    (vecs,) = call(copy_kernel, [((1, frames, nv), f32)], [vecs], "vectors", flops=1 << 30)
    order = [0]
    rows = {0: row_frames}
    for mask in row_masks:
        for slot in list(order):
            got = exchange(rows[slot], "col", mask, n_col)
            if not slot and mask == row_masks[0]:
                got, vecs = call(
                    after_far_kernel, [(got.shape, f32), ((2, frames, nv), f32)], [got, vecs, got_vecs], "after_far"
                )
            rows[slot ^ mask] = got
            order.append(slot ^ mask)
    col_order = [0]
    for mask in col_masks:
        col_order = col_order + [slot ^ mask for slot in col_order]
    cols = [col_frames] + [exchange(col_frames, "row", mask, n_row) for mask in col_order[1:]]
    got = exchange(vecs, "row", 1, n_row)
    (vecs,) = call(
        join_kernel, [((2, 2, frames, nv), f32)], [vecs[None], got[None], rows[row_masks[1]]], "vectors"
    )
    for mask in col_masks[1:]:
        got = exchange(vecs, "row", mask, n_row)
        (vecs,) = call(join_inner_kernel, [((2, 2 * vecs.shape[1], frames, nv), f32)], [vecs, got], "vectors")
    (blocks,) = call(
        functools.partial(columns_kernel, len(cols)), [((len(cols), *col_frames.shape), f32)],
        [*cols, rows[row_masks[0]], rows[row_masks[1]]], "columns", flops=10 << 30,
    )
    other = exchange(blocks, "row", 1, n_row)

    half_cols = n_row // 2 * frames
    count = min(n_col, max(1, LANES // frames)) * frames
    groups = n_col * frames // count
    moment = pltpu.VMEM((3 * count, 3 * half_cols), f32)
    tile = pltpu.VMEM((count, half_cols), f32)
    work = 2 * 3 * n_col * frames * 3 * half_cols * 3 * atoms
    outs = [
        ((groups, 3 * count, 3 * atoms), bf16), ((groups, count, LANES), f32), ((groups, count, half_cols), f32),
    ]
    *kept, side, norm = call(
        functools.partial(early_kernel, n_col - 1),
        outs + [((3 * half_cols, 3 * atoms), bf16), ((8, half_cols), f32)],
        [*[rows[slot] for slot in order[:-1]], blocks], "early_tile", [moment], 32, work,
    )
    kept = call(
        last_kernel, outs, [rows[order[-1]], side, norm, *kept], "last_tile",
        [pltpu.VMEM((3 * frames, 3 * half_cols), f32)], 32, work << 8, {3: 0, 4: 1, 5: 2},
    )
    parts = call(
        functools.partial(second_kernel, frames), [((frames, LANES), f32)] * n_col,
        [*kept, vecs, other], "second_tile", [moment, tile], 32, work,
    )
    shares = [parts[0]] + [
        exchange(parts[order.index(mask)], "col", mask, n_col) for mask in range(n_col - 1, 0, -1)
    ]
    (result,) = call(functools.partial(finish_kernel, nv), [((frames, nv), f32)], shares, "sum_divide")
    return result.T


def solution(mesh):
    return jax.shard_map(
        functools.partial(per_device, mesh.shape["row"], mesh.shape["col"]),
        mesh=mesh,
        in_specs=(
            P(None, ("row", "col"), None),
            P(None, ("col", "row"), None),
            P(None, ("col", "row")),
        ),
        out_specs=P(None, ("row", "col")),
        check_vma=False,
    )
```

```python
import functools

import jax
import jax.numpy as jnp
from jax import lax
from jax.experimental import pallas as pl
from jax.experimental.pallas import tpu as pltpu
from jax.sharding import PartitionSpec as P

NEWTON = 8
BAND = 2.0
LANES = 128
VM = pl.BlockSpec(memory_space=pltpu.VMEM)
NT = (((1,), (1,)), ((), ()))


def centre(frames):
    return frames - jnp.mean(frames, axis=-1, keepdims=True)


def split(x):
    high = x.astype(jnp.bfloat16)
    low = (x - high.astype(jnp.float32)).astype(jnp.bfloat16)
    return high, low


def copy_kernel(in_ref, out_ref):
    out_ref[...] = in_ref[...]


def pack_kernel(cols_ref, vec_ref, out_ref):
    comps, frames, atoms = cols_ref.shape
    for comp in range(comps):
        out_ref[comp * frames:(comp + 1) * frames, :] = cols_ref[comp]
    groups = atoms // vec_ref.shape[1]
    step = frames // groups
    out_ref[comps * frames:, :] = jnp.concatenate(
        [vec_ref[group * step:(group + 1) * step, :] for group in range(groups)], axis=1
    )


def copy_kernel(in_ref, out_ref):
    out_ref[...] = in_ref[...]


def columns_kernel(n_blocks, *refs):
    for at in range(n_blocks):
        refs[-1][at] = refs[at][...]


def inverse(x):
    guess = pl.reciprocal(x, approx=True)
    return guess * (2.0 - x * guess)


def eigen_tile(m, half_norm, atoms):
    s00, s01, s02, s10, s11, s12, s20, s21, s22 = m
    coef_two = -2.0 * (
        s00 * s00 + s01 * s01 + s02 * s02 + s10 * s10 + s11 * s11 + s12 * s12 + s20 * s20 + s21 * s21 + s22 * s22
    )
    coef_one = 8.0 * (s00 * s12 * s21 + s11 * s20 * s02 + s22 * s01 * s10) - 8.0 * (
        s00 * s11 * s22 + s12 * s20 * s01 + s21 * s10 * s02
    )
    k00 = s00 + s11 + s22
    k11 = s00 - s11 - s22
    k22 = s11 - s00 - s22
    k33 = s22 - s00 - s11
    k01 = s12 - s21
    k02 = s20 - s02
    k03 = s01 - s10
    k12 = s01 + s10
    k13 = s20 + s02
    k23 = s12 + s21
    top0 = k00 * k11 - k01 * k01
    top1 = k00 * k12 - k01 * k02
    top2 = k00 * k13 - k01 * k03
    top3 = k01 * k12 - k11 * k02
    top4 = k01 * k13 - k11 * k03
    top5 = k02 * k13 - k12 * k03
    low0 = k02 * k13 - k03 * k12
    low1 = k02 * k23 - k03 * k22
    low2 = k02 * k33 - k03 * k23
    low3 = k12 * k23 - k13 * k22
    low4 = k12 * k33 - k13 * k23
    low5 = k22 * k33 - k23 * k23
    coef_zero = top0 * low5 - top1 * low4 + top2 * low3 + top3 * low2 - top4 * low1 + top5 * low0
    eigen = half_norm
    twice = coef_two + coef_two
    for _ in range(NEWTON):
        eigen_sq = eigen * eigen
        value = (eigen_sq + coef_two) * eigen_sq + coef_one * eigen + coef_zero
        slope = (4.0 * eigen_sq + twice) * eigen + coef_one
        eigen = eigen - value * inverse(slope)
    squared = jnp.maximum(2.0 * (half_norm - eigen) / atoms, 0.0)
    return jnp.exp(-squared / BAND)


def column_side(blocks_ref, frames):
    count, _, atoms = blocks_ref.shape
    cols = [
        centre(jnp.concatenate([blocks_ref[at, comp * frames:(comp + 1) * frames, :] for at in range(count)], axis=0))
        for comp in range(3)
    ]
    col_square = cols[0] * cols[0] + cols[1] * cols[1] + cols[2] * cols[2]
    norm = lax.dot_general(
        jnp.ones((8, atoms), jnp.float32), col_square, NT,
        precision=lax.Precision.HIGHEST, preferred_element_type=jnp.float32,
    )
    high, low = split(jnp.concatenate(cols, axis=0))
    return jnp.concatenate([high, high, low], axis=1), norm


def vector_side(blocks_ref, frames, nv):
    count, _, atoms = blocks_ref.shape
    groups = atoms // nv
    step = frames // groups
    lane = lax.broadcasted_iota(jnp.int32, (step, LANES), 1)
    parts = []
    for at in range(count):
        for group in range(groups):
            place = group * nv
            piece = blocks_ref[at, 3 * frames:, place // LANES * LANES:place // LANES * LANES + LANES]
            if place % LANES:
                piece = pltpu.roll(piece, LANES - place % LANES, 1)
            parts.append(jnp.where(lane < nv, piece, jnp.where(lane == nv, 1.0, 0.0)))
    high, low = split(jnp.concatenate(parts, axis=0))
    return [high, high, low]


def row_side(slots):
    rows = [centre(jnp.concatenate([ref[comp] for ref in slots], axis=0)) for comp in range(3)]
    square = jnp.sum(rows[0] * rows[0] + rows[1] * rows[1] + rows[2] * rows[2], axis=1, keepdims=True)
    high, low = split(jnp.concatenate(rows, axis=0))
    return jnp.concatenate([high, low, high], axis=1), jnp.broadcast_to(square, (square.shape[0], LANES))


def kernel_tile(rows, row_norm, side, norm, moment, tile):
    count = row_norm.shape[0]
    count_cols = norm.shape[1]
    atoms = side.shape[1] // 3
    moment[0:3 * count, :] = lax.dot_general(rows, side, NT, preferred_element_type=jnp.float32)
    for at in range(0, count, 8):
        m = [
            moment[a * count + at:a * count + at + 8, b * count_cols:(b + 1) * count_cols]
            for a in range(3) for b in range(3)
        ]
        half_norm = 0.5 * (row_norm[at:at + 8, 0:1] + norm[0:1, :])
        tile[at:at + 8, :] = eigen_tile(m, half_norm, atoms)


def early_kernel(n_early, *refs):
    slots, blocks_ref = refs[:n_early], refs[n_early]
    rows_ref, row_norm_ref, tile_ref, side_ref, norm_ref, moment = refs[n_early + 1:]
    frames = slots[0].shape[1]
    groups, count, _ = tile_ref.shape
    side, norm = column_side(blocks_ref, frames)
    side_ref[...] = side
    norm_ref[...] = norm
    for group in range(groups):
        own = slots[group * count // frames:(group + 1) * count // frames]
        used = len(own) * frames
        rows, row_norm = row_side(own)
        for comp in range(3):
            rows_ref[group, comp * count:comp * count + used, :] = rows[comp * used:(comp + 1) * used]
        row_norm_ref[group, 0:used, :] = row_norm
        kernel_tile(rows, row_norm, side, norm, moment, tile_ref.at[group, 0:used])


def last_kernel(row_ref, side_ref, norm_ref, *refs):
    rows_ref, row_norm_ref, tile_ref, moment = refs[3:]
    frames = row_ref.shape[1]
    groups, count, _ = tile_ref.shape
    rows, row_norm = row_side([row_ref])
    for comp in range(3):
        rows_ref[groups - 1, (comp + 1) * count - frames:(comp + 1) * count, :] = rows[comp * frames:(comp + 1) * frames]
    row_norm_ref[groups - 1, count - frames:, :] = row_norm
    kernel_tile(rows, row_norm, side_ref[...], norm_ref[...], moment, tile_ref.at[groups - 1, count - frames:count])


def second_kernel(frames, nv, rows_ref, row_norm_ref, tile_ref, own_ref, blocks_ref, *refs):
    out_refs, moment, other_tile = refs[:-2], refs[-2], refs[-1]
    groups, count, _ = tile_ref.shape
    side, norm = column_side(blocks_ref, frames)
    vecs = jnp.concatenate(vector_side(own_ref, frames, nv) + vector_side(blocks_ref, frames, nv), axis=0)
    for group in range(groups):
        kernel_tile(rows_ref[group], row_norm_ref[group], side, norm, moment, other_tile)
        high, low = split(tile_ref[group])
        other_high, other_low = split(other_tile[...])
        total = jnp.dot(
            jnp.concatenate([high, low, high, other_high, other_low, other_high], axis=1), vecs,
            preferred_element_type=jnp.float32,
        )
        for at in range(count // frames):
            out_refs[group * count // frames + at][...] = total[at * frames:(at + 1) * frames, :]


def finish_kernel(nv, *refs):
    total = refs[0][...]
    for ref in refs[1:-1]:
        total = total + ref[...]
    refs[-1][...] = total[:, 0:nv] / total[:, nv:nv + 1]


def exchange(x, axis, mask, count):
    return lax.ppermute(x, axis, [(at, at ^ mask) for at in range(count)])


def call(kernel, outs, ins, name, scratch=(), megabytes=8, flops=0, aliases=None):
    out_shape = [jax.ShapeDtypeStruct(*out) for out in outs]
    moved = sum(x.size * 4 for x in ins)
    return pl.pallas_call(
        kernel,
        out_shape=out_shape,
        in_specs=[VM] * len(ins),
        out_specs=[VM] * len(outs),
        scratch_shapes=list(scratch),
        input_output_aliases=aliases or {},
        compiler_params=pltpu.CompilerParams(vmem_limit_bytes=megabytes * 1024 * 1024),
        cost_estimate=pl.CostEstimate(flops=flops, bytes_accessed=moved, transcendentals=0),
        name=name,
    )(*ins)


def per_device(n_row, n_col, row_frames, col_frames, vectors):
    comps, frames, atoms = row_frames.shape
    nv = vectors.shape[0]
    f32, bf16 = jnp.float32, jnp.bfloat16
    row_masks = [n_col >> at for at in range(1, n_col.bit_length())]
    col_masks = [1 << at for at in range(1, n_row.bit_length() - 1)]

    packed_shape = (comps * frames + frames * nv // atoms, atoms)
    (packed,) = call(pack_kernel, [(packed_shape, f32)], [col_frames, vectors.T], "pack")
    order = [0]
    rows = {0: row_frames}
    for mask in row_masks:
        for slot in list(order):
            got = exchange(rows[slot], "col", mask, n_col)
            if not slot and mask == row_masks[0]:
                (got,) = call(copy_kernel, [(got.shape, f32)], [got], "far_rows", flops=10 << 30)
            rows[slot ^ mask] = got
            order.append(slot ^ mask)
    col_order = [0]
    for mask in col_masks:
        col_order = col_order + [slot ^ mask for slot in col_order]
    cols = [packed] + [exchange(packed, "row", mask, n_row) for mask in col_order[1:]]
    (blocks,) = call(
        functools.partial(columns_kernel, len(cols)), [((len(cols), *packed_shape), f32)],
        [*cols, rows[row_masks[0]], rows[row_masks[1]]], "columns", flops=10 << 30,
    )
    other = exchange(blocks, "row", 1, n_row)

    half_cols = n_row // 2 * frames
    count = min(n_col, max(1, LANES // frames)) * frames
    groups = n_col * frames // count
    moment = pltpu.VMEM((3 * count, 3 * half_cols), f32)
    tile = pltpu.VMEM((count, half_cols), f32)
    work = 2 * 3 * n_col * frames * 3 * half_cols * 3 * atoms
    outs = [
        ((groups, 3 * count, 3 * atoms), bf16), ((groups, count, LANES), f32), ((groups, count, half_cols), f32),
    ]
    *kept, side, norm = call(
        functools.partial(early_kernel, n_col - 1),
        outs + [((3 * half_cols, 3 * atoms), bf16), ((8, half_cols), f32)],
        [*[rows[slot] for slot in order[:-1]], blocks], "early_tile", [moment], 32, work,
    )
    kept = call(
        last_kernel, outs, [rows[order[-1]], side, norm, *kept], "last_tile",
        [pltpu.VMEM((3 * frames, 3 * half_cols), f32)], 32, work << 8, {3: 0, 4: 1, 5: 2},
    )
    parts = call(
        functools.partial(second_kernel, frames, nv), [((frames, LANES), f32)] * n_col,
        [*kept, blocks, other], "second_tile", [moment, tile], 32, work,
    )
    shares = [parts[0]] + [
        exchange(parts[order.index(mask)], "col", mask, n_col) for mask in range(n_col - 1, 0, -1)
    ]
    (result,) = call(functools.partial(finish_kernel, nv), [((frames, nv), f32)], shares, "sum_divide")
    return result.T


def solution(mesh):
    return jax.shard_map(
        functools.partial(per_device, mesh.shape["row"], mesh.shape["col"]),
        mesh=mesh,
        in_specs=(
            P(None, ("row", "col"), None),
            P(None, ("col", "row"), None),
            P(None, ("col", "row")),
        ),
        out_specs=P(None, ("row", "col")),
        check_vma=False,
    )
```

```python
import functools

import jax
import jax.numpy as jnp
from jax import lax
from jax.experimental import pallas as pl
from jax.experimental.pallas import tpu as pltpu
from jax.sharding import PartitionSpec as P

NEWTON = 8
BAND = 2.0
LANES = 128
VM = pl.BlockSpec(memory_space=pltpu.VMEM)
NT = (((1,), (1,)), ((), ()))


def centre(frames):
    return frames - jnp.mean(frames, axis=-1, keepdims=True)


def split(x):
    high = x.astype(jnp.bfloat16)
    low = (x - high.astype(jnp.float32)).astype(jnp.bfloat16)
    return high, low


def copy_kernel(in_ref, out_ref):
    out_ref[...] = in_ref[...]


def pack_kernel(frames, nv, in_ref, out_ref):
    used = in_ref.shape[0] - frames
    groups = in_ref.shape[1] // nv
    step = frames // groups
    out_ref[0:used, :] = in_ref[0:used, :]
    out_ref[used:, :] = jnp.concatenate(
        [in_ref[used + group * step:used + (group + 1) * step, 0:nv] for group in range(groups)], axis=1
    )


def copy_kernel(in_ref, out_ref):
    out_ref[...] = in_ref[...]


def columns_kernel(n_blocks, *refs):
    for at in range(n_blocks):
        refs[-1][at] = refs[at][...]


def inverse(x):
    guess = pl.reciprocal(x, approx=True)
    return guess * (2.0 - x * guess)


def eigen_tile(m, half_norm, atoms):
    s00, s01, s02, s10, s11, s12, s20, s21, s22 = m
    coef_two = -2.0 * (
        s00 * s00 + s01 * s01 + s02 * s02 + s10 * s10 + s11 * s11 + s12 * s12 + s20 * s20 + s21 * s21 + s22 * s22
    )
    coef_one = 8.0 * (s00 * s12 * s21 + s11 * s20 * s02 + s22 * s01 * s10) - 8.0 * (
        s00 * s11 * s22 + s12 * s20 * s01 + s21 * s10 * s02
    )
    k00 = s00 + s11 + s22
    k11 = s00 - s11 - s22
    k22 = s11 - s00 - s22
    k33 = s22 - s00 - s11
    k01 = s12 - s21
    k02 = s20 - s02
    k03 = s01 - s10
    k12 = s01 + s10
    k13 = s20 + s02
    k23 = s12 + s21
    top0 = k00 * k11 - k01 * k01
    top1 = k00 * k12 - k01 * k02
    top2 = k00 * k13 - k01 * k03
    top3 = k01 * k12 - k11 * k02
    top4 = k01 * k13 - k11 * k03
    top5 = k02 * k13 - k12 * k03
    low0 = k02 * k13 - k03 * k12
    low1 = k02 * k23 - k03 * k22
    low2 = k02 * k33 - k03 * k23
    low3 = k12 * k23 - k13 * k22
    low4 = k12 * k33 - k13 * k23
    low5 = k22 * k33 - k23 * k23
    coef_zero = top0 * low5 - top1 * low4 + top2 * low3 + top3 * low2 - top4 * low1 + top5 * low0
    eigen = half_norm
    twice = coef_two + coef_two
    for _ in range(NEWTON):
        eigen_sq = eigen * eigen
        value = (eigen_sq + coef_two) * eigen_sq + coef_one * eigen + coef_zero
        slope = (4.0 * eigen_sq + twice) * eigen + coef_one
        eigen = eigen - value * inverse(slope)
    squared = jnp.maximum(2.0 * (half_norm - eigen) / atoms, 0.0)
    return jnp.exp(-squared / BAND)


def column_side(blocks_ref, frames):
    count, _, atoms = blocks_ref.shape
    cols = [
        centre(jnp.concatenate([blocks_ref[at, comp * frames:(comp + 1) * frames, :] for at in range(count)], axis=0))
        for comp in range(3)
    ]
    col_square = cols[0] * cols[0] + cols[1] * cols[1] + cols[2] * cols[2]
    norm = lax.dot_general(
        jnp.ones((8, atoms), jnp.float32), col_square, NT,
        precision=lax.Precision.HIGHEST, preferred_element_type=jnp.float32,
    )
    high, low = split(jnp.concatenate(cols, axis=0))
    return jnp.concatenate([high, high, low], axis=1), norm


def vector_side(blocks_ref, frames, nv):
    count, _, atoms = blocks_ref.shape
    groups = atoms // nv
    step = frames // groups
    lane = lax.broadcasted_iota(jnp.int32, (step, LANES), 1)
    parts = []
    for at in range(count):
        for group in range(groups):
            place = group * nv
            piece = blocks_ref[at, 3 * frames:, place // LANES * LANES:place // LANES * LANES + LANES]
            if place % LANES:
                piece = pltpu.roll(piece, LANES - place % LANES, 1)
            parts.append(jnp.where(lane < nv, piece, jnp.where(lane == nv, 1.0, 0.0)))
    high, low = split(jnp.concatenate(parts, axis=0))
    return [high, high, low]


def row_side(slots):
    rows = [centre(jnp.concatenate([ref[comp] for ref in slots], axis=0)) for comp in range(3)]
    square = jnp.sum(rows[0] * rows[0] + rows[1] * rows[1] + rows[2] * rows[2], axis=1, keepdims=True)
    high, low = split(jnp.concatenate(rows, axis=0))
    return jnp.concatenate([high, low, high], axis=1), jnp.broadcast_to(square, (square.shape[0], LANES))


def kernel_tile(rows, row_norm, side, norm, moment, tile):
    count = row_norm.shape[0]
    count_cols = norm.shape[1]
    atoms = side.shape[1] // 3
    moment[0:3 * count, :] = lax.dot_general(rows, side, NT, preferred_element_type=jnp.float32)
    for at in range(0, count, 8):
        m = [
            moment[a * count + at:a * count + at + 8, b * count_cols:(b + 1) * count_cols]
            for a in range(3) for b in range(3)
        ]
        half_norm = 0.5 * (row_norm[at:at + 8, 0:1] + norm[0:1, :])
        tile[at:at + 8, :] = eigen_tile(m, half_norm, atoms)


def early_kernel(n_early, *refs):
    slots, blocks_ref = refs[:n_early], refs[n_early]
    rows_ref, row_norm_ref, tile_ref, side_ref, norm_ref, moment = refs[n_early + 1:]
    frames = slots[0].shape[1]
    groups, count, _ = tile_ref.shape
    side, norm = column_side(blocks_ref, frames)
    side_ref[...] = side
    norm_ref[...] = norm
    for group in range(groups):
        own = slots[group * count // frames:(group + 1) * count // frames]
        used = len(own) * frames
        rows, row_norm = row_side(own)
        for comp in range(3):
            rows_ref[group, comp * count:comp * count + used, :] = rows[comp * used:(comp + 1) * used]
        row_norm_ref[group, 0:used, :] = row_norm
        kernel_tile(rows, row_norm, side, norm, moment, tile_ref.at[group, 0:used])


def last_kernel(row_ref, side_ref, norm_ref, *refs):
    rows_ref, row_norm_ref, tile_ref, moment = refs[3:]
    frames = row_ref.shape[1]
    groups, count, _ = tile_ref.shape
    rows, row_norm = row_side([row_ref])
    for comp in range(3):
        rows_ref[groups - 1, (comp + 1) * count - frames:(comp + 1) * count, :] = rows[comp * frames:(comp + 1) * frames]
    row_norm_ref[groups - 1, count - frames:, :] = row_norm
    kernel_tile(rows, row_norm, side_ref[...], norm_ref[...], moment, tile_ref.at[groups - 1, count - frames:count])


def second_kernel(frames, nv, rows_ref, row_norm_ref, tile_ref, own_ref, blocks_ref, *refs):
    out_refs, moment, other_tile = refs[:-2], refs[-2], refs[-1]
    groups, count, _ = tile_ref.shape
    side, norm = column_side(blocks_ref, frames)
    vecs = jnp.concatenate(vector_side(own_ref, frames, nv) + vector_side(blocks_ref, frames, nv), axis=0)
    for group in range(groups):
        kernel_tile(rows_ref[group], row_norm_ref[group], side, norm, moment, other_tile)
        high, low = split(tile_ref[group])
        other_high, other_low = split(other_tile[...])
        total = jnp.dot(
            jnp.concatenate([high, low, high, other_high, other_low, other_high], axis=1), vecs,
            preferred_element_type=jnp.float32,
        )
        for at in range(count // frames):
            out_refs[group * count // frames + at][...] = total[at * frames:(at + 1) * frames, :]


def finish_kernel(nv, *refs):
    total = refs[0][...]
    for ref in refs[1:-1]:
        total = total + ref[...]
    refs[-1][...] = total[:, 0:nv] / total[:, nv:nv + 1]


def exchange(x, axis, mask, count):
    return lax.ppermute(x, axis, [(at, at ^ mask) for at in range(count)])


def call(kernel, outs, ins, name, scratch=(), megabytes=8, flops=0, aliases=None):
    out_shape = [jax.ShapeDtypeStruct(*out) for out in outs]
    moved = sum(x.size * 4 for x in ins)
    return pl.pallas_call(
        kernel,
        out_shape=out_shape,
        in_specs=[VM] * len(ins),
        out_specs=[VM] * len(outs),
        scratch_shapes=list(scratch),
        input_output_aliases=aliases or {},
        compiler_params=pltpu.CompilerParams(vmem_limit_bytes=megabytes * 1024 * 1024),
        cost_estimate=pl.CostEstimate(flops=flops, bytes_accessed=moved, transcendentals=0),
        name=name,
    )(*ins)


def per_device(n_row, n_col, row_frames, col_frames, vectors):
    comps, frames, atoms = row_frames.shape
    nv = vectors.shape[0]
    f32, bf16 = jnp.float32, jnp.bfloat16
    row_masks = [n_col >> at for at in range(1, n_col.bit_length())]
    col_masks = [1 << at for at in range(1, n_row.bit_length() - 1)]

    packed_shape = (comps * frames + frames * nv // atoms, atoms)
    both = jnp.concatenate(
        [col_frames.reshape(comps * frames, atoms), jnp.pad(vectors.T, ((0, 0), (0, atoms - nv)))], axis=0
    )
    (packed,) = call(functools.partial(pack_kernel, frames, nv), [(packed_shape, f32)], [both], "pack")
    order = [0]
    rows = {0: row_frames}
    for mask in row_masks:
        for slot in list(order):
            got = exchange(rows[slot], "col", mask, n_col)
            if not slot and mask == row_masks[0]:
                (got,) = call(copy_kernel, [(got.shape, f32)], [got], "far_rows", flops=10 << 30)
            rows[slot ^ mask] = got
            order.append(slot ^ mask)
    col_order = [0]
    for mask in col_masks:
        col_order = col_order + [slot ^ mask for slot in col_order]
    cols = [packed] + [exchange(packed, "row", mask, n_row) for mask in col_order[1:]]
    (blocks,) = call(
        functools.partial(columns_kernel, len(cols)), [((len(cols), *packed_shape), f32)],
        [*cols, rows[row_masks[0]]], "columns", flops=10 << 30,
    )
    other = exchange(blocks, "row", 1, n_row)

    half_cols = n_row // 2 * frames
    count = min(n_col, max(1, LANES // frames)) * frames
    groups = n_col * frames // count
    moment = pltpu.VMEM((3 * count, 3 * half_cols), f32)
    tile = pltpu.VMEM((count, half_cols), f32)
    work = 2 * 3 * n_col * frames * 3 * half_cols * 3 * atoms
    outs = [
        ((groups, 3 * count, 3 * atoms), bf16), ((groups, count, LANES), f32), ((groups, count, half_cols), f32),
    ]
    *kept, side, norm = call(
        functools.partial(early_kernel, n_col - 1),
        outs + [((3 * half_cols, 3 * atoms), bf16), ((8, half_cols), f32)],
        [*[rows[slot] for slot in order[:-1]], blocks], "early_tile", [moment], 32, work,
    )
    kept = call(
        last_kernel, outs, [rows[order[-1]], side, norm, *kept], "last_tile",
        [pltpu.VMEM((3 * frames, 3 * half_cols), f32)], 32, work << 8, {3: 0, 4: 1, 5: 2},
    )
    parts = call(
        functools.partial(second_kernel, frames, nv), [((frames, LANES), f32)] * n_col,
        [*kept, blocks, other], "second_tile", [moment, tile], 32, work,
    )
    shares = [parts[0]] + [
        exchange(parts[order.index(mask)], "col", mask, n_col) for mask in range(n_col - 1, 0, -1)
    ]
    (result,) = call(functools.partial(finish_kernel, nv), [((frames, nv), f32)], shares, "sum_divide")
    return result.T


def solution(mesh):
    return jax.shard_map(
        functools.partial(per_device, mesh.shape["row"], mesh.shape["col"]),
        mesh=mesh,
        in_specs=(
            P(None, ("row", "col"), None),
            P(None, ("col", "row"), None),
            P(None, ("col", "row")),
        ),
        out_specs=P(None, ("row", "col")),
        check_vma=False,
    )
```

```python
import functools

import jax
import jax.numpy as jnp
from jax import lax
from jax.experimental import pallas as pl
from jax.experimental.pallas import tpu as pltpu
from jax.sharding import PartitionSpec as P

NEWTON = 8
BAND = 2.0
LANES = 128
CHUNK = 16
VM = pl.BlockSpec(memory_space=pltpu.VMEM)
NT = (((1,), (1,)), ((), ()))


def centre(frames):
    return frames - jnp.mean(frames, axis=-1, keepdims=True)


def split(x):
    high = x.astype(jnp.bfloat16)
    low = (x - high.astype(jnp.float32)).astype(jnp.bfloat16)
    return high, low


def copy_kernel(in_ref, out_ref):
    out_ref[...] = in_ref[...]


def pack_kernel(frames, nv, in_ref, out_ref):
    used = in_ref.shape[0] - frames
    groups = in_ref.shape[1] // nv
    step = frames // groups
    out_ref[0:used, :] = in_ref[0:used, :]
    out_ref[used:, :] = jnp.concatenate(
        [in_ref[used + group * step:used + (group + 1) * step, 0:nv] for group in range(groups)], axis=1
    )


def copy_kernel(in_ref, out_ref):
    out_ref[...] = in_ref[...]


def columns_kernel(n_blocks, *refs):
    for at in range(n_blocks):
        refs[-1][at] = refs[at][...]


def inverse(x):
    guess = pl.reciprocal(x, approx=True)
    return guess * (2.0 - x * guess)


def eigen_tile(m, half_norm, atoms):
    s00, s01, s02, s10, s11, s12, s20, s21, s22 = m
    coef_two = -2.0 * (
        s00 * s00 + s01 * s01 + s02 * s02 + s10 * s10 + s11 * s11 + s12 * s12 + s20 * s20 + s21 * s21 + s22 * s22
    )
    coef_one = 8.0 * (s00 * s12 * s21 + s11 * s20 * s02 + s22 * s01 * s10) - 8.0 * (
        s00 * s11 * s22 + s12 * s20 * s01 + s21 * s10 * s02
    )
    k00 = s00 + s11 + s22
    k11 = s00 - s11 - s22
    k22 = s11 - s00 - s22
    k33 = s22 - s00 - s11
    k01 = s12 - s21
    k02 = s20 - s02
    k03 = s01 - s10
    k12 = s01 + s10
    k13 = s20 + s02
    k23 = s12 + s21
    top0 = k00 * k11 - k01 * k01
    top1 = k00 * k12 - k01 * k02
    top2 = k00 * k13 - k01 * k03
    top3 = k01 * k12 - k11 * k02
    top4 = k01 * k13 - k11 * k03
    top5 = k02 * k13 - k12 * k03
    low0 = k02 * k13 - k03 * k12
    low1 = k02 * k23 - k03 * k22
    low2 = k02 * k33 - k03 * k23
    low3 = k12 * k23 - k13 * k22
    low4 = k12 * k33 - k13 * k23
    low5 = k22 * k33 - k23 * k23
    coef_zero = top0 * low5 - top1 * low4 + top2 * low3 + top3 * low2 - top4 * low1 + top5 * low0
    eigen = half_norm
    twice = coef_two + coef_two
    for _ in range(NEWTON):
        eigen_sq = eigen * eigen
        value = (eigen_sq + coef_two) * eigen_sq + coef_one * eigen + coef_zero
        slope = (4.0 * eigen_sq + twice) * eigen + coef_one
        eigen = eigen - value * inverse(slope)
    squared = jnp.maximum(2.0 * (half_norm - eigen) / atoms, 0.0)
    return jnp.exp(-squared / BAND)


def column_side(blocks_ref, frames):
    count, _, atoms = blocks_ref.shape
    cols = [
        centre(jnp.concatenate([blocks_ref[at, comp * frames:(comp + 1) * frames, :] for at in range(count)], axis=0))
        for comp in range(3)
    ]
    col_square = cols[0] * cols[0] + cols[1] * cols[1] + cols[2] * cols[2]
    norm = lax.dot_general(
        jnp.ones((8, atoms), jnp.float32), col_square, NT,
        precision=lax.Precision.HIGHEST, preferred_element_type=jnp.float32,
    )
    high, low = split(jnp.concatenate(cols, axis=0))
    return jnp.concatenate([high, high, low], axis=1), norm


def vector_side(blocks_ref, frames, nv):
    count, _, atoms = blocks_ref.shape
    groups = atoms // nv
    step = frames // groups
    lane = lax.broadcasted_iota(jnp.int32, (step, LANES), 1)
    parts = []
    for at in range(count):
        for group in range(groups):
            place = group * nv
            piece = blocks_ref[at, 3 * frames:, place // LANES * LANES:place // LANES * LANES + LANES]
            if place % LANES:
                piece = pltpu.roll(piece, LANES - place % LANES, 1)
            parts.append(jnp.where(lane < nv, piece, jnp.where(lane == nv, 1.0, 0.0)))
    high, low = split(jnp.concatenate(parts, axis=0))
    return [high, high, low]


def row_side(slots):
    rows = [centre(jnp.concatenate([ref[comp] for ref in slots], axis=0)) for comp in range(3)]
    square = jnp.sum(rows[0] * rows[0] + rows[1] * rows[1] + rows[2] * rows[2], axis=1, keepdims=True)
    high, low = split(jnp.concatenate(rows, axis=0))
    return jnp.concatenate([high, low, high], axis=1), jnp.broadcast_to(square, (square.shape[0], LANES))


def kernel_tile(rows, row_norm, side, norm, moment, tile):
    count = row_norm.shape[0]
    count_cols = norm.shape[1]
    atoms = side.shape[1] // 3
    moment[0:3 * count, :] = lax.dot_general(rows, side, NT, preferred_element_type=jnp.float32)
    for at in range(0, count, CHUNK):
        m = [
            moment[a * count + at:a * count + at + CHUNK, b * count_cols:(b + 1) * count_cols]
            for a in range(3) for b in range(3)
        ]
        half_norm = 0.5 * (row_norm[at:at + CHUNK, 0:1] + norm[0:1, :])
        tile[at:at + CHUNK, :] = eigen_tile(m, half_norm, atoms)


def early_kernel(n_early, *refs):
    slots, blocks_ref = refs[:n_early], refs[n_early]
    rows_ref, row_norm_ref, tile_ref, side_ref, norm_ref, moment = refs[n_early + 1:]
    frames = slots[0].shape[1]
    groups, count, _ = tile_ref.shape
    side, norm = column_side(blocks_ref, frames)
    side_ref[...] = side
    norm_ref[...] = norm
    for group in range(groups):
        own = slots[group * count // frames:(group + 1) * count // frames]
        used = len(own) * frames
        rows, row_norm = row_side(own)
        for comp in range(3):
            rows_ref[group, comp * count:comp * count + used, :] = rows[comp * used:(comp + 1) * used]
        row_norm_ref[group, 0:used, :] = row_norm
        kernel_tile(rows, row_norm, side, norm, moment, tile_ref.at[group, 0:used])


def last_kernel(row_ref, side_ref, norm_ref, *refs):
    rows_ref, row_norm_ref, tile_ref, moment = refs[3:]
    frames = row_ref.shape[1]
    groups, count, _ = tile_ref.shape
    rows, row_norm = row_side([row_ref])
    for comp in range(3):
        rows_ref[groups - 1, (comp + 1) * count - frames:(comp + 1) * count, :] = rows[comp * frames:(comp + 1) * frames]
    row_norm_ref[groups - 1, count - frames:, :] = row_norm
    kernel_tile(rows, row_norm, side_ref[...], norm_ref[...], moment, tile_ref.at[groups - 1, count - frames:count])


def second_kernel(frames, nv, rows_ref, row_norm_ref, tile_ref, own_ref, blocks_ref, *refs):
    out_refs, moment, other_tile = refs[:-2], refs[-2], refs[-1]
    groups, count, _ = tile_ref.shape
    side, norm = column_side(blocks_ref, frames)
    vecs = jnp.concatenate(vector_side(own_ref, frames, nv) + vector_side(blocks_ref, frames, nv), axis=0)
    for group in range(groups):
        kernel_tile(rows_ref[group], row_norm_ref[group], side, norm, moment, other_tile)
        high, low = split(tile_ref[group])
        other_high, other_low = split(other_tile[...])
        total = jnp.dot(
            jnp.concatenate([high, low, high, other_high, other_low, other_high], axis=1), vecs,
            preferred_element_type=jnp.float32,
        )
        for at in range(count // frames):
            out_refs[group * count // frames + at][...] = total[at * frames:(at + 1) * frames, :]


def finish_kernel(nv, *refs):
    total = refs[0][...]
    for ref in refs[1:-1]:
        total = total + ref[...]
    refs[-1][...] = total[:, 0:nv] / total[:, nv:nv + 1]


def exchange(x, axis, mask, count):
    return lax.ppermute(x, axis, [(at, at ^ mask) for at in range(count)])


def call(kernel, outs, ins, name, scratch=(), megabytes=8, flops=0, aliases=None):
    out_shape = [jax.ShapeDtypeStruct(*out) for out in outs]
    moved = sum(x.size * 4 for x in ins)
    return pl.pallas_call(
        kernel,
        out_shape=out_shape,
        in_specs=[VM] * len(ins),
        out_specs=[VM] * len(outs),
        scratch_shapes=list(scratch),
        input_output_aliases=aliases or {},
        compiler_params=pltpu.CompilerParams(vmem_limit_bytes=megabytes * 1024 * 1024),
        cost_estimate=pl.CostEstimate(flops=flops, bytes_accessed=moved, transcendentals=0),
        name=name,
    )(*ins)


def per_device(n_row, n_col, row_frames, col_frames, vectors):
    comps, frames, atoms = row_frames.shape
    nv = vectors.shape[0]
    f32, bf16 = jnp.float32, jnp.bfloat16
    row_masks = [n_col >> at for at in range(1, n_col.bit_length())]
    col_masks = [1 << at for at in range(1, n_row.bit_length() - 1)]

    packed_shape = (comps * frames + frames * nv // atoms, atoms)
    both = jnp.concatenate(
        [col_frames.reshape(comps * frames, atoms), jnp.pad(vectors.T, ((0, 0), (0, atoms - nv)))], axis=0
    )
    (packed,) = call(functools.partial(pack_kernel, frames, nv), [(packed_shape, f32)], [both], "pack")
    order = [0]
    rows = {0: row_frames}
    for mask in row_masks:
        for slot in list(order):
            got = exchange(rows[slot], "col", mask, n_col)
            if not slot and mask == row_masks[0]:
                (got,) = call(copy_kernel, [(got.shape, f32)], [got], "far_rows", flops=10 << 30)
            rows[slot ^ mask] = got
            order.append(slot ^ mask)
    col_order = [0]
    for mask in col_masks:
        col_order = col_order + [slot ^ mask for slot in col_order]
    cols = [packed] + [exchange(packed, "row", mask, n_row) for mask in col_order[1:]]
    (blocks,) = call(
        functools.partial(columns_kernel, len(cols)), [((len(cols), *packed_shape), f32)],
        [*cols, rows[row_masks[0]]], "columns", flops=10 << 30,
    )
    other = exchange(blocks, "row", 1, n_row)

    half_cols = n_row // 2 * frames
    count = min(n_col, max(1, LANES // frames)) * frames
    groups = n_col * frames // count
    moment = pltpu.VMEM((3 * count, 3 * half_cols), f32)
    tile = pltpu.VMEM((count, half_cols), f32)
    work = 2 * 3 * n_col * frames * 3 * half_cols * 3 * atoms
    outs = [
        ((groups, 3 * count, 3 * atoms), bf16), ((groups, count, LANES), f32), ((groups, count, half_cols), f32),
    ]
    *kept, side, norm = call(
        functools.partial(early_kernel, n_col - 1),
        outs + [((3 * half_cols, 3 * atoms), bf16), ((8, half_cols), f32)],
        [*[rows[slot] for slot in order[:-1]], blocks], "early_tile", [moment], 32, work,
    )
    kept = call(
        last_kernel, outs, [rows[order[-1]], side, norm, *kept], "last_tile",
        [pltpu.VMEM((3 * frames, 3 * half_cols), f32)], 32, work << 8, {3: 0, 4: 1, 5: 2},
    )
    parts = call(
        functools.partial(second_kernel, frames, nv), [((frames, LANES), f32)] * n_col,
        [*kept, blocks, other], "second_tile", [moment, tile], 32, work,
    )
    shares = [parts[0]] + [
        exchange(parts[order.index(mask)], "col", mask, n_col) for mask in range(n_col - 1, 0, -1)
    ]
    (result,) = call(functools.partial(finish_kernel, nv), [((frames, nv), f32)], shares, "sum_divide")
    return result.T


def solution(mesh):
    return jax.shard_map(
        functools.partial(per_device, mesh.shape["row"], mesh.shape["col"]),
        mesh=mesh,
        in_specs=(
            P(None, ("row", "col"), None),
            P(None, ("col", "row"), None),
            P(None, ("col", "row")),
        ),
        out_specs=P(None, ("row", "col")),
        check_vma=False,
    )
```

```python
import functools

import jax
import jax.numpy as jnp
from jax import lax
from jax.experimental import pallas as pl
from jax.experimental.pallas import tpu as pltpu
from jax.sharding import PartitionSpec as P

NEWTON = 8
BAND = 2.0
LANES = 128
VM = pl.BlockSpec(memory_space=pltpu.VMEM)
NT = (((1,), (1,)), ((), ()))


def centre(frames):
    return frames - jnp.mean(frames, axis=-1, keepdims=True)


def split(x):
    high = x.astype(jnp.bfloat16)
    low = (x - high.astype(jnp.float32)).astype(jnp.bfloat16)
    return high, low


def copy_kernel(in_ref, out_ref):
    out_ref[...] = in_ref[...]


def pack_kernel(frames, nv, in_ref, out_ref):
    used = in_ref.shape[0] - frames
    groups = in_ref.shape[1] // nv
    step = frames // groups
    out_ref[0:used, :] = in_ref[0:used, :]
    out_ref[used:, :] = jnp.concatenate(
        [in_ref[used + group * step:used + (group + 1) * step, 0:nv] for group in range(groups)], axis=1
    )


def copy_kernel(in_ref, out_ref):
    out_ref[...] = in_ref[...]


def columns_kernel(n_blocks, *refs):
    for at in range(n_blocks):
        refs[-1][at] = refs[at][...]


def inverse(x):
    guess = pl.reciprocal(x, approx=True)
    return guess * (2.0 - x * guess)


def eigen_tile(m, half_norm, atoms):
    s00, s01, s02, s10, s11, s12, s20, s21, s22 = m
    coef_two = -2.0 * (
        s00 * s00 + s01 * s01 + s02 * s02 + s10 * s10 + s11 * s11 + s12 * s12 + s20 * s20 + s21 * s21 + s22 * s22
    )
    coef_one = 8.0 * (s00 * s12 * s21 + s11 * s20 * s02 + s22 * s01 * s10) - 8.0 * (
        s00 * s11 * s22 + s12 * s20 * s01 + s21 * s10 * s02
    )
    k00 = s00 + s11 + s22
    k11 = s00 - s11 - s22
    k22 = s11 - s00 - s22
    k33 = s22 - s00 - s11
    k01 = s12 - s21
    k02 = s20 - s02
    k03 = s01 - s10
    k12 = s01 + s10
    k13 = s20 + s02
    k23 = s12 + s21
    top0 = k00 * k11 - k01 * k01
    top1 = k00 * k12 - k01 * k02
    top2 = k00 * k13 - k01 * k03
    top3 = k01 * k12 - k11 * k02
    top4 = k01 * k13 - k11 * k03
    top5 = k02 * k13 - k12 * k03
    low0 = k02 * k13 - k03 * k12
    low1 = k02 * k23 - k03 * k22
    low2 = k02 * k33 - k03 * k23
    low3 = k12 * k23 - k13 * k22
    low4 = k12 * k33 - k13 * k23
    low5 = k22 * k33 - k23 * k23
    coef_zero = top0 * low5 - top1 * low4 + top2 * low3 + top3 * low2 - top4 * low1 + top5 * low0
    eigen = half_norm
    twice = coef_two + coef_two
    for _ in range(NEWTON):
        eigen_sq = eigen * eigen
        value = (eigen_sq + coef_two) * eigen_sq + coef_one * eigen + coef_zero
        slope = (4.0 * eigen_sq + twice) * eigen + coef_one
        eigen = eigen - value * inverse(slope)
    squared = jnp.maximum(2.0 * (half_norm - eigen) / atoms, 0.0)
    return jnp.exp(-squared / BAND)


def column_side(blocks_ref, frames):
    count, _, atoms = blocks_ref.shape
    cols = [
        centre(jnp.concatenate([blocks_ref[at, comp * frames:(comp + 1) * frames, :] for at in range(count)], axis=0))
        for comp in range(3)
    ]
    col_square = cols[0] * cols[0] + cols[1] * cols[1] + cols[2] * cols[2]
    norm = lax.dot_general(
        jnp.ones((8, atoms), jnp.float32), col_square, NT,
        precision=lax.Precision.HIGHEST, preferred_element_type=jnp.float32,
    )
    high, low = split(jnp.concatenate(cols, axis=0))
    return jnp.concatenate([high, high, low], axis=1), norm


def vector_side(blocks_ref, frames, nv):
    count, _, atoms = blocks_ref.shape
    groups = atoms // nv
    step = frames // groups
    lane = lax.broadcasted_iota(jnp.int32, (step, LANES), 1)
    parts = []
    for at in range(count):
        for group in range(groups):
            place = group * nv
            piece = blocks_ref[at, 3 * frames:, place // LANES * LANES:place // LANES * LANES + LANES]
            if place % LANES:
                piece = pltpu.roll(piece, LANES - place % LANES, 1)
            parts.append(jnp.where(lane < nv, piece, jnp.where(lane == nv, 1.0, 0.0)))
    high, low = split(jnp.concatenate(parts, axis=0))
    return [high, high, low]


def row_side(slots):
    rows = [centre(jnp.concatenate([ref[comp] for ref in slots], axis=0)) for comp in range(3)]
    square = jnp.sum(rows[0] * rows[0] + rows[1] * rows[1] + rows[2] * rows[2], axis=1, keepdims=True)
    high, low = split(jnp.concatenate(rows, axis=0))
    return jnp.concatenate([high, low, high], axis=1), jnp.broadcast_to(square, (square.shape[0], LANES))


def kernel_tile(rows, row_norm, side, norm, moment, tile):
    count = row_norm.shape[0]
    count_cols = norm.shape[1]
    atoms = side.shape[1] // 3
    moment[0:3 * count, :] = lax.dot_general(rows, side, NT, preferred_element_type=jnp.float32)
    for at in range(0, count, 8):
        m = [
            moment[a * count + at:a * count + at + 8, b * count_cols:(b + 1) * count_cols]
            for a in range(3) for b in range(3)
        ]
        half_norm = 0.5 * (row_norm[at:at + 8, 0:1] + norm[0:1, :])
        tile[at:at + 8, :] = eigen_tile(m, half_norm, atoms)


def early_kernel(n_early, nv, *refs):
    slots, blocks_ref = refs[:n_early], refs[n_early]
    rows_ref, row_norm_ref, tile_ref, side_ref, norm_ref, vec_ref, moment = refs[n_early + 1:]
    frames = slots[0].shape[1]
    groups, count, _ = tile_ref.shape
    side, norm = column_side(blocks_ref, frames)
    side_ref[...] = side
    norm_ref[...] = norm
    vec_ref[...] = jnp.concatenate(vector_side(blocks_ref, frames, nv), axis=0)
    for group in range(groups):
        own = slots[group * count // frames:(group + 1) * count // frames]
        used = len(own) * frames
        rows, row_norm = row_side(own)
        for comp in range(3):
            rows_ref[group, comp * count:comp * count + used, :] = rows[comp * used:(comp + 1) * used]
        row_norm_ref[group, 0:used, :] = row_norm
        kernel_tile(rows, row_norm, side, norm, moment, tile_ref.at[group, 0:used])


def last_kernel(row_ref, side_ref, norm_ref, *refs):
    rows_ref, row_norm_ref, tile_ref, moment = refs[3:]
    frames = row_ref.shape[1]
    groups, count, _ = tile_ref.shape
    rows, row_norm = row_side([row_ref])
    for comp in range(3):
        rows_ref[groups - 1, (comp + 1) * count - frames:(comp + 1) * count, :] = rows[comp * frames:(comp + 1) * frames]
    row_norm_ref[groups - 1, count - frames:, :] = row_norm
    kernel_tile(rows, row_norm, side_ref[...], norm_ref[...], moment, tile_ref.at[groups - 1, count - frames:count])


def second_kernel(frames, nv, rows_ref, row_norm_ref, tile_ref, vec_ref, blocks_ref, *refs):
    out_refs, moment, other_tile = refs[:-2], refs[-2], refs[-1]
    groups, count, _ = tile_ref.shape
    side, norm = column_side(blocks_ref, frames)
    vecs = jnp.concatenate([vec_ref[...]] + vector_side(blocks_ref, frames, nv), axis=0)
    for group in range(groups):
        kernel_tile(rows_ref[group], row_norm_ref[group], side, norm, moment, other_tile)
        high, low = split(tile_ref[group])
        other_high, other_low = split(other_tile[...])
        total = jnp.dot(
            jnp.concatenate([high, low, high, other_high, other_low, other_high], axis=1), vecs,
            preferred_element_type=jnp.float32,
        )
        for at in range(count // frames):
            out_refs[group * count // frames + at][...] = total[at * frames:(at + 1) * frames, :]


def finish_kernel(nv, *refs):
    total = refs[0][...]
    for ref in refs[1:-1]:
        total = total + ref[...]
    refs[-1][...] = total[:, 0:nv] / total[:, nv:nv + 1]


def exchange(x, axis, mask, count):
    return lax.ppermute(x, axis, [(at, at ^ mask) for at in range(count)])


def call(kernel, outs, ins, name, scratch=(), megabytes=8, flops=0, aliases=None):
    out_shape = [jax.ShapeDtypeStruct(*out) for out in outs]
    moved = sum(x.size * 4 for x in ins)
    return pl.pallas_call(
        kernel,
        out_shape=out_shape,
        in_specs=[VM] * len(ins),
        out_specs=[VM] * len(outs),
        scratch_shapes=list(scratch),
        input_output_aliases=aliases or {},
        compiler_params=pltpu.CompilerParams(vmem_limit_bytes=megabytes * 1024 * 1024),
        cost_estimate=pl.CostEstimate(flops=flops, bytes_accessed=moved, transcendentals=0),
        name=name,
    )(*ins)


def per_device(n_row, n_col, row_frames, col_frames, vectors):
    comps, frames, atoms = row_frames.shape
    nv = vectors.shape[0]
    f32, bf16 = jnp.float32, jnp.bfloat16
    row_masks = [n_col >> at for at in range(1, n_col.bit_length())]
    col_masks = [1 << at for at in range(1, n_row.bit_length() - 1)]

    packed_shape = (comps * frames + frames * nv // atoms, atoms)
    both = jnp.concatenate(
        [col_frames.reshape(comps * frames, atoms), jnp.pad(vectors.T, ((0, 0), (0, atoms - nv)))], axis=0
    )
    (packed,) = call(functools.partial(pack_kernel, frames, nv), [(packed_shape, f32)], [both], "pack")
    order = [0]
    rows = {0: row_frames}
    for mask in row_masks:
        for slot in list(order):
            got = exchange(rows[slot], "col", mask, n_col)
            if not slot and mask == row_masks[0]:
                (got,) = call(copy_kernel, [(got.shape, f32)], [got], "far_rows", flops=10 << 30)
            rows[slot ^ mask] = got
            order.append(slot ^ mask)
    col_order = [0]
    for mask in col_masks:
        col_order = col_order + [slot ^ mask for slot in col_order]
    cols = [packed] + [exchange(packed, "row", mask, n_row) for mask in col_order[1:]]
    (blocks,) = call(
        functools.partial(columns_kernel, len(cols)), [((len(cols), *packed_shape), f32)],
        [*cols, rows[row_masks[0]]], "columns", flops=10 << 30,
    )
    other = exchange(blocks, "row", 1, n_row)

    half_cols = n_row // 2 * frames
    count = min(n_col, max(1, LANES // frames)) * frames
    groups = n_col * frames // count
    moment = pltpu.VMEM((3 * count, 3 * half_cols), f32)
    tile = pltpu.VMEM((count, half_cols), f32)
    work = 2 * 3 * n_col * frames * 3 * half_cols * 3 * atoms
    outs = [
        ((groups, 3 * count, 3 * atoms), bf16), ((groups, count, LANES), f32), ((groups, count, half_cols), f32),
    ]
    *kept, side, norm, vec = call(
        functools.partial(early_kernel, n_col - 1, nv),
        outs + [((3 * half_cols, 3 * atoms), bf16), ((8, half_cols), f32), ((3 * half_cols, LANES), bf16)],
        [*[rows[slot] for slot in order[:-1]], blocks], "early_tile", [moment], 32, work,
    )
    kept = call(
        last_kernel, outs, [rows[order[-1]], side, norm, *kept], "last_tile",
        [pltpu.VMEM((3 * frames, 3 * half_cols), f32)], 32, work << 8, {3: 0, 4: 1, 5: 2},
    )
    parts = call(
        functools.partial(second_kernel, frames, nv), [((frames, LANES), f32)] * n_col,
        [*kept, vec, other], "second_tile", [moment, tile], 32, work,
    )
    shares = [parts[0]] + [
        exchange(parts[order.index(mask)], "col", mask, n_col) for mask in range(n_col - 1, 0, -1)
    ]
    (result,) = call(functools.partial(finish_kernel, nv), [((frames, nv), f32)], shares, "sum_divide")
    return result.T


def solution(mesh):
    return jax.shard_map(
        functools.partial(per_device, mesh.shape["row"], mesh.shape["col"]),
        mesh=mesh,
        in_specs=(
            P(None, ("row", "col"), None),
            P(None, ("col", "row"), None),
            P(None, ("col", "row")),
        ),
        out_specs=P(None, ("row", "col")),
        check_vma=False,
    )
```

```python
import functools

import jax
import jax.numpy as jnp
from jax import lax
from jax.experimental import pallas as pl
from jax.experimental.pallas import tpu as pltpu
from jax.sharding import PartitionSpec as P

NEWTON = 8
BAND = 2.0
LANES = 128
VM = pl.BlockSpec(memory_space=pltpu.VMEM)
NT = (((1,), (1,)), ((), ()))


def centre(frames):
    return frames - jnp.mean(frames, axis=-1, keepdims=True)


def split(x):
    high = x.astype(jnp.bfloat16)
    low = (x - high.astype(jnp.float32)).astype(jnp.bfloat16)
    return high, low


def copy_kernel(in_ref, out_ref):
    out_ref[...] = in_ref[...]


def pack_kernel(frames, nv, in_ref, out_ref):
    used = in_ref.shape[0] - frames
    groups = in_ref.shape[1] // nv
    step = frames // groups
    out_ref[0:used, :] = in_ref[0:used, :]
    out_ref[used:, :] = jnp.concatenate(
        [in_ref[used + group * step:used + (group + 1) * step, 0:nv] for group in range(groups)], axis=1
    )


def copy_kernel(in_ref, out_ref):
    out_ref[...] = in_ref[...]


def columns_kernel(n_blocks, *refs):
    for at in range(n_blocks):
        refs[-1][at] = refs[at][...]


def inverse(x):
    guess = pl.reciprocal(x, approx=True)
    return guess * (2.0 - x * guess)


def eigen_tile(m, half_norm, atoms):
    s00, s01, s02, s10, s11, s12, s20, s21, s22 = m
    coef_two = -2.0 * (
        s00 * s00 + s01 * s01 + s02 * s02 + s10 * s10 + s11 * s11 + s12 * s12 + s20 * s20 + s21 * s21 + s22 * s22
    )
    coef_one = 8.0 * (s00 * s12 * s21 + s11 * s20 * s02 + s22 * s01 * s10) - 8.0 * (
        s00 * s11 * s22 + s12 * s20 * s01 + s21 * s10 * s02
    )
    k00 = s00 + s11 + s22
    k11 = s00 - s11 - s22
    k22 = s11 - s00 - s22
    k33 = s22 - s00 - s11
    k01 = s12 - s21
    k02 = s20 - s02
    k03 = s01 - s10
    k12 = s01 + s10
    k13 = s20 + s02
    k23 = s12 + s21
    top0 = k00 * k11 - k01 * k01
    top1 = k00 * k12 - k01 * k02
    top2 = k00 * k13 - k01 * k03
    top3 = k01 * k12 - k11 * k02
    top4 = k01 * k13 - k11 * k03
    top5 = k02 * k13 - k12 * k03
    low0 = k02 * k13 - k03 * k12
    low1 = k02 * k23 - k03 * k22
    low2 = k02 * k33 - k03 * k23
    low3 = k12 * k23 - k13 * k22
    low4 = k12 * k33 - k13 * k23
    low5 = k22 * k33 - k23 * k23
    coef_zero = top0 * low5 - top1 * low4 + top2 * low3 + top3 * low2 - top4 * low1 + top5 * low0
    eigen = half_norm
    twice = coef_two + coef_two
    for _ in range(NEWTON):
        eigen_sq = eigen * eigen
        value = (eigen_sq + coef_two) * eigen_sq + coef_one * eigen + coef_zero
        slope = (4.0 * eigen_sq + twice) * eigen + coef_one
        eigen = eigen - value * inverse(slope)
    squared = jnp.maximum(2.0 * (half_norm - eigen) / atoms, 0.0)
    return jnp.exp(-squared / BAND)


def column_side(blocks_ref, frames):
    count, _, atoms = blocks_ref.shape
    cols = [
        centre(jnp.concatenate([blocks_ref[at, comp * frames:(comp + 1) * frames, :] for at in range(count)], axis=0))
        for comp in range(3)
    ]
    col_square = cols[0] * cols[0] + cols[1] * cols[1] + cols[2] * cols[2]
    high, low = split(col_square)
    rest = (col_square - high.astype(jnp.float32) - low.astype(jnp.float32)).astype(jnp.bfloat16)
    norm = lax.dot_general(
        jnp.ones((8, 3 * atoms), jnp.bfloat16), jnp.concatenate([high, low, rest], axis=1), NT,
        preferred_element_type=jnp.float32,
    )
    high, low = split(jnp.concatenate(cols, axis=0))
    return jnp.concatenate([high, high, low], axis=1), norm


def vector_side(blocks_ref, frames, nv):
    count, _, atoms = blocks_ref.shape
    groups = atoms // nv
    step = frames // groups
    lane = lax.broadcasted_iota(jnp.int32, (step, LANES), 1)
    parts = []
    for at in range(count):
        for group in range(groups):
            place = group * nv
            piece = blocks_ref[at, 3 * frames:, place // LANES * LANES:place // LANES * LANES + LANES]
            if place % LANES:
                piece = pltpu.roll(piece, LANES - place % LANES, 1)
            parts.append(jnp.where(lane < nv, piece, jnp.where(lane == nv, 1.0, 0.0)))
    high, low = split(jnp.concatenate(parts, axis=0))
    return [high, high, low]


def row_side(slots):
    rows = [centre(jnp.concatenate([ref[comp] for ref in slots], axis=0)) for comp in range(3)]
    square = jnp.sum(rows[0] * rows[0] + rows[1] * rows[1] + rows[2] * rows[2], axis=1, keepdims=True)
    high, low = split(jnp.concatenate(rows, axis=0))
    return jnp.concatenate([high, low, high], axis=1), jnp.broadcast_to(square, (square.shape[0], LANES))


def kernel_tile(rows, row_norm, side, norm, moment, tile):
    count = row_norm.shape[0]
    count_cols = norm.shape[1]
    atoms = side.shape[1] // 3
    moment[0:3 * count, :] = lax.dot_general(rows, side, NT, preferred_element_type=jnp.float32)
    for at in range(0, count, 8):
        m = [
            moment[a * count + at:a * count + at + 8, b * count_cols:(b + 1) * count_cols]
            for a in range(3) for b in range(3)
        ]
        half_norm = 0.5 * (row_norm[at:at + 8, 0:1] + norm[0:1, :])
        tile[at:at + 8, :] = eigen_tile(m, half_norm, atoms)


def early_kernel(n_early, nv, *refs):
    slots, blocks_ref = refs[:n_early], refs[n_early]
    rows_ref, row_norm_ref, tile_ref, side_ref, norm_ref, vec_ref, moment = refs[n_early + 1:]
    frames = slots[0].shape[1]
    groups, count, _ = tile_ref.shape
    side, norm = column_side(blocks_ref, frames)
    side_ref[...] = side
    norm_ref[...] = norm
    vec_ref[...] = jnp.concatenate(vector_side(blocks_ref, frames, nv), axis=0)
    for group in range(groups):
        own = slots[group * count // frames:(group + 1) * count // frames]
        used = len(own) * frames
        rows, row_norm = row_side(own)
        for comp in range(3):
            rows_ref[group, comp * count:comp * count + used, :] = rows[comp * used:(comp + 1) * used]
        row_norm_ref[group, 0:used, :] = row_norm
        kernel_tile(rows, row_norm, side, norm, moment, tile_ref.at[group, 0:used])


def last_kernel(row_ref, side_ref, norm_ref, *refs):
    rows_ref, row_norm_ref, tile_ref, moment = refs[3:]
    frames = row_ref.shape[1]
    groups, count, _ = tile_ref.shape
    rows, row_norm = row_side([row_ref])
    for comp in range(3):
        rows_ref[groups - 1, (comp + 1) * count - frames:(comp + 1) * count, :] = rows[comp * frames:(comp + 1) * frames]
    row_norm_ref[groups - 1, count - frames:, :] = row_norm
    kernel_tile(rows, row_norm, side_ref[...], norm_ref[...], moment, tile_ref.at[groups - 1, count - frames:count])


def second_kernel(frames, nv, rows_ref, row_norm_ref, tile_ref, vec_ref, blocks_ref, *refs):
    out_refs, moment, other_tile = refs[:-2], refs[-2], refs[-1]
    groups, count, _ = tile_ref.shape
    side, norm = column_side(blocks_ref, frames)
    vecs = jnp.concatenate([vec_ref[...]] + vector_side(blocks_ref, frames, nv), axis=0)
    for group in range(groups):
        kernel_tile(rows_ref[group], row_norm_ref[group], side, norm, moment, other_tile)
        high, low = split(tile_ref[group])
        other_high, other_low = split(other_tile[...])
        total = jnp.dot(
            jnp.concatenate([high, low, high, other_high, other_low, other_high], axis=1), vecs,
            preferred_element_type=jnp.float32,
        )
        for at in range(count // frames):
            out_refs[group * count // frames + at][...] = total[at * frames:(at + 1) * frames, :]


def finish_kernel(nv, *refs):
    total = refs[0][...]
    for ref in refs[1:-1]:
        total = total + ref[...]
    refs[-1][...] = total[:, 0:nv] / total[:, nv:nv + 1]


def exchange(x, axis, mask, count):
    return lax.ppermute(x, axis, [(at, at ^ mask) for at in range(count)])


def call(kernel, outs, ins, name, scratch=(), megabytes=8, flops=0, aliases=None):
    out_shape = [jax.ShapeDtypeStruct(*out) for out in outs]
    moved = sum(x.size * 4 for x in ins)
    return pl.pallas_call(
        kernel,
        out_shape=out_shape,
        in_specs=[VM] * len(ins),
        out_specs=[VM] * len(outs),
        scratch_shapes=list(scratch),
        input_output_aliases=aliases or {},
        compiler_params=pltpu.CompilerParams(vmem_limit_bytes=megabytes * 1024 * 1024),
        cost_estimate=pl.CostEstimate(flops=flops, bytes_accessed=moved, transcendentals=0),
        name=name,
    )(*ins)


def per_device(n_row, n_col, row_frames, col_frames, vectors):
    comps, frames, atoms = row_frames.shape
    nv = vectors.shape[0]
    f32, bf16 = jnp.float32, jnp.bfloat16
    row_masks = [n_col >> at for at in range(1, n_col.bit_length())]
    col_masks = [1 << at for at in range(1, n_row.bit_length() - 1)]

    packed_shape = (comps * frames + frames * nv // atoms, atoms)
    both = jnp.concatenate(
        [col_frames.reshape(comps * frames, atoms), jnp.pad(vectors.T, ((0, 0), (0, atoms - nv)))], axis=0
    )
    (packed,) = call(functools.partial(pack_kernel, frames, nv), [(packed_shape, f32)], [both], "pack")
    order = [0]
    rows = {0: row_frames}
    for mask in row_masks:
        for slot in list(order):
            got = exchange(rows[slot], "col", mask, n_col)
            if not slot and mask == row_masks[0]:
                (got,) = call(copy_kernel, [(got.shape, f32)], [got], "far_rows", flops=10 << 30)
            rows[slot ^ mask] = got
            order.append(slot ^ mask)
    col_order = [0]
    for mask in col_masks:
        col_order = col_order + [slot ^ mask for slot in col_order]
    cols = [packed] + [exchange(packed, "row", mask, n_row) for mask in col_order[1:]]
    (blocks,) = call(
        functools.partial(columns_kernel, len(cols)), [((len(cols), *packed_shape), f32)],
        [*cols, rows[row_masks[0]]], "columns", flops=10 << 30,
    )
    other = exchange(blocks, "row", 1, n_row)

    half_cols = n_row // 2 * frames
    count = min(n_col, max(1, LANES // frames)) * frames
    groups = n_col * frames // count
    moment = pltpu.VMEM((3 * count, 3 * half_cols), f32)
    tile = pltpu.VMEM((count, half_cols), f32)
    work = 2 * 3 * n_col * frames * 3 * half_cols * 3 * atoms
    outs = [
        ((groups, 3 * count, 3 * atoms), bf16), ((groups, count, LANES), f32), ((groups, count, half_cols), f32),
    ]
    *kept, side, norm, vec = call(
        functools.partial(early_kernel, n_col - 1, nv),
        outs + [((3 * half_cols, 3 * atoms), bf16), ((8, half_cols), f32), ((3 * half_cols, LANES), bf16)],
        [*[rows[slot] for slot in order[:-1]], blocks], "early_tile", [moment], 32, work,
    )
    kept = call(
        last_kernel, outs, [rows[order[-1]], side, norm, *kept], "last_tile",
        [pltpu.VMEM((3 * frames, 3 * half_cols), f32)], 32, work << 8, {3: 0, 4: 1, 5: 2},
    )
    parts = call(
        functools.partial(second_kernel, frames, nv), [((frames, LANES), f32)] * n_col,
        [*kept, vec, other], "second_tile", [moment, tile], 32, work,
    )
    shares = [parts[0]] + [
        exchange(parts[order.index(mask)], "col", mask, n_col) for mask in range(n_col - 1, 0, -1)
    ]
    (result,) = call(functools.partial(finish_kernel, nv), [((frames, nv), f32)], shares, "sum_divide")
    return result.T


def solution(mesh):
    return jax.shard_map(
        functools.partial(per_device, mesh.shape["row"], mesh.shape["col"]),
        mesh=mesh,
        in_specs=(
            P(None, ("row", "col"), None),
            P(None, ("col", "row"), None),
            P(None, ("col", "row")),
        ),
        out_specs=P(None, ("row", "col")),
        check_vma=False,
    )
```

```python
import functools

import jax
import jax.numpy as jnp
from jax import lax
from jax.experimental import pallas as pl
from jax.experimental.pallas import tpu as pltpu
from jax.sharding import PartitionSpec as P

NEWTON = 8
BAND = 2.0
LANES = 128
VM = pl.BlockSpec(memory_space=pltpu.VMEM)
NT = (((1,), (1,)), ((), ()))


def centre(frames):
    return frames - jnp.mean(frames, axis=-1, keepdims=True)


def split(x):
    high = x.astype(jnp.bfloat16)
    low = (x - high.astype(jnp.float32)).astype(jnp.bfloat16)
    return high, low


def copy_kernel(in_ref, out_ref):
    out_ref[...] = in_ref[...]


def pack_kernel(frames, nv, in_ref, out_ref):
    used = in_ref.shape[0] - frames
    groups = in_ref.shape[1] // nv
    step = frames // groups
    out_ref[0:used, :] = in_ref[0:used, :]
    out_ref[used:, :] = jnp.concatenate(
        [in_ref[used + group * step:used + (group + 1) * step, 0:nv] for group in range(groups)], axis=1
    )


def copy_kernel(in_ref, out_ref):
    out_ref[...] = in_ref[...]


def columns_kernel(n_blocks, *refs):
    for at in range(n_blocks):
        refs[-1][at] = refs[at][...]


def inverse(x):
    guess = pl.reciprocal(x, approx=True)
    return guess * (2.0 - x * guess)


def eigen_tile(m, half_norm, atoms):
    s00, s01, s02, s10, s11, s12, s20, s21, s22 = m
    coef_two = -2.0 * (
        s00 * s00 + s01 * s01 + s02 * s02 + s10 * s10 + s11 * s11 + s12 * s12 + s20 * s20 + s21 * s21 + s22 * s22
    )
    coef_one = -8.0 * (
        s00 * (s11 * s22 - s12 * s21) + s01 * (s12 * s20 - s10 * s22) + s02 * (s10 * s21 - s11 * s20)
    )
    k00 = s00 + s11 + s22
    k11 = s00 - s11 - s22
    k22 = s11 - s00 - s22
    k33 = s22 - s00 - s11
    k01 = s12 - s21
    k02 = s20 - s02
    k03 = s01 - s10
    k12 = s01 + s10
    k13 = s20 + s02
    k23 = s12 + s21
    top0 = k00 * k11 - k01 * k01
    top1 = k00 * k12 - k01 * k02
    top2 = k00 * k13 - k01 * k03
    top3 = k01 * k12 - k11 * k02
    top4 = k01 * k13 - k11 * k03
    top5 = k02 * k13 - k12 * k03
    low0 = k02 * k13 - k03 * k12
    low1 = k02 * k23 - k03 * k22
    low2 = k02 * k33 - k03 * k23
    low3 = k12 * k23 - k13 * k22
    low4 = k12 * k33 - k13 * k23
    low5 = k22 * k33 - k23 * k23
    coef_zero = top0 * low5 - top1 * low4 + top2 * low3 + top3 * low2 - top4 * low1 + top5 * low0
    eigen = half_norm
    twice = coef_two + coef_two
    for _ in range(NEWTON):
        eigen_sq = eigen * eigen
        value = (eigen_sq + coef_two) * eigen_sq + coef_one * eigen + coef_zero
        slope = (4.0 * eigen_sq + twice) * eigen + coef_one
        eigen = eigen - value * inverse(slope)
    squared = jnp.maximum(2.0 * (half_norm - eigen) / atoms, 0.0)
    return jnp.exp(-squared / BAND)


def column_side(blocks_ref, frames):
    count, _, atoms = blocks_ref.shape
    cols = [
        centre(jnp.concatenate([blocks_ref[at, comp * frames:(comp + 1) * frames, :] for at in range(count)], axis=0))
        for comp in range(3)
    ]
    col_square = cols[0] * cols[0] + cols[1] * cols[1] + cols[2] * cols[2]
    high, low = split(col_square)
    rest = (col_square - high.astype(jnp.float32) - low.astype(jnp.float32)).astype(jnp.bfloat16)
    norm = lax.dot_general(
        jnp.ones((8, 3 * atoms), jnp.bfloat16), jnp.concatenate([high, low, rest], axis=1), NT,
        preferred_element_type=jnp.float32,
    )
    high, low = split(jnp.concatenate(cols, axis=0))
    return jnp.concatenate([high, high, low], axis=1), norm


def vector_side(blocks_ref, frames, nv):
    count, _, atoms = blocks_ref.shape
    groups = atoms // nv
    step = frames // groups
    lane = lax.broadcasted_iota(jnp.int32, (step, LANES), 1)
    parts = []
    for at in range(count):
        for group in range(groups):
            place = group * nv
            piece = blocks_ref[at, 3 * frames:, place // LANES * LANES:place // LANES * LANES + LANES]
            if place % LANES:
                piece = pltpu.roll(piece, LANES - place % LANES, 1)
            parts.append(jnp.where(lane < nv, piece, jnp.where(lane == nv, 1.0, 0.0)))
    high, low = split(jnp.concatenate(parts, axis=0))
    return [high, high, low]


def row_side(slots):
    rows = [centre(jnp.concatenate([ref[comp] for ref in slots], axis=0)) for comp in range(3)]
    square = jnp.sum(rows[0] * rows[0] + rows[1] * rows[1] + rows[2] * rows[2], axis=1, keepdims=True)
    high, low = split(jnp.concatenate(rows, axis=0))
    return jnp.concatenate([high, low, high], axis=1), jnp.broadcast_to(square, (square.shape[0], LANES))


def kernel_tile(rows, row_norm, side, norm, moment, tile):
    count = row_norm.shape[0]
    count_cols = norm.shape[1]
    atoms = side.shape[1] // 3
    moment[0:3 * count, :] = lax.dot_general(rows, side, NT, preferred_element_type=jnp.float32)
    for at in range(0, count, 8):
        m = [
            moment[a * count + at:a * count + at + 8, b * count_cols:(b + 1) * count_cols]
            for a in range(3) for b in range(3)
        ]
        half_norm = 0.5 * (row_norm[at:at + 8, 0:1] + norm[0:1, :])
        tile[at:at + 8, :] = eigen_tile(m, half_norm, atoms)


def early_kernel(n_early, nv, *refs):
    slots, blocks_ref = refs[:n_early], refs[n_early]
    rows_ref, row_norm_ref, tile_ref, side_ref, norm_ref, vec_ref, moment = refs[n_early + 1:]
    frames = slots[0].shape[1]
    groups, count, _ = tile_ref.shape
    side, norm = column_side(blocks_ref, frames)
    side_ref[...] = side
    norm_ref[...] = norm
    vec_ref[...] = jnp.concatenate(vector_side(blocks_ref, frames, nv), axis=0)
    for group in range(groups):
        own = slots[group * count // frames:(group + 1) * count // frames]
        used = len(own) * frames
        rows, row_norm = row_side(own)
        for comp in range(3):
            rows_ref[group, comp * count:comp * count + used, :] = rows[comp * used:(comp + 1) * used]
        row_norm_ref[group, 0:used, :] = row_norm
        kernel_tile(rows, row_norm, side, norm, moment, tile_ref.at[group, 0:used])


def last_kernel(row_ref, side_ref, norm_ref, *refs):
    rows_ref, row_norm_ref, tile_ref, moment = refs[3:]
    frames = row_ref.shape[1]
    groups, count, _ = tile_ref.shape
    rows, row_norm = row_side([row_ref])
    for comp in range(3):
        rows_ref[groups - 1, (comp + 1) * count - frames:(comp + 1) * count, :] = rows[comp * frames:(comp + 1) * frames]
    row_norm_ref[groups - 1, count - frames:, :] = row_norm
    kernel_tile(rows, row_norm, side_ref[...], norm_ref[...], moment, tile_ref.at[groups - 1, count - frames:count])


def second_kernel(frames, nv, rows_ref, row_norm_ref, tile_ref, vec_ref, blocks_ref, *refs):
    out_refs, moment, other_tile = refs[:-2], refs[-2], refs[-1]
    groups, count, _ = tile_ref.shape
    side, norm = column_side(blocks_ref, frames)
    vecs = jnp.concatenate([vec_ref[...]] + vector_side(blocks_ref, frames, nv), axis=0)
    for group in range(groups):
        kernel_tile(rows_ref[group], row_norm_ref[group], side, norm, moment, other_tile)
        high, low = split(tile_ref[group])
        other_high, other_low = split(other_tile[...])
        total = jnp.dot(
            jnp.concatenate([high, low, high, other_high, other_low, other_high], axis=1), vecs,
            preferred_element_type=jnp.float32,
        )
        for at in range(count // frames):
            out_refs[group * count // frames + at][...] = total[at * frames:(at + 1) * frames, :]


def finish_kernel(nv, *refs):
    total = refs[0][...]
    for ref in refs[1:-1]:
        total = total + ref[...]
    refs[-1][...] = total[:, 0:nv] / total[:, nv:nv + 1]


def exchange(x, axis, mask, count):
    return lax.ppermute(x, axis, [(at, at ^ mask) for at in range(count)])


def call(kernel, outs, ins, name, scratch=(), megabytes=8, flops=0, aliases=None):
    out_shape = [jax.ShapeDtypeStruct(*out) for out in outs]
    moved = sum(x.size * 4 for x in ins)
    return pl.pallas_call(
        kernel,
        out_shape=out_shape,
        in_specs=[VM] * len(ins),
        out_specs=[VM] * len(outs),
        scratch_shapes=list(scratch),
        input_output_aliases=aliases or {},
        compiler_params=pltpu.CompilerParams(vmem_limit_bytes=megabytes * 1024 * 1024),
        cost_estimate=pl.CostEstimate(flops=flops, bytes_accessed=moved, transcendentals=0),
        name=name,
    )(*ins)


def per_device(n_row, n_col, row_frames, col_frames, vectors):
    comps, frames, atoms = row_frames.shape
    nv = vectors.shape[0]
    f32, bf16 = jnp.float32, jnp.bfloat16
    row_masks = [n_col >> at for at in range(1, n_col.bit_length())]
    col_masks = [1 << at for at in range(1, n_row.bit_length() - 1)]

    packed_shape = (comps * frames + frames * nv // atoms, atoms)
    both = jnp.concatenate(
        [col_frames.reshape(comps * frames, atoms), jnp.pad(vectors.T, ((0, 0), (0, atoms - nv)))], axis=0
    )
    (packed,) = call(functools.partial(pack_kernel, frames, nv), [(packed_shape, f32)], [both], "pack")
    order = [0]
    rows = {0: row_frames}
    for mask in row_masks:
        for slot in list(order):
            got = exchange(rows[slot], "col", mask, n_col)
            if not slot and mask == row_masks[0]:
                (got,) = call(copy_kernel, [(got.shape, f32)], [got], "far_rows", flops=10 << 30)
            rows[slot ^ mask] = got
            order.append(slot ^ mask)
    col_order = [0]
    for mask in col_masks:
        col_order = col_order + [slot ^ mask for slot in col_order]
    cols = [packed] + [exchange(packed, "row", mask, n_row) for mask in col_order[1:]]
    (blocks,) = call(
        functools.partial(columns_kernel, len(cols)), [((len(cols), *packed_shape), f32)],
        [*cols, rows[row_masks[0]]], "columns", flops=10 << 30,
    )
    other = exchange(blocks, "row", 1, n_row)

    half_cols = n_row // 2 * frames
    count = min(n_col, max(1, LANES // frames)) * frames
    groups = n_col * frames // count
    moment = pltpu.VMEM((3 * count, 3 * half_cols), f32)
    tile = pltpu.VMEM((count, half_cols), f32)
    work = 2 * 3 * n_col * frames * 3 * half_cols * 3 * atoms
    outs = [
        ((groups, 3 * count, 3 * atoms), bf16), ((groups, count, LANES), f32), ((groups, count, half_cols), f32),
    ]
    *kept, side, norm, vec = call(
        functools.partial(early_kernel, n_col - 1, nv),
        outs + [((3 * half_cols, 3 * atoms), bf16), ((8, half_cols), f32), ((3 * half_cols, LANES), bf16)],
        [*[rows[slot] for slot in order[:-1]], blocks], "early_tile", [moment], 32, work,
    )
    kept = call(
        last_kernel, outs, [rows[order[-1]], side, norm, *kept], "last_tile",
        [pltpu.VMEM((3 * frames, 3 * half_cols), f32)], 32, work << 8, {3: 0, 4: 1, 5: 2},
    )
    parts = call(
        functools.partial(second_kernel, frames, nv), [((frames, LANES), f32)] * n_col,
        [*kept, vec, other], "second_tile", [moment, tile], 32, work,
    )
    shares = [parts[0]] + [
        exchange(parts[order.index(mask)], "col", mask, n_col) for mask in range(n_col - 1, 0, -1)
    ]
    (result,) = call(functools.partial(finish_kernel, nv), [((frames, nv), f32)], shares, "sum_divide")
    return result.T


def solution(mesh):
    return jax.shard_map(
        functools.partial(per_device, mesh.shape["row"], mesh.shape["col"]),
        mesh=mesh,
        in_specs=(
            P(None, ("row", "col"), None),
            P(None, ("col", "row"), None),
            P(None, ("col", "row")),
        ),
        out_specs=P(None, ("row", "col")),
        check_vma=False,
    )
```
